32 devices in a mesh: op: 4 (over y, core), lsec: 2 (over x), rsec: 4 (over z).
Axes of the slice: x: 2, y: 2, z: 4, core: 2. Of those that a mesh axis runs over, the one named last changes fastest.
Arguments:
- wavefn: float32 [8, 16, 128, 128], P('lsec', 'rsec'), may hold values from -6 to 6
- left_ops: float32 [28, 8, 128, 128], P('op', 'lsec'), may hold values from -0.5 to 0.5
- right_ops: float32 [28, 16, 128, 128], P('op', 'rsec'), may hold values from -0.09375 to 0.09375
- term_shift: int32 [28], P('op'), may hold values from 0 to 1
Outputs:
- sigma: float32 [8, 16, 128, 128], P('lsec', 'rsec', 'op')
The draws below stay inside these ranges and needn't reach their ends.
All inputs are finite; a program needn't handle non-finite values.
Results may differ from the reference program's by a relative error of at most 0.0001.
Values sent between devices are 32-bit elements; how exact they have to be, the bound alone decides.
No kernel may reach another device: no remote copies, remote signals or barrier semaphores. Data moves between devices by JAX's collectives and lax.ppermute only.
A program may use at most 64 MiB of HBM per device.

```python
import jax
import jax.numpy as jnp
from jax import lax

S = 128
LSL = 4
RSL = 4
NL = 8
NR = 16
TERMS = 28
N_LSEC = 2
N_RSEC = 4


def with_ends(values, rng, low, largest):
    longest = values.shape.index(max(values.shape))
    spots = []
    for shift in (0, 1):
        where = [jax.random.randint(jax.random.fold_in(rng, axis), (), 0, length) for axis, length in enumerate(values.shape)]
        where[longest] = (where[longest] + shift) % values.shape[longest]
        spots.append(tuple(where))
    return values.at[spots[0]].set(low).at[spots[1]].set(largest)


def shard_levels(own_key, dims, cuts, low, high):
    def one(axis_at, shards_of):
        draws = jax.random.uniform(jax.random.fold_in(jax.random.fold_in(own_key, 6), axis_at), (shards_of,), jnp.float32, low / len(cuts), high / len(cuts))
        return jnp.repeat(jnp.exp(draws), dims[axis_at] // shards_of).reshape((-1,) + (1,) * (len(dims) - axis_at - 1))

    loudness = one(*cuts[0])
    for cut in cuts[1:]:
        loudness = loudness * one(*cut)
    return loudness


def noise(own_key, dims, scale, reach, pieces=(), dtype=jnp.bfloat16):
    loudness = shard_levels(own_key, dims, pieces, -0.22, 0.18) if pieces else 1.0
    drawn = jax.random.normal(own_key, dims, jnp.float32) * scale * loudness
    return jnp.minimum(jnp.maximum(drawn, -reach), reach).astype(dtype)


def setup_inputs(seed: int = 0) -> dict:
    arg_keys = jax.random.split(jax.random.key(seed), 5)
    wavefn = noise(arg_keys[0], (NL, NR, S, S), 1.0, 6.0, ((0, 2), (1, 4)), jnp.float32)
    left_ops = noise(arg_keys[1], (TERMS, NL, S, S), S ** -0.5, 0.5, ((0, 4), (1, 2)), jnp.float32)
    right_ops = noise(arg_keys[2], (TERMS, NR, S, S), (S * TERMS) ** -0.5, 0.09375, ((0, 4), (1, 4)), jnp.float32)
    term_shift = with_ends(jax.random.randint(arg_keys[3], (TERMS,), 0, 2), jax.random.fold_in(arg_keys[3], 1), 0, 1).astype(jnp.int32)
    return dict(wavefn=wavefn, left_ops=left_ops, right_ops=right_ops, term_shift=term_shift)


def reference(wavefn, left_ops, right_ops, term_shift):
    high = lax.Precision.HIGHEST
    lq = jnp.arange(NL)
    rq = jnp.arange(NR)
    lpos = ((lq % N_LSEC) * LSL + lq // N_LSEC).astype(jnp.int32)
    rpos = ((rq % N_RSEC) * RSL + rq // N_RSEC).astype(jnp.int32)
    psi = wavefn[lpos][:, rpos]
    lop = left_ops[:, lpos]
    rop = right_ops[:, rpos]

    def one_term(carry, items):
        lblock, rblock, shift_bit = items
        inner = jnp.einsum('lij,lrjk->lrik', lblock, psi, precision=high)
        term_out = jnp.einsum('lrik,rmk->lrim', inner, rblock, precision=high)
        weight = shift_bit.astype(jnp.float32)
        return (carry[0] + weight * term_out, carry[1] + (1.0 - weight) * term_out), None

    zero = jnp.zeros((NL, NR, S, S), jnp.float32)
    (rising, falling), _ = lax.scan(one_term, (zero, zero), (lop, rop, term_shift))
    moved = jnp.zeros((NL, NR, S, S), jnp.float32)
    moved = moved.at[1:, :-1].add(rising[:-1, 1:])
    moved = moved.at[:-1, 1:].add(falling[1:, :-1])
    lp = jnp.arange(NL)
    rp = jnp.arange(NR)
    lsec_of = ((lp % LSL) * N_LSEC + lp // LSL).astype(jnp.int32)
    rsec_of = ((rp % RSL) * N_RSEC + rp // RSL).astype(jnp.int32)
    return moved[lsec_of][:, rsec_of]
```

```python
import functools

import jax
import jax.numpy as jnp
from jax import lax
from jax.experimental import pallas as pl
from jax.experimental.pallas import tpu as pltpu
from jax.sharding import PartitionSpec as P

CHUNKS = 1
CORES = 2
VMEM = 48 * 1024 * 1024
NT = (((1,), (1,)), ((), ()))


def split(value):
    high = value.astype(jnp.bfloat16)
    low = (value - high.astype(jnp.float32)).astype(jnp.bfloat16)
    return high, low


def class_sums(n_op, shift, psi, lops, rops, send, keep, left, right, inner):
    terms, slots, size, _ = lops.shape
    pair = psi.shape[1]
    rows = size // n_op
    ny = n_op // CORES
    core = lax.rem(lax.axis_index("op"), CORES)

    @pl.when(pl.program_id(0) == 0)
    def _():
        def one_left(index, carry):
            t = index // slots
            l = lax.rem(index, slots)
            blocks = []
            for who in (1 - core, core):
                for y in range(ny):
                    at = pl.multiple_of((y * CORES + who) * rows, rows)
                    blocks.append(lops[t, l, pl.ds(at, rows), :])
            high, low = split(jnp.concatenate(blocks, axis=0))
            at = pl.ds(pl.multiple_of(t * size, size), size)
            left[l, at, :size] = high
            left[l, at, size:] = low
            return carry

        lax.fori_loop(0, terms * slots, one_left, 0)

    for r in range(pair):
        for t in range(terms):
            high, low = split(rops[t, r])
            up = shift[t].astype(jnp.float32).astype(jnp.bfloat16)
            down = (1 - shift[t]).astype(jnp.float32).astype(jnp.bfloat16)
            columns = slice(t * size, (t + 1) * size)
            right[r, 0, :size, columns] = high * up
            right[r, 0, size:, columns] = high * down
            right[r, 1, :size, columns] = low * up
            right[r, 1, size:, columns] = low * down

    def one_slot(l, carry):
        highs, lows = zip(*[split(psi[l, r]) for r in range(pair)])
        high = jnp.concatenate(highs, axis=1)
        low = jnp.concatenate(lows, axis=1)
        both = left[l]
        out = jnp.dot(both, jnp.concatenate([high, high], axis=0), preferred_element_type=jnp.float32)
        out = out + jnp.dot(both[:, :size], low, preferred_element_type=jnp.float32)
        at = pl.ds(pl.multiple_of(l * size, size), size)
        for t in range(terms):
            for r in range(pair):
                block = out[t * size:(t + 1) * size, r * size:(r + 1) * size]
                high, low = split(block)
                inner[r, at, t * size:(t + 1) * size] = high
                inner[r, at, (terms + t) * size:(terms + t + 1) * size] = low
        return carry

    lax.fori_loop(0, slots, one_slot, 0)

    depth = terms * size
    for r in range(pair):
        out = lax.dot_general(inner[r, :, :depth], right[r, 0], NT, preferred_element_type=jnp.float32)
        out = out + lax.dot_general(inner[r, :, depth:], right[r, 0], NT, preferred_element_type=jnp.float32)
        out = out + lax.dot_general(inner[r, :, :depth], right[r, 1], NT, preferred_element_type=jnp.float32)
        for l in range(slots):
            for way in range(2):
                columns = slice(way * size, (way + 1) * size)
                for y in range(ny):
                    at = l * size + y * rows
                    send[y, way, l, r] = out[at:at + rows, columns]
                    at = at + size // 2
                    keep[y, way, l, r] = out[at:at + rows, columns]


def partial_sums(wavefn, left_ops, right_ops, term_shift, chunk):
    terms, slots, size, _ = left_ops.shape
    across = wavefn.shape[1]
    n_op = lax.axis_size("op")
    ny = n_op // CORES
    pair = 2
    steps = across // pair // CHUNKS
    result = jax.ShapeDtypeStruct((ny, 2, slots, steps * pair, size // n_op, size), jnp.float32)
    piece = pl.BlockSpec((ny, 2, slots, pair, size // n_op, size), lambda g: (0, 0, 0, g, 0, 0))
    depth = terms * size
    macs = steps * (slots * depth * 2 * size * pair * size + pair * slots * size * 3 * depth * 2 * size)
    return pl.pallas_call(
        functools.partial(class_sums, n_op),
        grid=(steps,),
        in_specs=[
            pl.BlockSpec(memory_space=pltpu.SMEM),
            pl.BlockSpec((slots, pair, size, size), lambda g: (0, g + chunk * steps, 0, 0)),
            pl.BlockSpec((terms, slots, size, size), lambda g: (0, 0, 0, 0)),
            pl.BlockSpec((terms, pair, size, size), lambda g: (0, g + chunk * steps, 0, 0)),
        ],
        out_specs=[piece, piece],
        out_shape=[result, result],
        scratch_shapes=[
            pltpu.VMEM((slots, depth, 2 * size), jnp.bfloat16),
            pltpu.VMEM((pair, 2, 2 * size, depth), jnp.bfloat16),
            pltpu.VMEM((pair, slots * size, 2 * depth), jnp.bfloat16),
        ],
        compiler_params=pltpu.CompilerParams(vmem_limit_bytes=VMEM),
        cost_estimate=pl.CostEstimate(flops=2 * macs, bytes_accessed=6 * 1024 * 1024, transcendentals=0),
    )(term_shift, wavefn, left_ops, right_ops)


def whole(count):
    return [pl.BlockSpec(memory_space=pltpu.VMEM)] * count


def add_cores(keep, arrived):
    ny = keep.shape[0]

    def kernel(a, b, *outs):
        mine = lax.axis_index("op") // CORES
        for ahead, out in enumerate(outs):
            y = lax.rem(mine + ahead, ny)
            out[...] = a[y] + b[y]

    shape = jax.ShapeDtypeStruct(keep.shape[1:], jnp.float32)
    return pl.pallas_call(
        kernel,
        in_specs=whole(2),
        out_specs=whole(ny),
        out_shape=[shape] * ny,
        compiler_params=pltpu.CompilerParams(vmem_limit_bytes=VMEM),
    )(keep, arrived)


def add_chips(*pieces):
    shape = jax.ShapeDtypeStruct(pieces[0].shape[1:], jnp.float32)

    def kernel(*refs):
        ins, outs = refs[:-2], refs[-2:]
        for way, out in enumerate(outs):
            total = ins[0][way]
            for ref in ins[1:]:
                total = total + ref[way]
            out[...] = total

    return pl.pallas_call(
        kernel,
        in_specs=whole(len(pieces)),
        out_specs=whole(2),
        out_shape=[shape] * 2,
        compiler_params=pltpu.CompilerParams(vmem_limit_bytes=VMEM),
    )(*pieces)


def settle(rising, falling):
    slots, wide, rows, size = rising[0].shape
    across = wide * len(rising)
    n_left, n_right = lax.axis_size("lsec"), lax.axis_size("rsec")

    def kernel(*refs):
        out = refs[-1]
        mine_l, mine_r = lax.axis_index("lsec"), lax.axis_index("rsec")
        first_l, last_l = (mine_l == 0).astype(jnp.int32), (mine_l == n_left - 1).astype(jnp.int32)
        first_r, last_r = (mine_r == 0).astype(jnp.int32), (mine_r == n_right - 1).astype(jnp.int32)
        out[...] = jnp.zeros_like(out)
        for way, (step_l, step_r) in enumerate(((first_l, -last_r), (-last_l, first_r))):
            for l in range(slots):
                for r in range(across):
                    ref = refs[way * len(rising) + r // wide]
                    to_l, to_r = l + step_l, r + step_r

                    @pl.when((to_l >= 0) & (to_l < slots) & (to_r >= 0) & (to_r < across))
                    def _():
                        out[to_l, to_r] += ref[l, r % wide]

    return pl.pallas_call(
        kernel,
        in_specs=whole(2 * len(rising)),
        out_specs=pl.BlockSpec(memory_space=pltpu.VMEM),
        out_shape=jax.ShapeDtypeStruct((slots, across, rows, size), jnp.float32),
        compiler_params=pltpu.CompilerParams(vmem_limit_bytes=VMEM),
    )(*rising, *falling)


def shards(wavefn, left_ops, right_ops, term_shift):
    n_op, n_left, n_right = (lax.axis_size(axis) for axis in ("op", "lsec", "rsec"))
    ny = n_op // CORES
    cores = [(i, i ^ 1) for i in range(n_op)]

    def ahead(value, by):
        perm = [(i, (i + CORES * by) % n_op) for i in range(n_op)]
        return lax.ppermute(value, "op", perm)

    def sectors(value, by_l, by_r):
        perm = [
            (l * n_right + r, (l + by_l) % n_left * n_right + (r + by_r) % n_right)
            for l in range(n_left) for r in range(n_right)
        ]
        return lax.ppermute(value, ("lsec", "rsec"), perm)

    rising, falling = [], []
    for chunk in range(CHUNKS):
        send, keep = partial_sums(wavefn, left_ops, right_ops, term_shift, chunk)
        arrived = lax.ppermute(send, "op", cores)
        mine, *others = add_cores(keep, arrived)
        came = [ahead(value, by) for by, value in enumerate(others, 1)]
        up, down = add_chips(mine, *came)
        rising.append(sectors(up, 1, -1))
        falling.append(sectors(down, -1, 1))
    return settle(rising, falling)


def solution(mesh):
    placed = (
        P("lsec", "rsec", None, None),
        P("op", "lsec", None, None),
        P("op", "rsec", None, None),
        P("op"),
    )
    return jax.shard_map(
        shards, mesh=mesh, in_specs=placed, out_specs=P("lsec", "rsec", "op", None), check_vma=False
    )
```

```python
import functools

import jax
import jax.numpy as jnp
from jax import lax
from jax.experimental import pallas as pl
from jax.experimental.pallas import tpu as pltpu
from jax.sharding import PartitionSpec as P

CHUNKS = 2
CORES = 2
VMEM = 48 * 1024 * 1024
NT = (((1,), (1,)), ((), ()))


def split(value):
    high = value.astype(jnp.bfloat16)
    low = (value - high.astype(jnp.float32)).astype(jnp.bfloat16)
    return high, low


def class_sums(n_op, shift, psi, lops, rops, send, keep, left, right, inner):
    terms, slots, size, _ = lops.shape
    pair = psi.shape[1]
    rows = size // n_op
    ny = n_op // CORES
    core = lax.rem(lax.axis_index("op"), CORES)

    @pl.when(pl.program_id(0) == 0)
    def _():
        def one_left(index, carry):
            t = index // slots
            l = lax.rem(index, slots)
            blocks = []
            for who in (1 - core, core):
                for y in range(ny):
                    at = pl.multiple_of((y * CORES + who) * rows, rows)
                    blocks.append(lops[t, l, pl.ds(at, rows), :])
            high, low = split(jnp.concatenate(blocks, axis=0))
            at = pl.ds(pl.multiple_of(t * size, size), size)
            left[l, at, :size] = high
            left[l, at, size:] = low
            return carry

        lax.fori_loop(0, terms * slots, one_left, 0)

    for r in range(pair):
        for t in range(terms):
            high, low = split(rops[t, r])
            up = shift[t].astype(jnp.float32).astype(jnp.bfloat16)
            down = (1 - shift[t]).astype(jnp.float32).astype(jnp.bfloat16)
            columns = slice(t * size, (t + 1) * size)
            right[r, 0, :size, columns] = high * up
            right[r, 0, size:, columns] = high * down
            right[r, 1, :size, columns] = low * up
            right[r, 1, size:, columns] = low * down

    def one_slot(l, carry):
        highs, lows = zip(*[split(psi[l, r]) for r in range(pair)])
        high = jnp.concatenate(highs, axis=1)
        low = jnp.concatenate(lows, axis=1)
        both = left[l]
        out = jnp.dot(both, jnp.concatenate([high, high], axis=0), preferred_element_type=jnp.float32)
        out = out + jnp.dot(both[:, :size], low, preferred_element_type=jnp.float32)
        at = pl.ds(pl.multiple_of(l * size, size), size)
        for t in range(terms):
            for r in range(pair):
                block = out[t * size:(t + 1) * size, r * size:(r + 1) * size]
                high, low = split(block)
                inner[r, at, t * size:(t + 1) * size] = high
                inner[r, at, (terms + t) * size:(terms + t + 1) * size] = low
        return carry

    lax.fori_loop(0, slots, one_slot, 0)

    depth = terms * size
    for r in range(pair):
        out = lax.dot_general(inner[r, :, :depth], right[r, 0], NT, preferred_element_type=jnp.float32)
        out = out + lax.dot_general(inner[r, :, depth:], right[r, 0], NT, preferred_element_type=jnp.float32)
        out = out + lax.dot_general(inner[r, :, :depth], right[r, 1], NT, preferred_element_type=jnp.float32)
        for l in range(slots):
            for way in range(2):
                columns = slice(way * size, (way + 1) * size)
                for y in range(ny):
                    at = l * size + y * rows
                    send[y, way, l, r] = out[at:at + rows, columns]
                    at = at + size // 2
                    keep[y, way, l, r] = out[at:at + rows, columns]


def partial_sums(wavefn, left_ops, right_ops, term_shift, chunk):
    terms, slots, size, _ = left_ops.shape
    across = wavefn.shape[1]
    n_op = lax.axis_size("op")
    ny = n_op // CORES
    pair = 2
    steps = across // pair // CHUNKS
    result = jax.ShapeDtypeStruct((ny, 2, slots, steps * pair, size // n_op, size), jnp.float32)
    piece = pl.BlockSpec((ny, 2, slots, pair, size // n_op, size), lambda g: (0, 0, 0, g, 0, 0))
    depth = terms * size
    macs = steps * (slots * depth * 2 * size * pair * size + pair * slots * size * 3 * depth * 2 * size)
    return pl.pallas_call(
        functools.partial(class_sums, n_op),
        grid=(steps,),
        in_specs=[
            pl.BlockSpec(memory_space=pltpu.SMEM),
            pl.BlockSpec((slots, pair, size, size), lambda g: (0, g + chunk * steps, 0, 0)),
            pl.BlockSpec((terms, slots, size, size), lambda g: (0, 0, 0, 0)),
            pl.BlockSpec((terms, pair, size, size), lambda g: (0, g + chunk * steps, 0, 0)),
        ],
        out_specs=[piece, piece],
        out_shape=[result, result],
        scratch_shapes=[
            pltpu.VMEM((slots, depth, 2 * size), jnp.bfloat16),
            pltpu.VMEM((pair, 2, 2 * size, depth), jnp.bfloat16),
            pltpu.VMEM((pair, slots * size, 2 * depth), jnp.bfloat16),
        ],
        compiler_params=pltpu.CompilerParams(vmem_limit_bytes=VMEM),
        cost_estimate=pl.CostEstimate(flops=2 * macs, bytes_accessed=6 * 1024 * 1024, transcendentals=0),
    )(term_shift, wavefn, left_ops, right_ops)


def whole(count):
    return [pl.BlockSpec(memory_space=pltpu.VMEM)] * count


def add_cores(keep, arrived):
    ny = keep.shape[0]

    def kernel(a, b, *outs):
        mine = lax.axis_index("op") // CORES
        for ahead, out in enumerate(outs):
            y = lax.rem(mine + ahead, ny)
            out[...] = a[y] + b[y]

    shape = jax.ShapeDtypeStruct(keep.shape[1:], jnp.float32)
    return pl.pallas_call(
        kernel,
        in_specs=whole(2),
        out_specs=whole(ny),
        out_shape=[shape] * ny,
        compiler_params=pltpu.CompilerParams(vmem_limit_bytes=VMEM),
    )(keep, arrived)


def add_chips(*pieces):
    shape = jax.ShapeDtypeStruct(pieces[0].shape[1:], jnp.float32)

    def kernel(*refs):
        ins, outs = refs[:-2], refs[-2:]
        for way, out in enumerate(outs):
            total = ins[0][way]
            for ref in ins[1:]:
                total = total + ref[way]
            out[...] = total

    return pl.pallas_call(
        kernel,
        in_specs=whole(len(pieces)),
        out_specs=whole(2),
        out_shape=[shape] * 2,
        compiler_params=pltpu.CompilerParams(vmem_limit_bytes=VMEM),
    )(*pieces)


def settle(rising, falling):
    slots, wide, rows, size = rising[0].shape
    across = wide * len(rising)
    n_left, n_right = lax.axis_size("lsec"), lax.axis_size("rsec")

    def kernel(*refs):
        out = refs[-1]
        mine_l, mine_r = lax.axis_index("lsec"), lax.axis_index("rsec")
        first_l, last_l = (mine_l == 0).astype(jnp.int32), (mine_l == n_left - 1).astype(jnp.int32)
        first_r, last_r = (mine_r == 0).astype(jnp.int32), (mine_r == n_right - 1).astype(jnp.int32)
        out[...] = jnp.zeros_like(out)
        for way, (step_l, step_r) in enumerate(((first_l, -last_r), (-last_l, first_r))):
            for l in range(slots):
                for r in range(across):
                    ref = refs[way * len(rising) + r // wide]
                    to_l, to_r = l + step_l, r + step_r

                    @pl.when((to_l >= 0) & (to_l < slots) & (to_r >= 0) & (to_r < across))
                    def _():
                        out[to_l, to_r] += ref[l, r % wide]

    return pl.pallas_call(
        kernel,
        in_specs=whole(2 * len(rising)),
        out_specs=pl.BlockSpec(memory_space=pltpu.VMEM),
        out_shape=jax.ShapeDtypeStruct((slots, across, rows, size), jnp.float32),
        compiler_params=pltpu.CompilerParams(vmem_limit_bytes=VMEM),
    )(*rising, *falling)


def shards(wavefn, left_ops, right_ops, term_shift):
    n_op, n_left, n_right = (lax.axis_size(axis) for axis in ("op", "lsec", "rsec"))
    ny = n_op // CORES
    cores = [(i, i ^ 1) for i in range(n_op)]

    def ahead(value, by):
        perm = [(i, (i + CORES * by) % n_op) for i in range(n_op)]
        return lax.ppermute(value, "op", perm)

    def sectors(value, by_l, by_r):
        perm = [
            (l * n_right + r, (l + by_l) % n_left * n_right + (r + by_r) % n_right)
            for l in range(n_left) for r in range(n_right)
        ]
        return lax.ppermute(value, ("lsec", "rsec"), perm)

    rising, falling = [], []
    for chunk in range(CHUNKS):
        send, keep = partial_sums(wavefn, left_ops, right_ops, term_shift, chunk)
        arrived = lax.ppermute(send, "op", cores)
        mine, *others = add_cores(keep, arrived)
        came = [ahead(value, by) for by, value in enumerate(others, 1)]
        up, down = add_chips(mine, *came)
        rising.append(sectors(up, 1, -1))
        falling.append(sectors(down, -1, 1))
    return settle(rising, falling)


def solution(mesh):
    placed = (
        P("lsec", "rsec", None, None),
        P("op", "lsec", None, None),
        P("op", "rsec", None, None),
        P("op"),
    )
    return jax.shard_map(
        shards, mesh=mesh, in_specs=placed, out_specs=P("lsec", "rsec", "op", None), check_vma=False
    )
```

```python
import functools

import jax
import jax.numpy as jnp
from jax import lax
from jax.experimental import pallas as pl
from jax.experimental.pallas import tpu as pltpu
from jax.sharding import PartitionSpec as P

WIDTHS = (2, 2)
CORES = 2
LIMIT = 32 * 1024 * 1024
NT = (((1,), (1,)), ((), ()))
PARAMS = pltpu.CompilerParams(vmem_limit_bytes=LIMIT)
HBM = pl.BlockSpec(memory_space=pltpu.HBM)
VMEM = pl.BlockSpec(memory_space=pltpu.VMEM)


def split(value):
    high = value.astype(jnp.bfloat16)
    low = (value - high.astype(jnp.float32)).astype(jnp.bfloat16)
    return high, low


def one_right_slot(n_op, chosen, psi, rops, left, right, inner, send, keep, r):
    terms = rops.shape[0]
    slots, _, twice = left.shape
    size = twice // 2
    rows = size // n_op
    depth = terms * size
    for t in range(terms):
        high, low = (part.reshape(-1, 16, size) for part in split(rops[t, r]))
        for way in range(2):
            at = (slice(way * size, (way + 1) * size), slice(t * size, (t + 1) * size))
            right[0, *at] = (high * chosen[t, way]).reshape(size, size)
            right[1, *at] = (low * chosen[t, way]).reshape(size, size)
    for l in range(slots):
        both = jnp.concatenate(split(psi[l, r]), axis=1)
        out = jnp.dot(left[l], jnp.concatenate([both, both], axis=0), preferred_element_type=jnp.float32)
        for t in range(terms):
            block = out[t * size:(t + 1) * size]
            high, low = split(block[:, :size] + block[:, size:])
            inner[l * size:(l + 1) * size, t * size:(t + 1) * size] = high
            inner[l * size:(l + 1) * size, depth + t * size:depth + (t + 1) * size] = low
    out = lax.dot_general(
        jnp.concatenate([inner[...], inner[:, :depth]], axis=1),
        jnp.concatenate([right[0], right[0], right[1]], axis=1),
        NT, preferred_element_type=jnp.float32,
    )
    for l in range(slots):
        for block in range(n_op):
            at = l * size + block * rows
            where = (block // CORES, block % CORES, l, r)
            keep[where] = out[at:at + rows, :size]
            send[where] = out[at:at + rows, size:]


def first_sums(n_op, shift, psi, lops, rops, *refs):
    terms, slots, size, _ = lops.shape
    wide = refs[0].shape[3]
    rest = psi.shape[1] - wide
    if rest:
        send, keep, left, chosen, psi_rest, rops_rest = refs[:6]
        refs = refs[6:]
    else:
        send, keep = refs[:2]
        left, chosen = refs[-2:]
        refs = refs[2:-2]
    bits, psi_now, rops_now, lops_now, right, inner, sems, lsems = refs
    copies = [
        pltpu.make_async_copy(shift, bits, sems.at[0]),
        pltpu.make_async_copy(rops.at[:, :wide], rops_now, sems.at[1]),
        pltpu.make_async_copy(psi.at[:, :wide], psi_now, sems.at[2]),
    ]
    lcopies = [pltpu.make_async_copy(lops.at[t], lops_now.at[t], lsems.at[t]) for t in range(terms)]
    later = []
    if rest:
        later = [
            pltpu.make_async_copy(rops.at[:, wide:], rops_rest, sems.at[3]),
            pltpu.make_async_copy(psi.at[:, wide:], psi_rest, sems.at[4]),
        ]
    for copy in lcopies + copies + later:
        copy.start()
    for t in range(terms):
        lcopies[t].wait()
        for l in range(slots):
            left[l, t * size:(t + 1) * size, :] = jnp.concatenate(split(lops_now[t, l]), axis=1)
    for copy in copies:
        copy.wait()
    core = lax.rem(lax.axis_index("op"), CORES)
    for t in range(terms):
        kept = (bits[t] + core == 1).astype(jnp.float32)
        chosen[t, 0] = jnp.full((16, size), kept, jnp.float32).astype(jnp.bfloat16)
        chosen[t, 1] = jnp.full((16, size), 1.0 - kept, jnp.float32).astype(jnp.bfloat16)
    for r in range(wide):
        one_right_slot(n_op, chosen, psi_now, rops_now, left, right, inner, send, keep, r)
    for copy in later:
        copy.wait()


def later_sums(n_op, start, left, chosen, psi, rops, send, keep, right, inner):
    for r in range(send.shape[3]):
        one_right_slot(
            n_op, chosen, psi.at[:, start:], rops.at[:, start:], left, right, inner, send, keep, r
        )


def cost(terms, slots, size, wide):
    macs = wide * slots * terms * size * (2 * size * 2 * size + 3 * size * 2 * size)
    return pl.CostEstimate(flops=2 * macs, bytes_accessed=8 * 1024 * 1024, transcendentals=0)


def partial_sums(wavefn, left_ops, right_ops, term_shift, widths):
    terms, slots, size, _ = left_ops.shape
    n_op = lax.axis_size("op")
    f32, bf16 = jnp.float32, jnp.bfloat16

    def result(wide):
        return jax.ShapeDtypeStruct((n_op // CORES, CORES, slots, wide, size // n_op, size), f32)

    work = [
        pltpu.VMEM((2, 2 * size, terms * size), bf16),
        pltpu.VMEM((slots * size, 2 * terms * size), bf16),
    ]
    wide, rest = widths[0], sum(widths[1:])
    shared = [(slots, terms * size, 2 * size), (terms, 2, 16, size)]
    out_shape = [result(wide)] * 2
    if rest:
        out_shape += [jax.ShapeDtypeStruct(shape, bf16) for shape in shared]
        out_shape += [
            jax.ShapeDtypeStruct((slots, rest, size, size), f32),
            jax.ShapeDtypeStruct((terms, rest, size, size), f32),
        ]
    scratch = [
        pltpu.SMEM(term_shift.shape, jnp.int32),
        pltpu.VMEM((slots, wide, size, size), f32),
        pltpu.VMEM((terms, wide, size, size), f32),
        pltpu.VMEM((terms, slots, size, size), f32),
        *work,
        pltpu.SemaphoreType.DMA((5,)),
        pltpu.SemaphoreType.DMA((terms,)),
    ]
    if not rest:
        scratch += [pltpu.VMEM(shape, bf16) for shape in shared]
    send, keep, *passed = pl.pallas_call(
        functools.partial(first_sums, n_op),
        in_specs=[HBM] * 4,
        out_specs=[VMEM] * len(out_shape),
        out_shape=out_shape,
        scratch_shapes=scratch,
        compiler_params=PARAMS,
        cost_estimate=cost(terms, slots, size, wide),
    )(*(pltpu.with_memory_space_constraint(x, pltpu.HBM) for x in (term_shift, wavefn, left_ops, right_ops)))
    sums = [(send, keep)]
    start = 0
    for wide in widths[1:]:
        sums.append(pl.pallas_call(
            functools.partial(later_sums, n_op, start),
            in_specs=[VMEM] * 4,
            out_specs=[VMEM] * 2,
            out_shape=[result(wide)] * 2,
            scratch_shapes=work,
            compiler_params=PARAMS,
            cost_estimate=cost(terms, slots, size, wide),
        )(*passed))
        start += wide
    return sums


def add_cores(keep, arrived):
    ny = keep.shape[0]

    def kernel(a, b, *outs):
        mine = lax.axis_index("op") // CORES
        for ahead, out in enumerate(outs):
            y = lax.rem(mine + ahead, ny)
            out[...] = a[y] + b[y]

    shape = jax.ShapeDtypeStruct(keep.shape[1:], jnp.float32)
    return pl.pallas_call(
        kernel, in_specs=[VMEM] * 2, out_specs=[VMEM] * ny, out_shape=[shape] * ny, compiler_params=PARAMS
    )(keep, arrived)


def add_chips(*pieces):
    def kernel(*refs):
        total = refs[0][...]
        for ref in refs[1:-1]:
            total = total + ref[...]
        refs[-1][...] = total

    shape = jax.ShapeDtypeStruct(pieces[0].shape, jnp.float32)
    return pl.pallas_call(
        kernel, in_specs=[VMEM] * len(pieces), out_specs=VMEM, out_shape=shape, compiler_params=PARAMS
    )(*pieces)


def other_rows(moved):
    def kernel(a, out):
        out[...] = a[1 - lax.rem(lax.axis_index("op"), CORES)]

    shape = jax.ShapeDtypeStruct(moved.shape[1:], jnp.float32)
    return pl.pallas_call(
        kernel, in_specs=[VMEM], out_specs=VMEM, out_shape=shape, compiler_params=PARAMS
    )(moved)


def settle(moved, swapped):
    count = len(moved)
    _, slots, _, rows, size = moved[0].shape
    places = [(i, r) for i, value in enumerate(moved) for r in range(value.shape[2])]
    across = len(places)
    n_left, n_right = lax.axis_size("lsec"), lax.axis_size("rsec")

    def kernel(*refs):
        out = refs[-1]
        core = lax.rem(lax.axis_index("op"), CORES)
        mine_l, mine_r = lax.axis_index("lsec"), lax.axis_index("rsec")
        first_l, last_l = (mine_l == 0).astype(jnp.int32), (mine_l == n_left - 1).astype(jnp.int32)
        first_r, last_r = (mine_r == 0).astype(jnp.int32), (mine_r == n_right - 1).astype(jnp.int32)
        out[...] = jnp.zeros_like(out)
        for kept in (True, False):
            rising = core == 0 if kept else core == 1
            step_l = jnp.where(rising, first_l, -last_l)
            step_r = jnp.where(rising, -last_r, first_r)
            for l in range(slots):
                for r, (chunk, at) in enumerate(places):
                    to_l, to_r = l + step_l, r + step_r

                    @pl.when((to_l >= 0) & (to_l < slots) & (to_r >= 0) & (to_r < across))
                    def _():
                        block = refs[chunk][core, l, at] if kept else refs[count + chunk][l, at]
                        out[to_l, to_r] += block

    return pl.pallas_call(
        kernel,
        in_specs=[VMEM] * (2 * count),
        out_specs=VMEM,
        out_shape=jax.ShapeDtypeStruct((slots, across, rows, size), jnp.float32),
        compiler_params=PARAMS,
    )(*moved, *swapped)


def shards(wavefn, left_ops, right_ops, term_shift):
    n_op, n_left, n_right = (lax.axis_size(axis) for axis in ("op", "lsec", "rsec"))
    across = wavefn.shape[1]
    cores = [(i, i ^ 1) for i in range(n_op)]

    def ahead(value, by):
        return lax.ppermute(value, "op", [(i, (i + CORES * by) % n_op) for i in range(n_op)])

    def sectors(value):
        def place(o, l, r):
            return (o * n_left + l % n_left) * n_right + r % n_right

        perm = [
            (place(o, l, r), place(o, l - 1, r + 1) if o % CORES else place(o, l + 1, r - 1))
            for o in range(n_op) for l in range(n_left) for r in range(n_right)
        ]
        return lax.ppermute(value, ("op", "lsec", "rsec"), perm)

    moved, swapped = [], []
    widths = WIDTHS if sum(WIDTHS) == across else (across,)
    for send, keep in partial_sums(wavefn, left_ops, right_ops, term_shift, widths):
        arrived = lax.ppermute(send, "op", cores)
        mine, *others = add_cores(keep, arrived)
        came = [ahead(value, by) for by, value in enumerate(others, 1)]
        moved.append(sectors(add_chips(mine, *came)))
        swapped.append(lax.ppermute(other_rows(moved[-1]), "op", cores))
    return settle(moved, swapped)


def solution(mesh):
    placed = (
        P("lsec", "rsec", None, None),
        P("op", "lsec", None, None),
        P("op", "rsec", None, None),
        P("op"),
    )
    return jax.shard_map(
        shards, mesh=mesh, in_specs=placed, out_specs=P("lsec", "rsec", "op", None), check_vma=False
    )
```

```python
import functools

import jax
import jax.numpy as jnp
from jax import lax
from jax.experimental import pallas as pl
from jax.experimental.pallas import tpu as pltpu
from jax.sharding import PartitionSpec as P

WIDTHS = (2, 2)
CORES = 2
LIMIT = 32 * 1024 * 1024
NT = (((1,), (1,)), ((), ()))
PARAMS = pltpu.CompilerParams(vmem_limit_bytes=LIMIT)
HBM = pl.BlockSpec(memory_space=pltpu.HBM)
VMEM = pl.BlockSpec(memory_space=pltpu.VMEM)
ANY = pl.BlockSpec(memory_space=pl.ANY)


def split(value):
    high = value.astype(jnp.bfloat16)
    low = (value - high.astype(jnp.float32)).astype(jnp.bfloat16)
    return high, low


def choose_rows(lops, aheads, left, t):
    _, slots, size, _ = lops.shape
    ny = lax.axis_size("op") // CORES
    mine = lax.axis_index("op") // CORES
    share = size // ny
    many = share * len(aheads)
    for l in range(slots):
        rows = [
            lops[t, l, pl.ds(pl.multiple_of(lax.rem(mine + ahead, ny) * share, share), share), :]
            for ahead in aheads
        ]
        left[l, t * many:(t + 1) * many, :] = jnp.concatenate(split(jnp.concatenate(rows, axis=0)), axis=1)


def choose_class(rops, chosen, right, r):
    terms, _, size, _ = rops.shape
    for t in range(terms):
        high, low = (part.reshape(-1, 16, size) for part in split(rops[t, r]))
        for way in range(2):
            at = (slice(way * size, (way + 1) * size), slice(t * size, (t + 1) * size))
            right[r, 0, *at] = (high * chosen[t, way]).reshape(size, size)
            right[r, 1, *at] = (low * chosen[t, way]).reshape(size, size)


def products(left, psi, right, inner, send, keep, start):
    slots, height, twice = left.shape
    size = twice // 2
    wide = right.shape[0]
    depth = right.shape[3]
    terms = depth // size
    many = height // terms
    rows = keep.shape[-2]
    for r in range(wide):
        for l in range(slots):
            both = jnp.concatenate(split(psi[l, start + r]), axis=1)
            out = jnp.dot(left[l], jnp.concatenate([both, both], axis=0), preferred_element_type=jnp.float32)
            for t in range(terms):
                block = out[t * many:(t + 1) * many]
                high, low = split(block[:, :size] + block[:, size:])
                inner[l * many:(l + 1) * many, t * size:(t + 1) * size] = high
                inner[l * many:(l + 1) * many, depth + t * size:depth + (t + 1) * size] = low
        out = lax.dot_general(
            jnp.concatenate([inner[...], inner[:, :depth]], axis=1),
            jnp.concatenate([right[r, 0], right[r, 0], right[r, 1]], axis=1),
            NT, preferred_element_type=jnp.float32,
        )
        for l in range(slots):
            for block in range(many // rows):
                at = l * many + block * rows
                where = (block // CORES, block % CORES, l, r)
                keep[where] = out[at:at + rows, :size]
                send[where] = out[at:at + rows, size:]


def first_others(aheads, shift, psi, lops, rops, send, keep, left, right, chosen, lops_all, psi_all, rops_rest, *refs):
    bits, rops_now, inner, sems, lsems = refs
    terms = lops.shape[0]
    size = psi.shape[-1]
    wide = right.shape[0]
    copies = [
        pltpu.make_async_copy(shift, bits, sems.at[0]),
        pltpu.make_async_copy(rops.at[:, :wide], rops_now, sems.at[1]),
        pltpu.make_async_copy(psi, psi_all, sems.at[2]),
    ]
    lcopies = [pltpu.make_async_copy(lops.at[t], lops_all.at[t], lsems.at[t]) for t in range(terms)]
    later = []
    if wide < rops.shape[1]:
        later = [pltpu.make_async_copy(rops.at[:, wide:], rops_rest, sems.at[3])]
    for copy in copies[:2] + lcopies + copies[2:] + later:
        copy.start()
    for copy in copies[:2]:
        copy.wait()
    core = lax.rem(lax.axis_index("op"), CORES)
    for t in range(terms):
        kept = (bits[t] + core == 1).astype(jnp.float32)
        chosen[t, 0] = jnp.full((16, size), kept, jnp.float32).astype(jnp.bfloat16)
        chosen[t, 1] = jnp.full((16, size), 1.0 - kept, jnp.float32).astype(jnp.bfloat16)
    for r in range(wide):
        choose_class(rops_now, chosen, right, r)
    for t in range(terms):
        lcopies[t].wait()
        choose_rows(lops_all, aheads, left, t)
    copies[2].wait()
    products(left, psi_all, right, inner, send, keep, 0)
    for copy in later:
        copy.wait()


def first_own(lops, psi, right, after, send, keep, left, inner):
    for t in range(lops.shape[0]):
        choose_rows(lops, [0], left, t)
    products(left, psi, right, inner, send, keep, 0)


def later_others(start, skip, left, psi, rops, chosen, send, keep, right, inner):
    for r in range(right.shape[0]):
        choose_class(rops.at[:, start - skip:], chosen, right, r)
    products(left, psi, right, inner, send, keep, start)


def later_own(start, left, psi, right, after, send, keep, inner):
    products(left, psi, right, inner, send, keep, start)


def call(kernel, operands, in_specs, out_shape, scratch, macs=1):
    return pl.pallas_call(
        kernel,
        in_specs=in_specs,
        out_specs=[VMEM] * len(out_shape),
        out_shape=out_shape,
        scratch_shapes=scratch,
        compiler_params=PARAMS,
        cost_estimate=pl.CostEstimate(flops=macs, bytes_accessed=1024, transcendentals=0),
    )(*operands)


def add_cores(keep, arrived):
    others = keep.shape[0]

    def kernel(a, b, *outs):
        for at, out in enumerate(outs):
            out[...] = a[at] + b[at]

    shape = jax.ShapeDtypeStruct(keep.shape[1:], jnp.float32)
    return pl.pallas_call(
        kernel, in_specs=[VMEM] * 2, out_specs=[VMEM] * others, out_shape=[shape] * others, compiler_params=PARAMS
    )(keep, arrived)


def add_chips(*pieces):
    def kernel(*refs):
        total = refs[0][...]
        for ref in refs[1:-1]:
            total = total + ref[...]
        refs[-1][...] = total

    shape = jax.ShapeDtypeStruct(pieces[0].shape, jnp.float32)
    return pl.pallas_call(
        kernel, in_specs=[VMEM] * len(pieces), out_specs=VMEM, out_shape=shape, compiler_params=PARAMS
    )(*pieces)


def other_rows(moved):
    def kernel(a, out):
        out[...] = a[1 - lax.rem(lax.axis_index("op"), CORES)]

    shape = jax.ShapeDtypeStruct(moved.shape[1:], jnp.float32)
    return pl.pallas_call(
        kernel, in_specs=[VMEM], out_specs=VMEM, out_shape=shape, compiler_params=PARAMS
    )(moved)


def settle(moved, swapped):
    count = len(moved)
    _, slots, _, rows, size = moved[0].shape
    places = [(i, r) for i, value in enumerate(moved) for r in range(value.shape[2])]
    across = len(places)
    n_left, n_right = lax.axis_size("lsec"), lax.axis_size("rsec")

    def kernel(*refs):
        out = refs[-1]
        core = lax.rem(lax.axis_index("op"), CORES)
        mine_l, mine_r = lax.axis_index("lsec"), lax.axis_index("rsec")
        first_l, last_l = (mine_l == 0).astype(jnp.int32), (mine_l == n_left - 1).astype(jnp.int32)
        first_r, last_r = (mine_r == 0).astype(jnp.int32), (mine_r == n_right - 1).astype(jnp.int32)
        out[...] = jnp.zeros_like(out)
        for kept in (True, False):
            rising = core == 0 if kept else core == 1
            step_l = jnp.where(rising, first_l, -last_l)
            step_r = jnp.where(rising, -last_r, first_r)
            for l in range(slots):
                for r, (chunk, at) in enumerate(places):
                    to_l, to_r = l + step_l, r + step_r

                    @pl.when((to_l >= 0) & (to_l < slots) & (to_r >= 0) & (to_r < across))
                    def _():
                        block = refs[chunk][core, l, at] if kept else refs[count + chunk][l, at]
                        out[to_l, to_r] += block

    return pl.pallas_call(
        kernel,
        in_specs=[VMEM] * (2 * count),
        out_specs=VMEM,
        out_shape=jax.ShapeDtypeStruct((slots, across, rows, size), jnp.float32),
        compiler_params=PARAMS,
    )(*moved, *swapped)


def shards(wavefn, left_ops, right_ops, term_shift):
    n_op, n_left, n_right = (lax.axis_size(axis) for axis in ("op", "lsec", "rsec"))
    across = wavefn.shape[1]
    cores = [(i, i ^ 1) for i in range(n_op)]

    def ahead(value, by):
        return lax.ppermute(value, "op", [(i, (i + CORES * by) % n_op) for i in range(n_op)])

    def sectors(value):
        def place(o, l, r):
            return (o * n_left + l % n_left) * n_right + r % n_right

        perm = [
            (place(o, l, r), place(o, l - 1, r + 1) if o % CORES else place(o, l + 1, r - 1))
            for o in range(n_op) for l in range(n_left) for r in range(n_right)
        ]
        return lax.ppermute(value, ("op", "lsec", "rsec"), perm)

    terms, slots, size, _ = left_ops.shape
    ny = n_op // CORES
    share = size // ny
    f32, bf16 = jnp.float32, jnp.bfloat16
    depth = terms * size
    others = (ny - 1) * share

    def result(chips, wide):
        return [jax.ShapeDtypeStruct((chips, CORES, slots, wide, size // n_op, size), f32)] * 2

    def work(many):
        return [pltpu.VMEM((slots * many, 2 * depth), bf16)]

    widths = WIDTHS if sum(WIDTHS) == across else (across,)
    starts = [sum(widths[:i]) for i in range(len(widths))]
    arrived, kept, weights = [], [], []
    for start, wide in zip(starts, widths):
        right_shape = jax.ShapeDtypeStruct((wide, 2, 2 * size, depth), bf16)
        if start == 0:
            arguments = (term_shift, wavefn, left_ops, right_ops)
            send, keep, left, right, chosen, lops, psi, rops = call(
                functools.partial(first_others, range(1, ny)),
                [pltpu.with_memory_space_constraint(value, pltpu.HBM) for value in arguments],
                [HBM] * 4,
                result(ny - 1, wide) + [
                    jax.ShapeDtypeStruct((slots, terms * others, 2 * size), bf16),
                    right_shape,
                    jax.ShapeDtypeStruct((terms, 2, 16, size), bf16),
                    jax.ShapeDtypeStruct(left_ops.shape, f32),
                    jax.ShapeDtypeStruct(wavefn.shape, f32),
                    jax.ShapeDtypeStruct((terms, max(across - wide, 1), size, size), f32),
                ],
                [
                    pltpu.SMEM(term_shift.shape, jnp.int32),
                    pltpu.VMEM((terms, wide, size, size), f32),
                    *work(others),
                    pltpu.SemaphoreType.DMA((4,)),
                    pltpu.SemaphoreType.DMA((terms,)),
                ],
            )
        else:
            send, keep, right = call(
                functools.partial(later_others, start, widths[0]),
                [left, psi, rops, chosen],
                [VMEM] * 4,
                result(ny - 1, wide) + [right_shape],
                work(others),
            )
        arrived.append(lax.ppermute(send, "op", cores))
        kept.append(keep)
        weights.append(right)
    moved = []
    for start, wide, keep, came, right in zip(starts, widths, kept, arrived, weights):
        sums = add_cores(keep, came)
        came = [ahead(value, by) for by, value in enumerate(sums, 1)]
        if start == 0:
            send, keep, own = call(
                first_own,
                [lops, psi, right, sums[0]],
                [VMEM] * 3 + [ANY],
                result(1, wide) + [jax.ShapeDtypeStruct((slots, terms * share, 2 * size), bf16)],
                work(share),
            )
        else:
            send, keep = call(
                functools.partial(later_own, start),
                [own, psi, right, sums[0]],
                [VMEM] * 3 + [ANY],
                result(1, wide),
                work(share),
            )
        swapped = lax.ppermute(send, "op", cores)
        moved.append(sectors(add_chips(add_chips(keep[0], *came), swapped[0])))
    swapped = [lax.ppermute(other_rows(value), "op", cores) for value in moved]
    return settle(moved, swapped)


def solution(mesh):
    placed = (
        P("lsec", "rsec", None, None),
        P("op", "lsec", None, None),
        P("op", "rsec", None, None),
        P("op"),
    )
    return jax.shard_map(
        shards, mesh=mesh, in_specs=placed, out_specs=P("lsec", "rsec", "op", None), check_vma=False
    )
```

```python
import functools

import jax
import jax.numpy as jnp
from jax import lax
from jax.experimental import pallas as pl
from jax.experimental.pallas import tpu as pltpu
from jax.sharding import PartitionSpec as P

WIDTHS = (2, 2)
CORES = 2
LIMIT = 32 * 1024 * 1024
NT = (((1,), (1,)), ((), ()))
PARAMS = pltpu.CompilerParams(vmem_limit_bytes=LIMIT)
HBM = pl.BlockSpec(memory_space=pltpu.HBM)
VMEM = pl.BlockSpec(memory_space=pltpu.VMEM)
ANY = pl.BlockSpec(memory_space=pl.ANY)


def position(core, l, slots):
    return jnp.where(core == 0, l, slots - 1 - l)


def split(value):
    high = value.astype(jnp.bfloat16)
    low = (value - high.astype(jnp.float32)).astype(jnp.bfloat16)
    return high, low


def choose_rows(lops, left, t):
    _, slots, many, _ = lops.shape
    for l in range(slots):
        left[l, t * many:(t + 1) * many, :] = jnp.concatenate(split(lops[t, l]), axis=1)


def choose_class(rops, chosen, right, r):
    terms, _, size, _ = rops.shape
    for t in range(terms):
        high, low = (part.reshape(-1, 16, size) for part in split(rops[t, r]))
        for way in range(2):
            at = (slice(way * size, (way + 1) * size), slice(t * size, (t + 1) * size))
            right[r, 0, *at] = (high * chosen[t, way]).reshape(size, size)
            right[r, 1, *at] = (low * chosen[t, way]).reshape(size, size)


def products(left, psi, right, inner, send, keep, start):
    slots, height, twice = left.shape
    size = twice // 2
    wide = right.shape[0]
    depth = right.shape[3]
    terms = depth // size
    many = height // terms
    rows = keep.shape[-2]
    core = lax.rem(lax.axis_index("op"), CORES)
    for r in range(wide):
        for l in range(slots):
            both = jnp.concatenate(split(psi[l, start + r]), axis=1)
            out = jnp.dot(left[l], jnp.concatenate([both, both], axis=0), preferred_element_type=jnp.float32)
            for t in range(terms):
                block = out[t * many:(t + 1) * many]
                high, low = split(block[:, :size] + block[:, size:])
                inner[l * many:(l + 1) * many, t * size:(t + 1) * size] = high
                inner[l * many:(l + 1) * many, depth + t * size:depth + (t + 1) * size] = low
        out = lax.dot_general(
            jnp.concatenate([inner[...], inner[:, :depth]], axis=1),
            jnp.concatenate([right[r, 0], right[r, 0], right[r, 1]], axis=1),
            NT, preferred_element_type=jnp.float32,
        )
        for l in range(slots):
            here, there = position(core, l, slots), position(1 - core, l, slots)
            for block in range(many // rows):
                at = l * many + block * rows
                keep[block // CORES, block % CORES, here, r] = out[at:at + rows, :size]
                send[block // CORES, block % CORES, there, r] = out[at:at + rows, size:]


def first_others(
    shift, psi, lops, rops, send, keep, left, right, chosen, lops_own, psi_all, rops_rest,
    bits, rops_now, lops_now, inner, sems, lsems,
):
    terms, slots, size, _ = lops.shape
    wide = right.shape[0]
    core = lax.rem(lax.axis_index("op"), CORES)
    mine = lax.axis_index("op") // CORES
    ny = lax.axis_size("op") // CORES
    share = size // ny

    def rows(t, ahead, target, sem):
        at = pl.multiple_of(lax.rem(mine + ahead, ny) * share, share)
        return pltpu.make_async_copy(lops.at[t, :, pl.ds(at, share)], target, sem)

    copies = [
        pltpu.make_async_copy(shift, bits, sems.at[0]),
        pltpu.make_async_copy(rops.at[:, :wide], rops_now, sems.at[1]),
        pltpu.make_async_copy(psi.at[:, :wide], psi_all.at[:, :wide], sems.at[2]),
    ]
    lcopies = [
        [
            rows(t, ahead, lops_now.at[t, :, pl.ds((ahead - 1) * share, share)], lsems.at[t, ahead])
            for ahead in range(1, ny)
        ]
        for t in range(terms)
    ]
    later = [rows(t, 0, lops_own.at[t], lsems.at[t, 0]) for t in range(terms)]
    if wide < rops.shape[1]:
        later += [
            pltpu.make_async_copy(rops.at[:, wide:], rops_rest, sems.at[3]),
            pltpu.make_async_copy(psi.at[:, wide:], psi_all.at[:, wide:], sems.at[4]),
        ]
    for copy in copies + sum(lcopies, []):
        copy.start()
    for copy in copies[:2]:
        copy.wait()
    for t in range(terms):
        kept = (bits[t] + core == 1).astype(jnp.float32)
        chosen[t, 0] = jnp.full((16, size), kept, jnp.float32).astype(jnp.bfloat16)
        chosen[t, 1] = jnp.full((16, size), 1.0 - kept, jnp.float32).astype(jnp.bfloat16)
    for r in range(wide):
        choose_class(rops_now, chosen, right, r)
    for t in range(terms):
        for copy in lcopies[t]:
            copy.wait()
        choose_rows(lops_now, left, t)
    copies[2].wait()
    for copy in later:
        copy.start()
    products(left, psi_all, right, inner, send, keep, 0)
    for copy in later:
        copy.wait()


def part(send_all, send, far, before):
    near = send.shape[2]
    start = far.shape[3] - send.shape[3]
    send[...] = send_all[:, :, :near]
    far[:, :, :, start:] = send_all[:, :, near:]
    if start:
        far[:, :, :, :start] = before[...]


def first_own(lops, psi, right, after, send, far, keep, left, send_all, inner):
    for t in range(lops.shape[0]):
        choose_rows(lops, left, t)
    products(left, psi, right, inner, send_all, keep, 0)
    part(send_all, send, far, None)


def later_others(start, skip, left, psi, rops, chosen, send, keep, right, inner):
    for r in range(right.shape[0]):
        choose_class(rops.at[:, start - skip:], chosen, right, r)
    products(left, psi, right, inner, send, keep, start)


def later_own(start, left, psi, right, before, after, send, far, keep, send_all, inner):
    products(left, psi, right, inner, send_all, keep, start)
    part(send_all, send, far, before)


def call(kernel, operands, in_specs, out_shape, scratch=()):
    return pl.pallas_call(
        kernel,
        in_specs=in_specs,
        out_specs=[VMEM] * len(out_shape),
        out_shape=out_shape,
        scratch_shapes=scratch,
        compiler_params=PARAMS,
        cost_estimate=pl.CostEstimate(flops=1, bytes_accessed=1024, transcendentals=0),
    )(*operands)


def sums(kernel, count, shape, operands, after=None):
    reads = len(operands)
    specs = [VMEM] * reads

    def body(*refs):
        kernel(refs[:reads], refs[-count:])

    if after is not None:
        operands = [*operands, after]
        specs.append(ANY)
    return call(body, operands, specs, [jax.ShapeDtypeStruct(shape, jnp.float32)] * count)


def settle(moved, swapped):
    count = len(moved)
    rows, size = moved[0].shape[-2:]
    slots = sum(value.shape[1] for value in (moved[0], moved[-1]))
    across = moved[-1].shape[2]
    n_left, n_right = lax.axis_size("lsec"), lax.axis_size("rsec")

    def kernel(refs, outs):
        refs, every = refs[:2 * count], outs[1]
        core = lax.rem(lax.axis_index("op"), CORES)
        mine_l, mine_r = lax.axis_index("lsec"), lax.axis_index("rsec")
        first_l, last_l = (mine_l == 0).astype(jnp.int32), (mine_l == n_left - 1).astype(jnp.int32)
        first_r, last_r = (mine_r == 0).astype(jnp.int32), (mine_r == n_right - 1).astype(jnp.int32)
        steps = []
        for side, way in enumerate((core, 1 - core)):
            steps.append((jnp.where(way == 0, first_l, -last_l), jnp.where(way == 0, -last_r, first_r)))
            start = 0
            for i, value in enumerate(moved):
                _, tall, wide, _, _ = value.shape
                last = i == count - 1
                for p in range(tall):
                    l = position(way, slots - 1 if last else p, slots)
                    for r in range(wide):
                        at = r if last else start + r
                        every[side, l, at] = refs[count + i][p, r] if side else refs[i][core, p, r]
                start += wide
        for l in range(slots):
            for r in range(across):
                total = jnp.zeros((rows, size), jnp.float32)
                for side, (step_l, step_r) in enumerate(steps):
                    from_l, from_r = l - step_l, r - step_r
                    inside = (from_l >= 0) & (from_l < slots) & (from_r >= 0) & (from_r < across)
                    block = every[side, jnp.clip(from_l, 0, slots - 1), jnp.clip(from_r, 0, across - 1)]
                    total = total + jnp.where(inside, block, 0.0)
                outs[0][l, r] = total

    def body(*refs):
        kernel(refs[:2 * count], refs[2 * count:])

    return call(
        body, [*moved, *swapped], [VMEM] * (2 * count),
        [jax.ShapeDtypeStruct((slots, across, rows, size), jnp.float32)],
        [pltpu.VMEM((2, slots, across, rows, size), jnp.float32)],
    )[0]


def shards(wavefn, left_ops, right_ops, term_shift):
    n_op, n_left, n_right = (lax.axis_size(axis) for axis in ("op", "lsec", "rsec"))
    across = wavefn.shape[1]
    terms, slots, size, _ = left_ops.shape
    ny = n_op // CORES
    share = size // ny
    others = (ny - 1) * share
    rows = size // n_op
    depth = terms * size
    near = slots - 1
    f32, bf16 = jnp.float32, jnp.bfloat16
    cores = [(i, i ^ 1) for i in range(n_op)]

    def place(o, l, r):
        return (o % n_op * n_left + l % n_left) * n_right + r % n_right

    def permute(value, target, inside=False):
        perm = [
            (place(o, l, r), target(o, l, r))
            for o in range(n_op) for l in range(n_left) for r in range(n_right)
            if not inside or l != (0 if o % CORES else n_left - 1)
        ]
        return lax.ppermute(value, ("op", "lsec", "rsec"), perm)

    def ahead(value, by, inside=False):
        return permute(value, lambda o, l, r: place(o + CORES * by, l, r), inside)

    def sectors(value, inside=False):
        return permute(
            value, lambda o, l, r: place(o, l - 1, r + 1) if o % CORES else place(o, l + 1, r - 1), inside
        )

    def result(chips, wide):
        return [jax.ShapeDtypeStruct((chips, CORES, slots, wide, rows, size), f32)] * 2

    def work(many):
        return [pltpu.VMEM((slots * many, 2 * depth), bf16)]

    widths = WIDTHS if sum(WIDTHS) == across else (across,)
    spans = [(sum(widths[:i]), wide) for i, wide in enumerate(widths)]

    arrived, kept, weights = [], [], []
    for start, wide in spans:
        right_shape = jax.ShapeDtypeStruct((wide, 2, 2 * size, depth), bf16)
        if start == 0:
            arguments = (term_shift, wavefn, left_ops, right_ops)
            send, keep, left, right, chosen, lops, psi, rops = call(
                first_others,
                [pltpu.with_memory_space_constraint(value, pltpu.HBM) for value in arguments],
                [HBM] * 4,
                result(ny - 1, wide) + [
                    jax.ShapeDtypeStruct((slots, terms * others, 2 * size), bf16),
                    right_shape,
                    jax.ShapeDtypeStruct((terms, 2, 16, size), bf16),
                    jax.ShapeDtypeStruct((terms, slots, share, size), f32),
                    jax.ShapeDtypeStruct(wavefn.shape, f32),
                    jax.ShapeDtypeStruct((terms, max(across - wide, 1), size, size), f32),
                ],
                [
                    pltpu.SMEM(term_shift.shape, jnp.int32),
                    pltpu.VMEM((terms, wide, size, size), f32),
                    pltpu.VMEM((terms, slots, others, size), f32),
                    *work(others),
                    pltpu.SemaphoreType.DMA((5,)),
                    pltpu.SemaphoreType.DMA((terms, ny)),
                ],
            )
        else:
            send, keep, right = call(
                functools.partial(later_others, start, widths[0]),
                [left, psi, rops, chosen],
                [VMEM] * 4,
                result(ny - 1, wide) + [right_shape],
                work(others),
            )
        arrived.append(lax.ppermute(send, "op", cores))
        kept.append(keep)
        weights.append(right)

    def add_cores(refs, outs):
        for at, out in enumerate(outs):
            out[...] = refs[0][at, :, :near] + refs[1][at, :, :near]

    def add_chips(refs, outs):
        total = refs[0][0, :, :near]
        for ref in refs[1:]:
            total = total + ref[...]
        outs[0][...] = total

    def add_own(refs, outs):
        outs[0][...] = refs[0][...] + refs[1][0]

    def add_cores_far(refs, outs):
        for at, out in enumerate(outs):
            for (start, wide), a, b in zip(spans, refs[:len(spans)], refs[len(spans):]):
                out[:, :, start:start + wide] = a[at, :, near:] + b[at, :, near:]

    def add_all_far(refs, outs):
        for i, (start, wide) in enumerate(spans):
            total = refs[i][0, :, near:] + refs[len(spans)][0, :, :, start:start + wide]
            for ref in refs[len(spans) + 1:]:
                total = total + ref[:, :, start:start + wide]
            outs[0][:, :, start:start + wide] = total

    moved, own_kept, summed = [], [], []
    for (start, wide), keep, came, right in zip(spans, kept, arrived, weights):
        shape = (CORES, near, wide, rows, size)
        pieces = sums(add_cores, ny - 1, shape, [keep, came])
        came = [ahead(value, by) for by, value in enumerate(pieces, 1)]
        whole = (1, CORES, slots, wide, rows, size)
        pieces_out = [
            jax.ShapeDtypeStruct((1, CORES, near, wide, rows, size), f32),
            jax.ShapeDtypeStruct((1, CORES, slots - near, start + wide, rows, size), f32),
            jax.ShapeDtypeStruct(whole, f32),
        ]
        scratch = [pltpu.VMEM(whole, f32), *work(share)]
        if start == 0:
            send, far, keep, own = call(
                first_own,
                [lops, psi, right, pieces[0]],
                [VMEM] * 3 + [ANY],
                pieces_out + [jax.ShapeDtypeStruct((slots, terms * share, 2 * size), bf16)],
                scratch,
            )
        else:
            send, far, keep = call(
                functools.partial(later_own, start),
                [own, psi, right, far, pieces[0]],
                [VMEM] * 4 + [ANY],
                pieces_out,
                scratch,
            )
        own_kept.append(keep)
        own_arrived = lax.ppermute(send, "op", cores)
        total = sums(add_chips, 1, shape, [keep, *came])[0]
        summed.append(sums(add_own, 1, shape, [total, own_arrived])[0])
        moved.append(sectors(summed[-1]))

    far_arrived = lax.ppermute(far, "op", cores)

    def other_rows(value, after=None):
        def kernel(refs, outs):
            outs[0][...] = refs[0][1 - lax.rem(lax.axis_index("op"), CORES)]

        return sums(kernel, 1, value.shape[1:], [value], after)[0]

    swapped = [other_rows(value) for value in moved]
    shape = (CORES, slots - near, across, rows, size)
    pieces = sums(add_cores_far, ny - 1, shape, [*kept, *arrived], summed[0])
    came = [ahead(value, by, True) for by, value in enumerate(pieces, 1)]
    total = sums(add_all_far, 1, shape, [*own_kept, far_arrived, *came], swapped[0])[0]
    moved.append(sectors(total, True))
    swapped.append(other_rows(moved[-1]))
    return settle(moved, [lax.ppermute(value, "op", cores) for value in swapped])


def solution(mesh):
    placed = (
        P("lsec", "rsec", None, None),
        P("op", "lsec", None, None),
        P("op", "rsec", None, None),
        P("op"),
    )
    return jax.shard_map(
        shards, mesh=mesh, in_specs=placed, out_specs=P("lsec", "rsec", "op", None), check_vma=False
    )
```

```python
import functools

import jax
import jax.numpy as jnp
from jax import lax
from jax.experimental import pallas as pl
from jax.experimental.pallas import tpu as pltpu
from jax.sharding import PartitionSpec as P

WIDTHS = (2, 1, 1)
CORES = 2
LIMIT = 32 * 1024 * 1024
NT = (((1,), (1,)), ((), ()))
PARAMS = pltpu.CompilerParams(vmem_limit_bytes=LIMIT)
HBM = pl.BlockSpec(memory_space=pltpu.HBM)
VMEM = pl.BlockSpec(memory_space=pltpu.VMEM)
ANY = pl.BlockSpec(memory_space=pl.ANY)


def split(value):
    high = value.astype(jnp.bfloat16)
    low = (value - high.astype(jnp.float32)).astype(jnp.bfloat16)
    return high, low


def choose_rows(lops, aheads, left, t):
    _, slots, size, _ = lops.shape
    ny = lax.axis_size("op") // CORES
    mine = lax.axis_index("op") // CORES
    share = size // ny
    many = share * len(aheads)
    for l in range(slots):
        rows = [
            lops[t, l, pl.ds(pl.multiple_of(lax.rem(mine + ahead, ny) * share, share), share), :]
            for ahead in aheads
        ]
        left[l, t * many:(t + 1) * many, :] = jnp.concatenate(split(jnp.concatenate(rows, axis=0)), axis=1)


def choose_class(rops, chosen, right, r):
    terms, _, size, _ = rops.shape
    for t in range(terms):
        high, low = (part.reshape(-1, 16, size) for part in split(rops[t, r]))
        for way in range(2):
            at = (slice(way * size, (way + 1) * size), slice(t * size, (t + 1) * size))
            right[r, 0, *at] = (high * chosen[t, way]).reshape(size, size)
            right[r, 1, *at] = (low * chosen[t, way]).reshape(size, size)


def products(left, psi, right, inner, done, send, keep, start):
    slots, height, twice = left.shape
    size = twice // 2
    wide, _, _, depth = right.shape
    terms = depth // size
    many = height // terms
    chips, blocks, rows, _ = keep.shape
    near = blocks // (CORES * wide)
    core = lax.rem(lax.axis_index("op"), CORES)
    x = lax.axis_index("lsec")
    for r in range(wide):
        for l in range(slots):
            both = jnp.concatenate(split(psi[l, start + r]), axis=1)
            out = jnp.dot(left[l], jnp.concatenate([both, both], axis=0), preferred_element_type=jnp.float32)
            for t in range(terms):
                block = out[t * many:(t + 1) * many]
                high, low = split(block[:, :size] + block[:, size:])
                inner[l * many:(l + 1) * many, t * size:(t + 1) * size] = high
                inner[l * many:(l + 1) * many, depth + t * size:depth + (t + 1) * size] = low
        done[...] = lax.dot_general(
            jnp.concatenate([inner[...], inner[:, :depth]], axis=1),
            jnp.concatenate([right[r, 0], right[r, 0], right[r, 1]], axis=1),
            NT, preferred_element_type=jnp.float32,
        )

        def take(l, chip, c, way):
            at = pl.ds(pl.multiple_of(l * many + (chip * CORES + c) * rows, rows), rows)
            return done[at, pl.ds(pl.multiple_of(way * size, size), size)]

        for chip in range(chips):
            for p in range(near):
                up, down = jnp.where(core == 0, p, slots - 1 - p), jnp.where(core == 0, slots - 1 - p, p)
                for c in range(CORES):
                    at = (c * near + p) * wide + r
                    keep[chip, at] = take(up, chip, c, 0)
                    send[chip, at] = take(down, chip, c, 1)
            if near < slots:
                at = CORES * near * wide + r
                l, way = jnp.where(x == 0, slots - 1, 0), jnp.where(core == x, 0, 1)
                keep[chip, at] = take(l, chip, core, way)
                send[chip, at] = take(l, chip, 1 - core, way)


def first_others(aheads, shift, psi, lops, rops, send, keep, left, right, chosen, lops_all, psi_all, rops_rest, *refs):
    bits, rops_now, inner, done, sems, lsems = refs
    terms = lops.shape[0]
    size = psi.shape[-1]
    wide = right.shape[0]
    copies = [
        pltpu.make_async_copy(shift, bits, sems.at[0]),
        pltpu.make_async_copy(rops.at[:, :wide], rops_now, sems.at[1]),
        pltpu.make_async_copy(psi, psi_all, sems.at[2]),
    ]
    lcopies = [pltpu.make_async_copy(lops.at[t], lops_all.at[t], lsems.at[t]) for t in range(terms)]
    later = []
    if wide < rops.shape[1]:
        later = [pltpu.make_async_copy(rops.at[:, wide:], rops_rest, sems.at[3])]
    for copy in copies[:2] + lcopies + copies[2:] + later:
        copy.start()
    for copy in copies[:2]:
        copy.wait()
    core = lax.rem(lax.axis_index("op"), CORES)
    for t in range(terms):
        kept = (bits[t] + core == 1).astype(jnp.float32)
        chosen[t, 0] = jnp.full((16, size), kept, jnp.float32).astype(jnp.bfloat16)
        chosen[t, 1] = jnp.full((16, size), 1.0 - kept, jnp.float32).astype(jnp.bfloat16)
    for r in range(wide):
        choose_class(rops_now, chosen, right, r)
    for t in range(terms):
        lcopies[t].wait()
        choose_rows(lops_all, aheads, left, t)
    copies[2].wait()
    products(left, psi_all, right, inner, done, send, keep, 0)
    for copy in later:
        copy.wait()


def first_own(lops, psi, right, after, send, keep, left, inner, done):
    for t in range(lops.shape[0]):
        choose_rows(lops, [0], left, t)
    products(left, psi, right, inner, done, send, keep, 0)


def later_others(start, skip, left, psi, rops, chosen, after, send, keep, right, inner, done):
    for r in range(right.shape[0]):
        choose_class(rops.at[:, start - skip:], chosen, right, r)
    products(left, psi, right, inner, done, send, keep, start)


def later_own(start, left, psi, right, after, send, keep, inner, done):
    products(left, psi, right, inner, done, send, keep, start)


def call(kernel, operands, in_specs, out_shape, scratch=()):
    return pl.pallas_call(
        kernel,
        in_specs=in_specs,
        out_specs=[VMEM] * len(out_shape),
        out_shape=out_shape,
        scratch_shapes=scratch,
        compiler_params=PARAMS,
        cost_estimate=pl.CostEstimate(flops=1, bytes_accessed=1024, transcendentals=0),
    )(*operands)


def sums(kernel, shapes, operands, after=None):
    reads = len(operands)
    specs = [VMEM] * reads

    def body(*refs):
        kernel(refs[:reads], refs[len(specs):])

    if after is not None:
        operands = [*operands, after]
        specs.append(ANY)
    return call(body, operands, specs, [jax.ShapeDtypeStruct(shape, jnp.float32) for shape in shapes])


def settle(slots, widths, moved, swapped, far):
    rows, size = moved[0].shape[-2:]
    across = sum(widths)
    near = moved[0].shape[0] // (CORES * widths[0])
    n_left, n_right = lax.axis_size("lsec"), lax.axis_size("rsec")
    count = len(moved)

    def kernel(*refs):
        out, every = refs[-2:]
        core = lax.rem(lax.axis_index("op"), CORES)
        mine_l, mine_r = lax.axis_index("lsec"), lax.axis_index("rsec")
        first_l, last_l = (mine_l == 0).astype(jnp.int32), (mine_l == n_left - 1).astype(jnp.int32)
        first_r, last_r = (mine_r == 0).astype(jnp.int32), (mine_r == n_right - 1).astype(jnp.int32)
        steps = ((first_l, -last_r), (-last_l, first_r))
        start = 0
        for i, wide in enumerate(widths):
            for p in range(near):
                up, down = jnp.where(core == 0, p, slots - 1 - p), jnp.where(core == 0, slots - 1 - p, p)
                for r in range(wide):
                    every[core, up, start + r] = refs[i][(core * near + p) * wide + r]
                    every[1 - core, down, start + r] = refs[count + i][p * wide + r]
            start += wide
        if far:
            for r in range(across):
                block = refs[2 * count][r]
                every[0, slots - 1, r] = block
                every[1, 0, r] = block
        for l in range(slots):
            for r in range(across):
                total = jnp.zeros((rows, size), jnp.float32)
                for way, (step_l, step_r) in enumerate(steps):
                    from_l, from_r = l - step_l, r - step_r
                    inside = (from_l >= 0) & (from_l < slots) & (from_r >= 0) & (from_r < across)
                    block = every[way, jnp.clip(from_l, 0, slots - 1), jnp.clip(from_r, 0, across - 1)]
                    total = total + jnp.where(inside, block, 0.0)
                out[l, r] = total

    operands = [*moved, *swapped, *far]
    return call(
        kernel, operands, [VMEM] * len(operands),
        [jax.ShapeDtypeStruct((slots, across, rows, size), jnp.float32)],
        [pltpu.VMEM((2, slots, across, rows, size), jnp.float32)],
    )[0]


def shards(wavefn, left_ops, right_ops, term_shift):
    n_op, n_left, n_right = (lax.axis_size(axis) for axis in ("op", "lsec", "rsec"))
    across = wavefn.shape[1]
    terms, slots, size, _ = left_ops.shape
    ny = n_op // CORES
    share = size // ny
    others = (ny - 1) * share
    rows = size // n_op
    depth = terms * size
    trim = n_left == 2
    near = slots - 1 if trim else slots
    f32, bf16 = jnp.float32, jnp.bfloat16

    def permute(value, target):
        def place(o, l, r):
            return (o % n_op * n_left + l % n_left) * n_right + r % n_right

        perm = [
            (place(o, l, r), place(*target(o, l, r)))
            for o in range(n_op) for l in range(n_left) for r in range(n_right)
        ]
        return lax.ppermute(value, ("op", "lsec", "rsec"), perm)

    def swap(value):
        return permute(value, lambda o, l, r: (o ^ 1, l, r))

    def ahead(value, by):
        return permute(value, lambda o, l, r: (o + CORES * by, l, r))

    def sectors(value):
        return permute(value, lambda o, l, r: (o, l - 1, r + 1) if o % CORES else (o, l + 1, r - 1))

    def farthest(value):
        return permute(value, lambda o, l, r: (o, 0, r + 1) if l else (o, 1, r - 1))

    def total_blocks(wide):
        return (CORES * near + trim) * wide

    def result(chips, wide):
        return [jax.ShapeDtypeStruct((chips, total_blocks(wide), rows, size), f32)] * 2

    def work(many):
        return [pltpu.VMEM((slots * many, 2 * depth), bf16), pltpu.VMEM((slots * many, 2 * size), f32)]

    def add_cores(refs, outs):
        for at, out in enumerate(outs):
            out[...] = refs[0][at] + refs[1][at]

    def add_chips(refs, outs):
        total = refs[0][0]
        for ref in refs[1:]:
            total = total + ref[...]
        outs[0][...] = total

    def add_own(refs, outs):
        total = refs[0][...] + refs[1][0]
        blocks = outs[0].shape[0]
        outs[0][...] = total[:blocks]
        if trim:
            before = outs[1].shape[0] - (total.shape[0] - blocks)
            outs[1][before:] = total[blocks:]
            if before:
                outs[1][:before] = refs[2][...]

    def other_rows(refs, outs):
        count = outs[0].shape[0]
        outs[0][...] = refs[0][pl.ds((1 - lax.rem(lax.axis_index("op"), CORES)) * count, count)]

    widths = WIDTHS if sum(WIDTHS) == across else (across,)
    starts = [sum(widths[:i]) for i in range(len(widths))]
    count = len(widths)
    kept, arrived, weights, pieces, own_kept, own_arrived, summed, moved, swapped = ([] for _ in range(9))
    far = []

    def work_others(i):
        nonlocal left, chosen, lops, psi, rops
        wide, start = widths[i], starts[i]
        right_shape = jax.ShapeDtypeStruct((wide, 2, 2 * size, depth), bf16)
        if i == 0:
            arguments = (term_shift, wavefn, left_ops, right_ops)
            send, keep, left, right, chosen, lops, psi, rops = call(
                functools.partial(first_others, range(1, ny)),
                [pltpu.with_memory_space_constraint(value, pltpu.HBM) for value in arguments],
                [HBM] * 4,
                result(ny - 1, wide) + [
                    jax.ShapeDtypeStruct((slots, terms * others, 2 * size), bf16),
                    right_shape,
                    jax.ShapeDtypeStruct((terms, 2, 16, size), bf16),
                    jax.ShapeDtypeStruct(left_ops.shape, f32),
                    jax.ShapeDtypeStruct(wavefn.shape, f32),
                    jax.ShapeDtypeStruct((terms, max(across - wide, 1), size, size), f32),
                ],
                [
                    pltpu.SMEM(term_shift.shape, jnp.int32),
                    pltpu.VMEM((terms, wide, size, size), f32),
                    *work(others),
                    pltpu.SemaphoreType.DMA((4,)),
                    pltpu.SemaphoreType.DMA((terms,)),
                ],
            )
        else:
            send, keep, right = call(
                functools.partial(later_others, start, widths[0]),
                [left, psi, rops, chosen, own_kept[i - 2] if i > 1 else kept[0]],
                [VMEM] * 4 + [ANY],
                result(ny - 1, wide) + [right_shape],
                work(others),
            )
        kept.append(keep)
        weights.append(right)
        arrived.append(swap(send))

    def work_own(i):
        nonlocal own
        wide = widths[i]
        if i == 0:
            send, keep, own = call(
                first_own,
                [lops, psi, weights[i], pieces[i][0]],
                [VMEM] * 3 + [ANY],
                result(1, wide) + [jax.ShapeDtypeStruct((slots, terms * share, 2 * size), bf16)],
                work(share),
            )
        else:
            send, keep = call(
                functools.partial(later_own, starts[i]),
                [own, psi, weights[i], pieces[i][0]],
                [VMEM] * 3 + [ANY],
                result(1, wide),
                work(share),
            )
        own_kept.append(keep)
        own_arrived.append(swap(send))

    def start_chips(i):
        shape = (total_blocks(widths[i]), rows, size)
        pieces.append(sums(add_cores, [shape] * (ny - 1), [kept[i], arrived[i]], summed[i - 2] if i > 1 else None))

    def finish_chips(i):
        nonlocal far
        shape = (total_blocks(widths[i]), rows, size)
        came = [ahead(value, by) for by, value in enumerate(pieces[i], 1)]
        after = None
        if i > 1:
            after = swapped[i - 2]
        elif i + 1 < count:
            after = pieces[i + 1][0]
        total = sums(add_chips, [shape], [own_kept[i], *came], after)[0]
        shapes = [(CORES * near * widths[i], rows, size)]
        if trim:
            shapes.append((starts[i] + widths[i], rows, size))
        value, *far = sums(add_own, shapes, [total, own_arrived[i], *far])
        summed.append(value)
        moved.append(sectors(value))
        swapped.append(sums(other_rows, [(near * widths[i], rows, size)], [moved[i]])[0])

    left = chosen = lops = psi = rops = own = None
    work_others(0)
    if count > 1:
        work_others(1)
    for i in range(count):
        if i < 2:
            start_chips(i)
            work_own(i)
            if i + 2 < count:
                work_others(i + 2)
    for i in range(count):
        finish_chips(i)
        if i + 2 < count:
            start_chips(i + 2)
            work_own(i + 2)
    far = [farthest(value) for value in far]
    return settle(slots, widths, moved, [swap(value) for value in swapped], far)


def solution(mesh):
    placed = (
        P("lsec", "rsec", None, None),
        P("op", "lsec", None, None),
        P("op", "rsec", None, None),
        P("op"),
    )
    return jax.shard_map(
        shards, mesh=mesh, in_specs=placed, out_specs=P("lsec", "rsec", "op", None), check_vma=False
    )
```

```python
import functools

import jax
import jax.numpy as jnp
from jax import lax
from jax.experimental import pallas as pl
from jax.experimental.pallas import tpu as pltpu
from jax.sharding import PartitionSpec as P

CORES = 2
LIMIT = 32 * 1024 * 1024
NT = (((1,), (1,)), ((), ()))
PARAMS = pltpu.CompilerParams(vmem_limit_bytes=LIMIT)
HBM = pl.BlockSpec(memory_space=pltpu.HBM)
VMEM = pl.BlockSpec(memory_space=pltpu.VMEM)
ANY = pl.BlockSpec(memory_space=pl.ANY)


def split(value):
    high = value.astype(jnp.bfloat16)
    low = (value - high.astype(jnp.float32)).astype(jnp.bfloat16)
    return high, low


def choose_rows(lops, aheads, left, t):
    _, slots, size, _ = lops.shape
    ny = lax.axis_size("op") // CORES
    mine = lax.axis_index("op") // CORES
    share = size // ny
    many = share * len(aheads)
    for l in range(slots):
        rows = [
            lops[t, l, pl.ds(pl.multiple_of(lax.rem(mine + ahead, ny) * share, share), share), :]
            for ahead in aheads
        ]
        left[l, t * many:(t + 1) * many, :] = jnp.concatenate(split(jnp.concatenate(rows, axis=0)), axis=1)


def choose_class(rops, chosen, right, r):
    terms, _, size, _ = rops.shape
    for t in range(terms):
        high, low = (part.reshape(-1, 16, size) for part in split(rops[t, r]))
        for way in range(2):
            at = (slice(way * size, (way + 1) * size), slice(t * size, (t + 1) * size))
            right[r, 0, *at] = (high * chosen[t, way]).reshape(size, size)
            right[r, 1, *at] = (low * chosen[t, way]).reshape(size, size)


def products(left, psi, right, inner, done, outs, far, prepare=None):
    slots, height, twice = left.shape
    size = twice // 2
    across, _, _, depth = right.shape
    terms = depth // size
    many = height // terms
    keep, send = outs
    chips, _, rows, _ = keep[0].shape
    near = slots - (1 if far else 0)
    core = lax.rem(lax.axis_index("op"), CORES)
    x = lax.axis_index("lsec")
    for r in range(across):
        if prepare is not None:
            prepare(r)
        for l in range(slots):
            both = jnp.concatenate(split(psi[l, r]), axis=1)
            out = jnp.dot(left[l], jnp.concatenate([both, both], axis=0), preferred_element_type=jnp.float32)
            for t in range(terms):
                block = out[t * many:(t + 1) * many]
                high, low = split(block[:, :size] + block[:, size:])
                inner[l * many:(l + 1) * many, t * size:(t + 1) * size] = high
                inner[l * many:(l + 1) * many, depth + t * size:depth + (t + 1) * size] = low
        done[...] = lax.dot_general(
            jnp.concatenate([inner[...], inner[:, :depth]], axis=1),
            jnp.concatenate([right[r, 0], right[r, 0], right[r, 1]], axis=1),
            NT, preferred_element_type=jnp.float32,
        )

        def take(l, chip, c, way):
            at = pl.ds(pl.multiple_of(l * many + (chip * CORES + c) * rows, rows), rows)
            return done[at, pl.ds(pl.multiple_of(way * size, size), size)]

        half = across // 2
        for chip in range(chips):
            for p in range(near):
                up, down = jnp.where(core == 0, p, slots - 1 - p), jnp.where(core == 0, slots - 1 - p, p)
                for c in range(CORES):
                    at = ((r % half) * CORES + c) * near + p + (far if r < half else 0)
                    keep[r // half][chip, at] = take(up, chip, c, 0)
                    send[r // half][chip, at] = take(down, chip, c, 1)
            if far:
                l, way = jnp.where(x == 0, slots - 1, 0), jnp.where(core == x, 0, 1)
                keep[0][chip, r] = take(l, chip, core, way)
                send[0][chip, r] = take(l, chip, 1 - core, way)


def others_sums(aheads, far, shift, psi, lops, rops, *refs):
    send, keep, (right, lops_all, psi_all) = refs[:2], refs[2:4], refs[4:7]
    bits, chosen, rops_all, left, inner, done, sems, lsems = refs[7:]
    terms, _, size, _ = lops.shape
    copies = [
        pltpu.make_async_copy(shift, bits, sems.at[0]),
        pltpu.make_async_copy(rops, rops_all, sems.at[1]),
        pltpu.make_async_copy(psi, psi_all, sems.at[2]),
    ]
    lcopies = [pltpu.make_async_copy(lops.at[t], lops_all.at[t], lsems.at[t]) for t in range(terms)]
    for copy in copies[:1] + lcopies + copies[1:]:
        copy.start()
    copies[0].wait()
    core = lax.rem(lax.axis_index("op"), CORES)
    for t in range(terms):
        kept = (bits[t] + core == 1).astype(jnp.float32)
        chosen[t, 0] = jnp.full((16, size), kept, jnp.float32).astype(jnp.bfloat16)
        chosen[t, 1] = jnp.full((16, size), 1.0 - kept, jnp.float32).astype(jnp.bfloat16)
    for t in range(terms):
        lcopies[t].wait()
        choose_rows(lops_all, aheads, left, t)
    for copy in copies[1:]:
        copy.wait()
    products(
        left, psi_all, right, inner, done, (keep, send), far,
        lambda r: choose_class(rops_all, chosen, right, r),
    )


def own_sums(far, lops, psi, right, after, *refs):
    send, keep, (left, inner, done) = refs[:2], refs[2:4], refs[4:]
    for t in range(lops.shape[0]):
        choose_rows(lops, [0], left, t)
    products(left, psi, right, inner, done, (keep, send), far)


def call(kernel, operands, in_specs, out_shape, scratch=()):
    return pl.pallas_call(
        kernel,
        in_specs=in_specs,
        out_specs=[VMEM] * len(out_shape),
        out_shape=out_shape,
        scratch_shapes=scratch,
        compiler_params=PARAMS,
        cost_estimate=pl.CostEstimate(flops=1, bytes_accessed=1024, transcendentals=0),
    )(*operands)


def sums(kernel, shapes, operands, after=None):
    reads = len(operands)
    specs = [VMEM] * reads

    def body(*refs):
        kernel(refs[:reads], refs[len(specs):])

    if after is not None:
        operands = [*operands, after]
        specs.append(ANY)
    return call(body, operands, specs, [jax.ShapeDtypeStruct(shape, jnp.float32) for shape in shapes])


def settle(slots, moved, swapped, far):
    half, _, near, rows, size = moved[0].shape
    across = half * len(moved)
    n_left, n_right = lax.axis_size("lsec"), lax.axis_size("rsec")
    count = len(moved)

    def kernel(*refs):
        out, every = refs[-2:]
        core = lax.rem(lax.axis_index("op"), CORES)
        mine_l, mine_r = lax.axis_index("lsec"), lax.axis_index("rsec")
        first_l, last_l = (mine_l == 0).astype(jnp.int32), (mine_l == n_left - 1).astype(jnp.int32)
        first_r, last_r = (mine_r == 0).astype(jnp.int32), (mine_r == n_right - 1).astype(jnp.int32)
        steps = ((first_l, -last_r), (-last_l, first_r))
        for r in range(across):
            for p in range(near):
                up, down = jnp.where(core == 0, p, slots - 1 - p), jnp.where(core == 0, slots - 1 - p, p)
                every[core, up, r] = refs[r // half][r % half, core, p]
                every[1 - core, down, r] = refs[count + r // half][r % half, p]
            if far:
                block = refs[2 * count][r]
                every[0, slots - 1, r] = block
                every[1, 0, r] = block
        for l in range(slots):
            for r in range(across):
                total = jnp.zeros((rows, size), jnp.float32)
                for way, (step_l, step_r) in enumerate(steps):
                    from_l, from_r = l - step_l, r - step_r
                    inside = (from_l >= 0) & (from_l < slots) & (from_r >= 0) & (from_r < across)
                    block = every[way, jnp.clip(from_l, 0, slots - 1), jnp.clip(from_r, 0, across - 1)]
                    total = total + jnp.where(inside, block, 0.0)
                out[l, r] = total

    operands = [*moved, *swapped, *far]
    return call(
        kernel, operands, [VMEM] * len(operands),
        [jax.ShapeDtypeStruct((slots, across, rows, size), jnp.float32)],
        [pltpu.VMEM((2, slots, across, rows, size), jnp.float32)],
    )[0]


def shards(wavefn, left_ops, right_ops, term_shift):
    n_op, n_left, n_right = (lax.axis_size(axis) for axis in ("op", "lsec", "rsec"))
    across = wavefn.shape[1]
    terms, slots, size, _ = left_ops.shape
    ny = n_op // CORES
    rows = size // n_op
    depth = terms * size
    trim = n_left == 2
    near = slots - 1 if trim else slots
    far = across if trim else 0
    half = across // 2
    spread = CORES * near * half
    f32, bf16 = jnp.float32, jnp.bfloat16

    def permute(value, target):
        def place(o, l, r):
            return (o % n_op * n_left + l % n_left) * n_right + r % n_right

        perm = [
            (place(o, l, r), place(*target(o, l, r)))
            for o in range(n_op) for l in range(n_left) for r in range(n_right)
        ]
        return lax.ppermute(value, ("op", "lsec", "rsec"), perm)

    def swap(value):
        return permute(value, lambda o, l, r: (o ^ 1, l, r))

    def ahead(value, by):
        return permute(value, lambda o, l, r: (o + CORES * by, l, r))

    def sectors(value):
        return permute(value, lambda o, l, r: (o, l - 1, r + 1) if o % CORES else (o, l + 1, r - 1))

    def farthest(value):
        return permute(value, lambda o, l, r: (o, 0, r + 1) if l else (o, 1, r - 1))

    def result(chips):
        return [jax.ShapeDtypeStruct((chips, blocks, rows, size), f32) for blocks in (far + spread, spread)] * 2

    def work(chips):
        many = chips * size // ny
        return [
            pltpu.VMEM((slots, terms * many, 2 * size), bf16),
            pltpu.VMEM((slots * many, 2 * depth), bf16),
            pltpu.VMEM((slots * many, 2 * size), f32),
        ]

    def add_cores(refs, outs):
        for at, out in enumerate(outs):
            out[...] = refs[0][at] + refs[1][at]

    def add_chips(refs, outs):
        total = refs[0][0]
        for ref in refs[1:]:
            total = total + ref[...]
        outs[0][...] = total

    def add_own(refs, outs):
        total = refs[0][...] + refs[1][0]
        if len(outs) > 1:
            outs[1][...] = total[:far]
        outs[0][...] = total[-spread:].reshape(outs[0].shape)

    def other_rows(refs, outs):
        for r in range(half):
            outs[0][r] = refs[0][r, 1 - lax.rem(lax.axis_index("op"), CORES)]

    arguments = (term_shift, wavefn, left_ops, right_ops)
    *results, right, lops, psi = call(
        functools.partial(others_sums, range(1, ny), far),
        [pltpu.with_memory_space_constraint(value, pltpu.HBM) for value in arguments],
        [HBM] * 4,
        result(ny - 1) + [
            jax.ShapeDtypeStruct((across, 2, 2 * size, depth), bf16),
            jax.ShapeDtypeStruct(left_ops.shape, f32),
            jax.ShapeDtypeStruct(wavefn.shape, f32),
        ],
        [
            pltpu.SMEM(term_shift.shape, jnp.int32),
            pltpu.VMEM((terms, 2, 16, size), bf16),
            pltpu.VMEM(right_ops.shape, f32),
            *work(ny - 1),
            pltpu.SemaphoreType.DMA((3,)),
            pltpu.SemaphoreType.DMA((terms,)),
        ],
    )
    send, keep = results[:2], results[2:]
    arrived = [swap(value) for value in send]
    pieces = [sums(add_cores, [keep[0].shape[1:]] * (ny - 1), [keep[0], arrived[0]])]
    results = call(
        functools.partial(own_sums, far), [lops, psi, right, pieces[0][0]], [VMEM] * 3 + [ANY], result(1), work(1)
    )
    own_send, own_keep = results[:2], results[2:]
    own_arrived = [swap(value) for value in own_send]
    pieces.append(sums(add_cores, [keep[1].shape[1:]] * (ny - 1), [keep[1], arrived[1]], own_keep[0]))
    moved, distant = [], []
    value = None
    for i in range(2):
        came = [ahead(value, by) for by, value in enumerate(pieces[i], 1)]
        total = sums(add_chips, [own_keep[i].shape[1:]], [own_keep[i], *came], value)[0]
        shapes = [(half, CORES, near, rows, size)]
        if far and not i:
            shapes.append((far, rows, size))
        value, *rest = sums(add_own, shapes, [total, own_arrived[i]], distant[0] if distant else None)
        moved.append(sectors(value))
        distant += [farthest(value) for value in rest]
    swapped = []
    ready = None
    for value in moved:
        ready = sums(other_rows, [(half, near, rows, size)], [value], ready)[0]
        swapped.append(swap(ready))
    return settle(slots, moved, swapped, distant)


def solution(mesh):
    placed = (
        P("lsec", "rsec", None, None),
        P("op", "lsec", None, None),
        P("op", "rsec", None, None),
        P("op"),
    )
    return jax.shard_map(
        shards, mesh=mesh, in_specs=placed, out_specs=P("lsec", "rsec", "op", None), check_vma=False
    )
```

```python
import functools

import jax
import jax.numpy as jnp
from jax import lax
from jax.experimental import pallas as pl
from jax.experimental.pallas import tpu as pltpu
from jax.sharding import PartitionSpec as P

WIDTHS = (2, 2)
CORES = 2
LIMIT = 32 * 1024 * 1024
NT = (((1,), (1,)), ((), ()))
PARAMS = pltpu.CompilerParams(vmem_limit_bytes=LIMIT)
HBM = pl.BlockSpec(memory_space=pltpu.HBM)
VMEM = pl.BlockSpec(memory_space=pltpu.VMEM)
ANY = pl.BlockSpec(memory_space=pl.ANY)


def split(value):
    high = value.astype(jnp.bfloat16)
    low = (value - high.astype(jnp.float32)).astype(jnp.bfloat16)
    return high, low


def choose_rows(lops, aheads, left, l):
    terms, _, size, _ = lops.shape
    ny = lax.axis_size("op") // CORES
    mine = lax.axis_index("op") // CORES
    share = size // ny
    many = share * len(aheads)
    for t in range(terms):
        rows = [
            lops[t, l, pl.ds(pl.multiple_of(lax.rem(mine + ahead, ny) * share, share), share), :]
            for ahead in aheads
        ]
        left[l, t * many:(t + 1) * many, :] = jnp.concatenate(split(jnp.concatenate(rows, axis=0)), axis=1)


def products(left, psi, right, chosen, inner, total, send, keep, start, rows_of, rops=None):
    slots, height, twice = left.shape
    size = twice // 2
    wide, terms = right.shape[:2]
    many = height // terms
    rows = keep.shape[-2]
    for r in range(wide):
        for l in range(slots):
            if r == 0 and rows_of is not None:
                rows_of(l)
            both = jnp.concatenate(split(psi[l, start + r]), axis=1)
            out = jnp.dot(left[l], jnp.concatenate([both, both], axis=0), preferred_element_type=jnp.float32)
            for t in range(terms):
                block = out[t * many:(t + 1) * many]
                parts = split(block[:, :size] + block[:, size:])
                inner[t, l * many:(l + 1) * many, :] = jnp.concatenate(parts, axis=1)
        for t in range(terms):
            if rops is not None:
                right[r, t] = jnp.concatenate(split(rops[t, r]), axis=0)
            both = right[r, t]
            out = lax.dot_general(
                inner[t], jnp.concatenate([both, both], axis=1), NT, preferred_element_type=jnp.float32
            )
            out = (out[:, :size] + out[:, size:]).reshape(-1, 8, size)
            for way in range(2):
                mine = out * chosen[t, way]
                total[way] = mine if t == 0 else total[way] + mine
        for l in range(slots):
            for block in range(many // rows):
                at = l * many + block * rows
                where = (block // CORES, block % CORES, l, r)
                lines = slice(at // 8, (at + rows) // 8)
                keep[where] = total[0, lines].reshape(rows, size)
                send[where] = total[1, lines].reshape(rows, size)


def first_others(aheads, shift, psi, lops, rops, send, keep, left, right, chosen, lops_all, psi_all, rops_rest, *refs):
    bits, rops_now, inner, total, sems = refs
    terms = lops.shape[0]
    size = psi.shape[-1]
    wide = right.shape[0]
    copies = [
        pltpu.make_async_copy(shift, bits, sems.at[0]),
        pltpu.make_async_copy(lops, lops_all, sems.at[1]),
        pltpu.make_async_copy(psi.at[:, :wide], psi_all.at[:, :wide], sems.at[2]),
        pltpu.make_async_copy(rops.at[:, :wide], rops_now, sems.at[3]),
    ]
    later = []
    if wide < rops.shape[1]:
        later = [
            pltpu.make_async_copy(psi.at[:, wide:], psi_all.at[:, wide:], sems.at[4]),
            pltpu.make_async_copy(rops.at[:, wide:], rops_rest, sems.at[5]),
        ]
    for copy in copies:
        copy.start()
    for copy in copies:
        copy.wait()
    for copy in later:
        copy.start()
    core = lax.rem(lax.axis_index("op"), CORES)
    for t in range(terms):
        kept = (bits[t] + core == 1).astype(jnp.float32)
        chosen[t, 0] = jnp.full((8, size), kept, jnp.float32)
        chosen[t, 1] = jnp.full((8, size), 1.0 - kept, jnp.float32)
    products(
        left, psi_all, right, chosen, inner, total, send, keep, 0,
        lambda l: choose_rows(lops_all, aheads, left, l), rops_now,
    )
    for copy in later:
        copy.wait()


def first_own(lops, psi, right, chosen, after, send, keep, left, inner, total):
    products(
        left, psi, right, chosen, inner, total, send, keep, 0, lambda l: choose_rows(lops, [0], left, l)
    )


def later_others(start, skip, left, psi, rops, chosen, send, keep, right, inner, total):
    products(
        left, psi, right, chosen, inner, total, send, keep, start, None, rops.at[:, start - skip:]
    )


def later_own(start, left, psi, right, chosen, after, send, keep, inner, total):
    products(left, psi, right, chosen, inner, total, send, keep, start, None)


def call(kernel, operands, in_specs, out_shape, scratch, macs=1):
    return pl.pallas_call(
        kernel,
        in_specs=in_specs,
        out_specs=[VMEM] * len(out_shape),
        out_shape=out_shape,
        scratch_shapes=scratch,
        compiler_params=PARAMS,
        cost_estimate=pl.CostEstimate(flops=macs, bytes_accessed=1024, transcendentals=0),
    )(*operands)


def add_cores(keep, arrived, after=None):
    others = keep.shape[0]

    def kernel(a, b, *refs):
        for at, out in enumerate(refs[-others:]):
            out[...] = a[at] + b[at]

    operands, specs = [keep, arrived], [VMEM] * 2
    if after is not None:
        operands.append(after)
        specs.append(ANY)
    return call(kernel, operands, specs, [jax.ShapeDtypeStruct(keep.shape[1:], jnp.float32)] * others, ())


def add_chips(*pieces):
    def kernel(*refs):
        total = refs[0][...]
        for ref in refs[1:-1]:
            total = total + ref[...]
        refs[-1][...] = total

    shape = jax.ShapeDtypeStruct(pieces[0].shape, jnp.float32)
    return pl.pallas_call(
        kernel, in_specs=[VMEM] * len(pieces), out_specs=VMEM, out_shape=shape, compiler_params=PARAMS
    )(*pieces)


def other_rows(moved):
    def kernel(a, out):
        out[...] = a[1 - lax.rem(lax.axis_index("op"), CORES)]

    shape = jax.ShapeDtypeStruct(moved.shape[1:], jnp.float32)
    return pl.pallas_call(
        kernel, in_specs=[VMEM], out_specs=VMEM, out_shape=shape, compiler_params=PARAMS
    )(moved)


def settle(moved, swapped):
    count = len(moved)
    _, slots, _, rows, size = moved[0].shape
    places = [(i, r) for i, value in enumerate(moved) for r in range(value.shape[2])]
    across = len(places)
    n_left, n_right = lax.axis_size("lsec"), lax.axis_size("rsec")

    def kernel(*refs):
        out = refs[-1]
        core = lax.rem(lax.axis_index("op"), CORES)
        mine_l, mine_r = lax.axis_index("lsec"), lax.axis_index("rsec")
        first_l, last_l = (mine_l == 0).astype(jnp.int32), (mine_l == n_left - 1).astype(jnp.int32)
        first_r, last_r = (mine_r == 0).astype(jnp.int32), (mine_r == n_right - 1).astype(jnp.int32)
        out[...] = jnp.zeros_like(out)
        for kept in (True, False):
            rising = core == 0 if kept else core == 1
            step_l = jnp.where(rising, first_l, -last_l)
            step_r = jnp.where(rising, -last_r, first_r)
            for l in range(slots):
                for r, (chunk, at) in enumerate(places):
                    to_l, to_r = l + step_l, r + step_r

                    @pl.when((to_l >= 0) & (to_l < slots) & (to_r >= 0) & (to_r < across))
                    def _():
                        block = refs[chunk][core, l, at] if kept else refs[count + chunk][l, at]
                        out[to_l, to_r] += block

    return pl.pallas_call(
        kernel,
        in_specs=[VMEM] * (2 * count),
        out_specs=VMEM,
        out_shape=jax.ShapeDtypeStruct((slots, across, rows, size), jnp.float32),
        compiler_params=PARAMS,
    )(*moved, *swapped)


def shards(wavefn, left_ops, right_ops, term_shift):
    n_op, n_left, n_right = (lax.axis_size(axis) for axis in ("op", "lsec", "rsec"))
    across = wavefn.shape[1]
    cores = [(i, i ^ 1) for i in range(n_op)]

    def ahead(value, by):
        return lax.ppermute(value, "op", [(i, (i + CORES * by) % n_op) for i in range(n_op)])

    def sectors(value):
        def place(o, l, r):
            return (o * n_left + l % n_left) * n_right + r % n_right

        perm = [
            (place(o, l, r), place(o, l - 1, r + 1) if o % CORES else place(o, l + 1, r - 1))
            for o in range(n_op) for l in range(n_left) for r in range(n_right)
        ]
        return lax.ppermute(value, ("op", "lsec", "rsec"), perm)

    terms, slots, size, _ = left_ops.shape
    ny = n_op // CORES
    share = size // ny
    f32, bf16 = jnp.float32, jnp.bfloat16
    others = (ny - 1) * share

    def result(chips, wide):
        return [jax.ShapeDtypeStruct((chips, CORES, slots, wide, size // n_op, size), f32)] * 2

    def work(many):
        return [
            pltpu.VMEM((terms, slots * many, 2 * size), bf16),
            pltpu.VMEM((2, slots * many // 8, 8, size), f32),
        ]

    widths = WIDTHS if sum(WIDTHS) == across else (across,)
    starts = [sum(widths[:i]) for i in range(len(widths))]
    arrived, kept, weights = [], [], []
    for start, wide in zip(starts, widths):
        right_shape = jax.ShapeDtypeStruct((wide, terms, 2 * size, size), bf16)
        if start == 0:
            arguments = (term_shift, wavefn, left_ops, right_ops)
            send, keep, left, right, chosen, lops, psi, rops = call(
                functools.partial(first_others, range(1, ny)),
                [pltpu.with_memory_space_constraint(value, pltpu.HBM) for value in arguments],
                [HBM] * 4,
                result(ny - 1, wide) + [
                    jax.ShapeDtypeStruct((slots, terms * others, 2 * size), bf16),
                    right_shape,
                    jax.ShapeDtypeStruct((terms, 2, 8, size), f32),
                    jax.ShapeDtypeStruct(left_ops.shape, f32),
                    jax.ShapeDtypeStruct(wavefn.shape, f32),
                    jax.ShapeDtypeStruct((terms, max(across - wide, 1), size, size), f32),
                ],
                [
                    pltpu.SMEM(term_shift.shape, jnp.int32),
                    pltpu.VMEM((terms, wide, size, size), f32),
                    *work(others),
                    pltpu.SemaphoreType.DMA((6,)),
                ],
            )
        else:
            send, keep, right = call(
                functools.partial(later_others, start, widths[0]),
                [left, psi, rops, chosen],
                [VMEM] * 4,
                result(ny - 1, wide) + [right_shape],
                work(others),
            )
        arrived.append(lax.ppermute(send, "op", cores))
        kept.append(keep)
        weights.append(right)
    sums, own_kept, own_arrived, moved = [], [], [], []
    for i, (start, wide, right) in enumerate(zip(starts, widths, weights)):
        if start == 0:
            sums.append(add_cores(kept[0], arrived[0]))
            send, keep, own = call(
                first_own,
                [lops, psi, right, chosen, sums[0][0]],
                [VMEM] * 4 + [ANY],
                result(1, wide) + [jax.ShapeDtypeStruct((slots, terms * share, 2 * size), bf16)],
                work(share),
            )
        else:
            send, keep = call(
                functools.partial(later_own, start),
                [own, psi, right, chosen, own_kept[-1]],
                [VMEM] * 4 + [ANY],
                result(1, wide),
                work(share),
            )
        own_kept.append(keep)
        own_arrived.append(lax.ppermute(send, "op", cores))
    for i in range(1, len(widths)):
        sums.append(add_cores(kept[i], arrived[i], own_kept[-1]))
    for i, keep in enumerate(own_kept):
        came = [ahead(value, by) for by, value in enumerate(sums[i], 1)]
        if i == 0:
            total = add_chips(add_chips(keep[0], *came), own_arrived[i][0])
        else:
            total = add_chips(add_chips(keep[0], own_arrived[i][0]), *came)
        moved.append(sectors(total))
    swapped = [lax.ppermute(other_rows(value), "op", cores) for value in moved]
    return settle(moved, swapped)


def solution(mesh):
    placed = (
        P("lsec", "rsec", None, None),
        P("op", "lsec", None, None),
        P("op", "rsec", None, None),
        P("op"),
    )
    return jax.shard_map(
        shards, mesh=mesh, in_specs=placed, out_specs=P("lsec", "rsec", "op", None), check_vma=False
    )
```

```python
import functools

import jax
import jax.numpy as jnp
from jax import lax
from jax.experimental import pallas as pl
from jax.experimental.pallas import tpu as pltpu
from jax.sharding import PartitionSpec as P

WIDTHS = (2, 2)
CORES = 2
ARRANGE_COST = 10 ** 9
ADD_COST = 10 ** 9
LIMIT = 32 * 1024 * 1024
NT = (((1,), (1,)), ((), ()))
PARAMS = pltpu.CompilerParams(vmem_limit_bytes=LIMIT)
HBM = pl.BlockSpec(memory_space=pltpu.HBM)
VMEM = pl.BlockSpec(memory_space=pltpu.VMEM)
ANY = pl.BlockSpec(memory_space=pl.ANY)


def split(value):
    high = value.astype(jnp.bfloat16)
    low = (value - high.astype(jnp.float32)).astype(jnp.bfloat16)
    return high, low


def choose_rows(lops, aheads, left, l):
    terms, _, size, _ = lops.shape
    ny = lax.axis_size("op") // CORES
    mine = lax.axis_index("op") // CORES
    share = size // ny
    many = share * len(aheads)
    for t in range(terms):
        rows = [
            lops[t, l, pl.ds(pl.multiple_of(lax.rem(mine + ahead, ny) * share, share), share), :]
            for ahead in aheads
        ]
        left[l, t * many:(t + 1) * many, :] = jnp.concatenate(split(jnp.concatenate(rows, axis=0)), axis=1)


def products(left, psi, right, chosen, inner, total, send, keep, start, rows_of, rops=None):
    slots, height, twice = left.shape
    size = twice // 2
    wide, terms = right.shape[:2]
    many = height // terms
    chips, blocks, rows, _ = keep.shape
    second = blocks // wide - slots
    core = lax.rem(lax.axis_index("op"), CORES)
    for r in range(wide):
        for l in range(slots):
            if r == 0 and rows_of is not None:
                rows_of(l)
            both = jnp.concatenate(split(psi[l, start + r]), axis=1)
            out = jnp.dot(left[l], jnp.concatenate([both, both], axis=0), preferred_element_type=jnp.float32)
            for t in range(terms):
                block = out[t * many:(t + 1) * many]
                parts = split(block[:, :size] + block[:, size:])
                inner[t, l * many:(l + 1) * many, :] = jnp.concatenate(parts, axis=1)
        for t in range(terms):
            if rops is not None:
                right[r, t] = jnp.concatenate(split(rops[t, r]), axis=0)
            both = right[r, t]
            out = lax.dot_general(
                inner[t], jnp.concatenate([both, both], axis=1), NT, preferred_element_type=jnp.float32
            )
            out = (out[:, :size] + out[:, size:]).reshape(-1, 8, size)
            for way in range(2):
                mine = out * chosen[t, way]
                total[way] = mine if t == 0 else total[way] + mine
        for chip in range(chips):
            for at in range(slots + second):
                way = 0 if at < slots else 1
                l = at if at < slots else at - slots + skipped(slots, second)
                for ref, c in ((keep, core), (send, 1 - core)):
                    line = (l * many + (chip * CORES + c) * rows) // 8
                    block = total[way, pl.ds(line, rows // 8)].reshape(rows, size)
                    if isinstance(ref, (list, tuple)):
                        ref[r][chip, at] = block
                    else:
                        ref[chip, at * wide + r] = block


def skipped(slots, second):
    return 0 if second == slots else 1 - lax.axis_index("lsec")


def first_others(aheads, shift, psi, lops, rops, send, keep, left, right, chosen, lops_all, psi_all, rops_rest, *refs):
    bits, rops_now, inner, total, sems = refs
    terms = lops.shape[0]
    size = psi.shape[-1]
    wide = right.shape[0]
    copies = [
        pltpu.make_async_copy(shift, bits, sems.at[0]),
        pltpu.make_async_copy(lops, lops_all, sems.at[1]),
        pltpu.make_async_copy(psi.at[:, :wide], psi_all.at[:, :wide], sems.at[2]),
        pltpu.make_async_copy(rops.at[:, :wide], rops_now, sems.at[3]),
    ]
    later = []
    if wide < rops.shape[1]:
        later = [
            pltpu.make_async_copy(psi.at[:, wide:], psi_all.at[:, wide:], sems.at[4]),
            pltpu.make_async_copy(rops.at[:, wide:], rops_rest, sems.at[5]),
        ]
    for copy in copies:
        copy.start()
    for copy in copies:
        copy.wait()
    for copy in later:
        copy.start()
    paired = keep.shape[1] < 2 * wide * lops.shape[1]
    for t in range(terms):
        kept = (bits[t] + lax.axis_index("lsec") == 1 if paired else bits[t] == 1).astype(jnp.float32)
        chosen[t, 0] = jnp.full((8, size), kept, jnp.float32)
        chosen[t, 1] = jnp.full((8, size), 1.0 - kept, jnp.float32)
    products(
        left, psi_all, right, chosen, inner, total, send, keep, 0,
        lambda l: choose_rows(lops_all, aheads, left, l), rops_now,
    )
    for copy in later:
        copy.wait()


def first_own(lops, psi, right, chosen, after, send, keep, left, inner, total):
    products(
        left, psi, right, chosen, inner, total, send, keep, 0, lambda l: choose_rows(lops, [0], left, l)
    )


def later_others(start, skip, left, psi, rops, chosen, after, *refs):
    wide = refs[-3].shape[0]
    send, (keep, right, inner, total) = refs[:wide], refs[wide:]
    products(
        left, psi, right, chosen, inner, total, send, keep, start, None, rops.at[:, start - skip:]
    )


def later_own(start, left, psi, right, chosen, after, send, keep, inner, total):
    products(left, psi, right, chosen, inner, total, send, keep, start, None)


def call(kernel, operands, in_specs, out_shape, scratch=(), flops=1):
    return pl.pallas_call(
        kernel,
        in_specs=in_specs,
        out_specs=[VMEM] * len(out_shape),
        out_shape=out_shape,
        scratch_shapes=scratch,
        compiler_params=PARAMS,
        cost_estimate=pl.CostEstimate(flops=flops, bytes_accessed=1024, transcendentals=0),
    )(*operands)


def sums(kernel, shapes, operands, after=None, flops=1):
    reads = len(operands)
    specs = [VMEM] * reads

    def body(*refs):
        kernel(refs[:reads], refs[len(specs):])

    if after is not None:
        operands = [*operands, after]
        specs.append(ANY)
    return call(body, operands, specs, [jax.ShapeDtypeStruct(shape, jnp.float32) for shape in shapes], (), flops)


def arrange(slots, first, second):
    wide, rows, size = first.shape[1:]
    more = second.shape[0]

    def kernel(refs, outs):
        way = 1 - lax.axis_index("lsec") if more < slots else 0
        skip = 1 - skipped(slots, more) if more < slots else 0
        for l in range(slots):
            outs[0][way, l] = refs[0][l]
        for j in range(more):
            outs[0][1 - way, j + skip] = refs[1][j]

    return sums(kernel, [(2, slots, wide, rows, size)], [first, second], None, ARRANGE_COST)[0]


def settle(arranged, first, second):
    slots = first.shape[0]
    rows, size = first.shape[2:]
    more = second.shape[0]
    widths = [value.shape[2] for value in arranged] + [first.shape[1]]
    across = sum(widths)
    n_left, n_right = lax.axis_size("lsec"), lax.axis_size("rsec")

    def kernel(*refs):
        out, every = refs[-2:]
        mine_l, mine_r = lax.axis_index("lsec"), lax.axis_index("rsec")
        first_l, last_l = (mine_l == 0).astype(jnp.int32), (mine_l == n_left - 1).astype(jnp.int32)
        first_r, last_r = (mine_r == 0).astype(jnp.int32), (mine_r == n_right - 1).astype(jnp.int32)
        steps = ((first_l, -last_r), (-last_l, first_r))
        start = 0
        for i, wide in enumerate(widths[:-1]):
            every[:, :, start:start + wide] = refs[i][...]
            start += wide
        way = 1 - mine_l if more < slots else 0
        skip = 1 - skipped(slots, more) if more < slots else 0
        a, b = refs[len(arranged):len(arranged) + 2]
        for l in range(slots):
            every[way, l, start:] = a[l]
        for j in range(more):
            every[1 - way, j + skip, start:] = b[j]
        for l in range(slots):
            for r in range(across):
                block = jnp.zeros((rows, size), jnp.float32)
                for side, (step_l, step_r) in enumerate(steps):
                    from_l, from_r = l - step_l, r - step_r
                    inside = (from_l >= 0) & (from_l < slots) & (from_r >= 0) & (from_r < across)
                    part = every[side, jnp.clip(from_l, 0, slots - 1), jnp.clip(from_r, 0, across - 1)]
                    block = block + jnp.where(inside, part, 0.0)
                out[l, r] = block

    operands = [*arranged, first, second]
    return call(
        kernel, operands, [VMEM] * len(operands),
        [jax.ShapeDtypeStruct((slots, across, rows, size), jnp.float32)],
        [pltpu.VMEM((2, slots, across, rows, size), jnp.float32)],
    )[0]


def shards(wavefn, left_ops, right_ops, term_shift):
    n_op, n_left, n_right = (lax.axis_size(axis) for axis in ("op", "lsec", "rsec"))
    across = wavefn.shape[1]
    terms, slots, size, _ = left_ops.shape
    ny = n_op // CORES
    share = size // ny
    others = (ny - 1) * share
    rows = size // n_op
    second = slots - 1 if n_left == 2 else slots
    f32, bf16 = jnp.float32, jnp.bfloat16

    def permute(value, target):
        def place(o, l, r):
            return (o % n_op * n_left + l % n_left) * n_right + r % n_right

        perm = [
            (place(o, l, r), place(*target(o, l, r)))
            for o in range(n_op) for l in range(n_left) for r in range(n_right)
        ]
        return lax.ppermute(value, ("op", "lsec", "rsec"), perm)

    def swap(value):
        return permute(value, lambda o, l, r: (o ^ 1, l, r))

    def ahead(value, by):
        return permute(value, lambda o, l, r: (o + CORES * by, l, r))

    def sectors(value, way):
        def target(o, l, r):
            up = way == (l if second < slots else 0)
            return (o, l + 1, r - 1) if up else (o, l - 1, r + 1)

        return permute(value, target)

    def blocks(wide):
        return (slots + second) * wide

    def result(chips, wide):
        return jax.ShapeDtypeStruct((chips, blocks(wide), rows, size), f32)

    def work(many):
        return [
            pltpu.VMEM((terms, slots * many, 2 * size), bf16),
            pltpu.VMEM((2, slots * many // 8, 8, size), f32),
        ]

    def add_cores(refs, outs):
        for at, out in enumerate(outs):
            if len(refs) == 2:
                out[...] = refs[0][at] + refs[1][at]
            else:
                wide = len(refs) - 1
                for block in range(out.shape[0]):
                    out[block] = refs[0][at, block] + refs[1 + block % wide][at, block // wide]

    def add_all(refs, outs):
        total = refs[0][...]
        for ref in refs[1:]:
            total = total + ref[...].reshape(total.shape)
        total = total.reshape(-1, rows, size)
        start = 0
        for out in outs:
            count = 1
            for length in out.shape[:-2]:
                count *= length
            out[...] = total[start:start + count].reshape(out.shape)
            start += count

    widths = WIDTHS if sum(WIDTHS) == across else (across,)
    starts = [sum(widths[:i]) for i in range(len(widths))]
    count = len(widths)
    pieces, own_kept, own_arrived, arrived, kept = [], [], [], [], []

    arguments = (term_shift, wavefn, left_ops, right_ops)
    wide = widths[0]
    send, keep, left, right, chosen, lops, psi, rops = call(
        functools.partial(first_others, range(1, ny)),
        [pltpu.with_memory_space_constraint(value, pltpu.HBM) for value in arguments],
        [HBM] * 4,
        [result(ny - 1, wide)] * 2 + [
            jax.ShapeDtypeStruct((slots, terms * others, 2 * size), bf16),
            jax.ShapeDtypeStruct((wide, terms, 2 * size, size), bf16),
            jax.ShapeDtypeStruct((terms, 2, 8, size), f32),
            jax.ShapeDtypeStruct(left_ops.shape, f32),
            jax.ShapeDtypeStruct(wavefn.shape, f32),
            jax.ShapeDtypeStruct((terms, max(across - wide, 1), size, size), f32),
        ],
        [
            pltpu.SMEM(term_shift.shape, jnp.int32),
            pltpu.VMEM((terms, wide, size, size), f32),
            *work(others),
            pltpu.SemaphoreType.DMA((6,)),
        ],
    )
    pieces.append(sums(add_cores, [(blocks(wide), rows, size)] * (ny - 1), [keep, swap(send)]))
    send, keep, own = call(
        first_own,
        [lops, psi, right, chosen, pieces[0][0]],
        [VMEM] * 4 + [ANY],
        [result(1, wide)] * 2 + [jax.ShapeDtypeStruct((slots, terms * share, 2 * size), bf16)],
        work(share),
    )
    own_kept.append(keep)
    own_arrived.append(swap(send))
    for start, wide in zip(starts[1:], widths[1:]):
        *send, keep, right = call(
            functools.partial(later_others, start, widths[0]),
            [left, psi, rops, chosen, own_kept[-1]],
            [VMEM] * 4 + [ANY],
            [result(ny - 1, 1)] * wide + [
                result(ny - 1, wide), jax.ShapeDtypeStruct((wide, terms, 2 * size, size), bf16)
            ],
            work(others),
        )
        arrived.append([swap(value) for value in send])
        kept.append(keep)
        send, keep = call(
            functools.partial(later_own, start),
            [own, psi, right, chosen, keep],
            [VMEM] * 4 + [ANY],
            [result(1, wide)] * 2,
            work(share),
        )
        own_kept.append(keep)
        own_arrived.append(swap(send))
        pieces.append(sums(
            add_cores, [(blocks(wide), rows, size)] * (ny - 1), [kept[-1], *arrived[-1]], own_kept[-1]
        ))
    arranged = []
    for i, (wide, keep, came) in enumerate(zip(widths, own_kept, own_arrived)):
        landed = [ahead(value, by) for by, value in enumerate(pieces[i], 1)]
        before, after = ([keep, *landed], [came]) if i == 0 else ([keep, came], landed)
        total = sums(add_all, [keep.shape], before, pieces[i + 1][0] if i + 1 < count else None)[0]
        value = sums(add_all, [(slots, wide, rows, size), (second, wide, rows, size)], [total, *after], None, ADD_COST if i == 0 else 1)
        value = [sectors(part, way) for way, part in enumerate(value)]
        if i + 1 < count:
            arranged.append(arrange(slots, *value))
    return settle(arranged, *value)


def solution(mesh):
    placed = (
        P("lsec", "rsec", None, None),
        P("op", "lsec", None, None),
        P("op", "rsec", None, None),
        P("op"),
    )
    return jax.shard_map(
        shards, mesh=mesh, in_specs=placed, out_specs=P("lsec", "rsec", "op", None), check_vma=False
    )
```

```python
import functools

import jax
import jax.numpy as jnp
from jax import lax
from jax.experimental import pallas as pl
from jax.experimental.pallas import tpu as pltpu
from jax.sharding import PartitionSpec as P

WIDTHS = (2, 2)
CORES = 2
ARRANGE_COST = 10 ** 9
ADD_COST = 10 ** 9
LIMIT = 32 * 1024 * 1024
NT = (((1,), (1,)), ((), ()))
PARAMS = pltpu.CompilerParams(vmem_limit_bytes=LIMIT)
HBM = pl.BlockSpec(memory_space=pltpu.HBM)
VMEM = pl.BlockSpec(memory_space=pltpu.VMEM)
ANY = pl.BlockSpec(memory_space=pl.ANY)


def split(value):
    high = value.astype(jnp.bfloat16)
    low = (value - high.astype(jnp.float32)).astype(jnp.bfloat16)
    return high, low


def choose_rows(lops, left, l):
    terms, _, many, _ = lops.shape
    for t in range(terms):
        left[l, t * many:(t + 1) * many, :] = jnp.concatenate(split(lops[t, l]), axis=1)


def lines(many, rows, slots, second):
    core = lax.rem(lax.axis_index("op"), CORES)
    return core * (rows // 8), (1 - core) * (rows // 8), skipped(slots, second) * (many // 8)


def products(left, psi, right, chosen, inner, total, send, keep, start, begins, lops=None, rops=None, ready=()):
    slots, height, twice = left.shape
    size = twice // 2
    wide, terms = right.shape[:2]
    many = height // terms
    chips, blocks, rows, _ = keep.shape
    second = blocks // wide - slots
    here, there, skip = begins
    for r in range(wide):
        for l in range(slots):
            if r == 0 and lops is not None:
                choose_rows(lops, left, l)
            both = jnp.concatenate(split(psi[l, start + r]), axis=1)
            out = jnp.dot(left[l], jnp.concatenate([both, both], axis=0), preferred_element_type=jnp.float32)
            for t in range(terms):
                block = out[t * many:(t + 1) * many]
                parts = split(block[:, :size] + block[:, size:])
                inner[t, l * many:(l + 1) * many, :] = jnp.concatenate(parts, axis=1)
        if r == 0:
            for copy in ready:
                copy.wait()
        for t in range(terms):
            if rops is not None:
                right[r, t] = jnp.concatenate(split(rops[t, r]), axis=0)
            both = right[r, t]
            out = lax.dot_general(
                inner[t], jnp.concatenate([both, both], axis=1), NT, preferred_element_type=jnp.float32
            )
            out = (out[:, :size] + out[:, size:]).reshape(-1, 8, size)
            for way in range(2):
                mine = out * chosen[t, way]
                total[way] = mine if t == 0 else total[way] + mine
        for chip in range(chips):
            for at in range(slots + second):
                way = 0 if at < slots else 1
                l = at if at < slots else at - slots
                for ref, begin in ((keep, here), (send, there)):
                    line = begin + (l * many + chip * CORES * rows) // 8 + (skip if way else 0)
                    block = total[way, pl.ds(line, rows // 8)].reshape(rows, size)
                    if isinstance(ref, (list, tuple)):
                        ref[r][chip, at] = block
                    else:
                        ref[chip, at * wide + r] = block


def skipped(slots, second):
    return 0 if second == slots else 1 - lax.axis_index("lsec")


def first_others(shift, psi, lops, rops, send, keep, left, right, chosen, lops_own, psi_all, rops_rest, *refs):
    bits, lops_now, rops_now, inner, total, sems, lsems = refs
    terms, slots, size, _ = lops.shape
    wide = right.shape[0]
    ny = lax.axis_size("op") // CORES
    mine = lax.div(lax.axis_index("op"), CORES)
    share = size // ny

    def rows(ahead, target):
        at = pl.multiple_of(lax.rem(mine + ahead, ny) * share, share)
        return pltpu.make_async_copy(lops.at[:, :, pl.ds(at, share)], target, lsems.at[ahead])

    copies = [rows(ahead, lops_now.at[:, :, pl.ds((ahead - 1) * share, share)]) for ahead in range(1, ny)] + [
        pltpu.make_async_copy(psi.at[:, :wide], psi_all.at[:, :wide], sems.at[0]),
        pltpu.make_async_copy(shift, bits, sems.at[1]),
    ]
    ready = [pltpu.make_async_copy(rops.at[:, :wide], rops_now, sems.at[2])]
    later = [rows(0, lops_own)]
    if wide < rops.shape[1]:
        later += [
            pltpu.make_async_copy(psi.at[:, wide:], psi_all.at[:, wide:], sems.at[3]),
            pltpu.make_async_copy(rops.at[:, wide:], rops_rest, sems.at[4]),
        ]
    for copy in copies + ready:
        copy.start()
    second = keep.shape[1] // wide - slots
    begins = lines(lops_now.shape[2], keep.shape[2], slots, second)
    flip = lax.axis_index("lsec") if second < slots else 0
    for copy in copies:
        copy.wait()
    for copy in later:
        copy.start()
    for t in range(terms):
        kept = jnp.where(flip == 1, 1 - bits[t], bits[t]).astype(jnp.float32)
        chosen[t, 0] = jnp.full((8, size), kept, jnp.float32)
        chosen[t, 1] = jnp.full((8, size), 1.0 - kept, jnp.float32)
    products(
        left, psi_all, right, chosen, inner, total, send, keep, 0, begins, lops_now, rops_now, ready
    )
    for copy in later:
        copy.wait()


def find(left, keep, right):
    slots, height, _ = left.shape
    wide, terms = right.shape[:2]
    return lines(height // terms, keep.shape[2], slots, keep.shape[1] // wide - slots)


def first_own(lops, psi, right, chosen, send, keep, left, inner, total):
    products(left, psi, right, chosen, inner, total, send, keep, 0, find(left, keep, right), lops)


def later_others(start, skip, left, psi, rops, chosen, after, *refs):
    wide = refs[-3].shape[0]
    send, (keep, right, inner, total) = refs[:wide], refs[wide:]
    products(
        left, psi, right, chosen, inner, total, send, keep, start, find(left, keep, right),
        rops=rops.at[:, start - skip:],
    )


def later_own(start, left, psi, right, chosen, after, send, keep, inner, total):
    products(left, psi, right, chosen, inner, total, send, keep, start, find(left, keep, right))


def call(kernel, operands, in_specs, out_shape, scratch=(), flops=1):
    return pl.pallas_call(
        kernel,
        in_specs=in_specs,
        out_specs=[VMEM] * len(out_shape),
        out_shape=out_shape,
        scratch_shapes=scratch,
        compiler_params=PARAMS,
        cost_estimate=pl.CostEstimate(flops=flops, bytes_accessed=1024, transcendentals=0),
    )(*operands)


def sums(kernel, shapes, operands, after=None, flops=1):
    reads = len(operands)
    specs = [VMEM] * reads

    def body(*refs):
        kernel(refs[:reads], refs[len(specs):])

    if after is not None:
        operands = [*operands, after]
        specs.append(ANY)
    return call(body, operands, specs, [jax.ShapeDtypeStruct(shape, jnp.float32) for shape in shapes], (), flops)


def arrange(slots, first, second):
    wide, rows, size = first.shape[1:]
    more = second.shape[0]

    def kernel(refs, outs):
        way = 1 - lax.axis_index("lsec") if more < slots else 0
        skip = 1 - skipped(slots, more) if more < slots else 0
        for l in range(slots):
            outs[0][way, l] = refs[0][l]
        for j in range(more):
            outs[0][1 - way, j + skip] = refs[1][j]

    return sums(kernel, [(2, slots, wide, rows, size)], [first, second], None, ARRANGE_COST)[0]


def settle(arranged, first, second):
    slots = first.shape[0]
    rows, size = first.shape[2:]
    more = second.shape[0]
    widths = [value.shape[2] for value in arranged] + [first.shape[1]]
    across = sum(widths)
    n_left, n_right = lax.axis_size("lsec"), lax.axis_size("rsec")

    def kernel(*refs):
        out, every = refs[-2:]
        mine_l, mine_r = lax.axis_index("lsec"), lax.axis_index("rsec")
        first_l, last_l = (mine_l == 0).astype(jnp.int32), (mine_l == n_left - 1).astype(jnp.int32)
        first_r, last_r = (mine_r == 0).astype(jnp.int32), (mine_r == n_right - 1).astype(jnp.int32)
        steps = ((first_l, -last_r), (-last_l, first_r))
        start = 0
        for i, wide in enumerate(widths[:-1]):
            every[:, :, start:start + wide] = refs[i][...]
            start += wide
        way = 1 - mine_l if more < slots else 0
        skip = 1 - skipped(slots, more) if more < slots else 0
        a, b = refs[len(arranged):len(arranged) + 2]
        for l in range(slots):
            every[way, l, start:] = a[l]
        for j in range(more):
            every[1 - way, j + skip, start:] = b[j]
        for l in range(slots):
            for r in range(across):
                block = jnp.zeros((rows, size), jnp.float32)
                for side, (step_l, step_r) in enumerate(steps):
                    from_l, from_r = l - step_l, r - step_r
                    inside = (from_l >= 0) & (from_l < slots) & (from_r >= 0) & (from_r < across)
                    part = every[side, jnp.clip(from_l, 0, slots - 1), jnp.clip(from_r, 0, across - 1)]
                    block = block + jnp.where(inside, part, 0.0)
                out[l, r] = block

    operands = [*arranged, first, second]
    return call(
        kernel, operands, [VMEM] * len(operands),
        [jax.ShapeDtypeStruct((slots, across, rows, size), jnp.float32)],
        [pltpu.VMEM((2, slots, across, rows, size), jnp.float32)],
    )[0]


def shards(wavefn, left_ops, right_ops, term_shift):
    n_op, n_left, n_right = (lax.axis_size(axis) for axis in ("op", "lsec", "rsec"))
    across = wavefn.shape[1]
    terms, slots, size, _ = left_ops.shape
    ny = n_op // CORES
    share = size // ny
    others = (ny - 1) * share
    rows = size // n_op
    second = slots - 1 if n_left == 2 else slots
    f32, bf16 = jnp.float32, jnp.bfloat16

    def permute(value, target):
        def place(o, l, r):
            return (o % n_op * n_left + l % n_left) * n_right + r % n_right

        perm = [
            (place(o, l, r), place(*target(o, l, r)))
            for o in range(n_op) for l in range(n_left) for r in range(n_right)
        ]
        return lax.ppermute(value, ("op", "lsec", "rsec"), perm)

    def swap(value):
        return permute(value, lambda o, l, r: (o ^ 1, l, r))

    def ahead(value, by):
        return permute(value, lambda o, l, r: (o + CORES * by, l, r))

    def sectors(value, way):
        def target(o, l, r):
            up = way == (l if second < slots else 0)
            return (o, l + 1, r - 1) if up else (o, l - 1, r + 1)

        return permute(value, target)

    def blocks(wide):
        return (slots + second) * wide

    def result(chips, wide):
        return jax.ShapeDtypeStruct((chips, blocks(wide), rows, size), f32)

    def work(many):
        return [
            pltpu.VMEM((terms, slots * many, 2 * size), bf16),
            pltpu.VMEM((2, slots * many // 8, 8, size), f32),
        ]

    def add_cores(refs, outs):
        for at, out in enumerate(outs):
            if len(refs) == 2:
                out[...] = refs[0][at] + refs[1][at]
            else:
                wide = len(refs) - 1
                for block in range(out.shape[0]):
                    out[block] = refs[0][at, block] + refs[1 + block % wide][at, block // wide]

    def add_all(refs, outs):
        total = refs[0][...]
        for ref in refs[1:]:
            total = total + ref[...].reshape(total.shape)
        total = total.reshape(-1, rows, size)
        start = 0
        for out in outs:
            count = 1
            for length in out.shape[:-2]:
                count *= length
            out[...] = total[start:start + count].reshape(out.shape)
            start += count

    widths = WIDTHS if sum(WIDTHS) == across else (across,)
    starts = [sum(widths[:i]) for i in range(len(widths))]
    count = len(widths)
    pieces, own_kept, own_arrived, arrived, kept = [], [], [], [], []

    arguments = (term_shift, wavefn, left_ops, right_ops)
    wide = widths[0]
    send, keep, left, right, chosen, lops, psi, rops = call(
        first_others,
        [pltpu.with_memory_space_constraint(value, pltpu.HBM) for value in arguments],
        [HBM] * 4,
        [result(ny - 1, wide)] * 2 + [
            jax.ShapeDtypeStruct((slots, terms * others, 2 * size), bf16),
            jax.ShapeDtypeStruct((wide, terms, 2 * size, size), bf16),
            jax.ShapeDtypeStruct((terms, 2, 8, size), f32),
            jax.ShapeDtypeStruct((terms, slots, share, size), f32),
            jax.ShapeDtypeStruct(wavefn.shape, f32),
            jax.ShapeDtypeStruct((terms, max(across - wide, 1), size, size), f32),
        ],
        [
            pltpu.SMEM(term_shift.shape, jnp.int32),
            pltpu.VMEM((terms, slots, others, size), f32),
            pltpu.VMEM((terms, wide, size, size), f32),
            *work(others),
            pltpu.SemaphoreType.DMA((5,)),
            pltpu.SemaphoreType.DMA((ny,)),
        ],
    )
    kept.append(keep)
    arrived.append(swap(send))
    send, keep, own = call(
        first_own,
        [lops, psi, right, chosen],
        [VMEM] * 4,
        [result(1, wide)] * 2 + [jax.ShapeDtypeStruct((slots, terms * share, 2 * size), bf16)],
        work(share),
    )
    own_kept.append(keep)
    own_arrived.append(swap(send))
    pieces.append(sums(add_cores, [(blocks(wide), rows, size)] * (ny - 1), [kept[0], arrived[0]], keep))
    for start, wide in zip(starts[1:], widths[1:]):
        *send, keep, right = call(
            functools.partial(later_others, start, widths[0]),
            [left, psi, rops, chosen, pieces[-1][0]],
            [VMEM] * 4 + [ANY],
            [result(ny - 1, 1)] * wide + [
                result(ny - 1, wide), jax.ShapeDtypeStruct((wide, terms, 2 * size, size), bf16)
            ],
            work(others),
        )
        arrived.append([swap(value) for value in send])
        kept.append(keep)
        send, keep = call(
            functools.partial(later_own, start),
            [own, psi, right, chosen, keep],
            [VMEM] * 4 + [ANY],
            [result(1, wide)] * 2,
            work(share),
        )
        own_kept.append(keep)
        own_arrived.append(swap(send))
        pieces.append(sums(
            add_cores, [(blocks(wide), rows, size)] * (ny - 1), [kept[-1], *arrived[-1]], own_kept[-1]
        ))
    arranged = []
    for i, (wide, keep, came) in enumerate(zip(widths, own_kept, own_arrived)):
        landed = [ahead(value, by) for by, value in enumerate(pieces[i], 1)]
        total = sums(add_all, [keep.shape], [keep, came], pieces[i + 1][0] if i + 1 < count else None)[0]
        value = sums(add_all, [(slots, wide, rows, size), (second, wide, rows, size)], [total, *landed], None, ADD_COST if i == 0 else 1)
        value = [sectors(part, way) for way, part in enumerate(value)]
        if i + 1 < count:
            arranged.append(arrange(slots, *value))
    return settle(arranged, *value)


def solution(mesh):
    placed = (
        P("lsec", "rsec", None, None),
        P("op", "lsec", None, None),
        P("op", "rsec", None, None),
        P("op"),
    )
    return jax.shard_map(
        shards, mesh=mesh, in_specs=placed, out_specs=P("lsec", "rsec", "op", None), check_vma=False
    )
```

```python
import functools

import jax
import jax.numpy as jnp
from jax import lax
from jax.experimental import pallas as pl
from jax.experimental.pallas import tpu as pltpu
from jax.sharding import PartitionSpec as P

WIDTHS = (2, 2)
CORES = 2
ARRANGE_COST = 10 ** 9
ADD_COST = 10 ** 9
LIMIT = 32 * 1024 * 1024
NT = (((1,), (1,)), ((), ()))
PARAMS = pltpu.CompilerParams(vmem_limit_bytes=LIMIT)
HBM = pl.BlockSpec(memory_space=pltpu.HBM)
VMEM = pl.BlockSpec(memory_space=pltpu.VMEM)
ANY = pl.BlockSpec(memory_space=pl.ANY)


def split(value):
    high = value.astype(jnp.bfloat16)
    low = (value - high.astype(jnp.float32)).astype(jnp.bfloat16)
    return high, low


def choose_rows(lops, left, l):
    terms, _, many, _ = lops.shape
    for t in range(terms):
        left[l, t * many:(t + 1) * many, :] = jnp.concatenate(split(lops[t, l]), axis=1)


def lines(many, rows, slots, second):
    core = lax.rem(lax.axis_index("op"), CORES)
    return core * (rows // 8), (1 - core) * (rows // 8), skipped(slots, second) * (many // 8)


def products(left, psi, right, chosen, inner, total, send, keep, start, begins, lops=None, rops=None, waits={}, classes=None):
    slots, height, twice = left.shape
    size = twice // 2
    wide, terms = right.shape[:2]
    many = height // terms
    chips, blocks, rows, _ = keep.shape
    second = blocks // wide - slots
    here, there, skip = begins
    for r in range(wide):
        for l in range(slots):
            if r == 0:
                for copy in waits.get(l, ()):
                    copy.wait()
                if lops is not None:
                    choose_rows(lops, left, l)
            both = jnp.concatenate(split(psi[l, start + r]), axis=1)
            out = jnp.dot(left[l], jnp.concatenate([both, both], axis=0), preferred_element_type=jnp.float32)
            for t in range(terms):
                block = out[t * many:(t + 1) * many]
                parts = split(block[:, :size] + block[:, size:])
                inner[t, l * many:(l + 1) * many, :] = jnp.concatenate(parts, axis=1)
        if r == 0:
            for copy in waits.get(slots, ()):
                copy.wait()
            if classes is not None:
                classes()
        for t in range(terms):
            if rops is not None:
                right[r, t] = jnp.concatenate(split(rops[t, r]), axis=0)
            both = right[r, t]
            out = lax.dot_general(
                inner[t], jnp.concatenate([both, both], axis=1), NT, preferred_element_type=jnp.float32
            )
            out = (out[:, :size] + out[:, size:]).reshape(-1, 8, size)
            for way in range(2):
                mine = out * chosen[t, way]
                total[way] = mine if t == 0 else total[way] + mine
        for chip in range(chips):
            for at in range(slots + second):
                way = 0 if at < slots else 1
                l = at if at < slots else at - slots
                for ref, begin in ((keep, here), (send, there)):
                    line = begin + (l * many + chip * CORES * rows) // 8 + (skip if way else 0)
                    block = total[way, pl.ds(line, rows // 8)].reshape(rows, size)
                    if isinstance(ref, (list, tuple)):
                        ref[r][chip, at] = block
                    else:
                        ref[chip, at * wide + r] = block


def skipped(slots, second):
    return 0 if second == slots else 1 - lax.axis_index("lsec")


def first_others(shift, psi, lops, rops, send, keep, left, right, chosen, lops_own, psi_all, rops_rest, *refs):
    bits, lops_now, rops_now, inner, total, sems, lsems = refs
    terms, slots, size, _ = lops.shape
    wide = right.shape[0]
    ny = lax.axis_size("op") // CORES
    mine = lax.div(lax.axis_index("op"), CORES)
    share = size // ny

    def rows(l, ahead, target):
        at = pl.multiple_of(lax.rem(mine + ahead, ny) * share, share)
        return pltpu.make_async_copy(lops.at[:, l, pl.ds(at, share)], target, lsems.at[ahead, l.start])

    waits = {}
    half = slots // 2
    for l in (slice(0, half), slice(half, slots)):
        waits[l.start] = [
            rows(l, ahead, lops_now.at[:, l, pl.ds((ahead - 1) * share, share)]) for ahead in range(1, ny)
        ] + [pltpu.make_async_copy(psi.at[l, :wide], psi_all.at[l, :wide], sems.at[l.start])]
    waits[slots] = [
        pltpu.make_async_copy(rops.at[:, :wide], rops_now, sems.at[slots]),
        pltpu.make_async_copy(shift, bits, sems.at[slots + 1]),
    ]
    later = [rows(slice(0, slots), 0, lops_own)]
    if wide < rops.shape[1]:
        later += [
            pltpu.make_async_copy(psi.at[:, wide:], psi_all.at[:, wide:], sems.at[slots + 2]),
            pltpu.make_async_copy(rops.at[:, wide:], rops_rest, sems.at[slots + 3]),
        ]
    for copy in sum(waits.values(), []):
        copy.start()
    second = keep.shape[1] // wide - slots
    begins = lines(lops_now.shape[2], keep.shape[2], slots, second)
    flip = lax.axis_index("lsec") if second < slots else 0

    def classes():
        for copy in later:
            copy.start()
        for t in range(terms):
            kept = jnp.where(flip == 1, 1 - bits[t], bits[t]).astype(jnp.float32)
            chosen[t, 0] = jnp.full((8, size), kept, jnp.float32)
            chosen[t, 1] = jnp.full((8, size), 1.0 - kept, jnp.float32)

    products(
        left, psi_all, right, chosen, inner, total, send, keep, 0, begins, lops_now, rops_now, waits, classes
    )
    for copy in later:
        copy.wait()


def find(left, keep, right):
    slots, height, _ = left.shape
    wide, terms = right.shape[:2]
    return lines(height // terms, keep.shape[2], slots, keep.shape[1] // wide - slots)


def first_own(lops, psi, right, chosen, after, send, keep, left, inner, total):
    products(left, psi, right, chosen, inner, total, send, keep, 0, find(left, keep, right), lops)


def later_others(start, skip, left, psi, rops, chosen, after, *refs):
    wide = refs[-3].shape[0]
    send, (keep, right, inner, total) = refs[:wide], refs[wide:]
    products(
        left, psi, right, chosen, inner, total, send, keep, start, find(left, keep, right),
        rops=rops.at[:, start - skip:],
    )


def later_own(start, left, psi, right, chosen, after, send, keep, inner, total):
    products(left, psi, right, chosen, inner, total, send, keep, start, find(left, keep, right))


def call(kernel, operands, in_specs, out_shape, scratch=(), flops=1):
    return pl.pallas_call(
        kernel,
        in_specs=in_specs,
        out_specs=[VMEM] * len(out_shape),
        out_shape=out_shape,
        scratch_shapes=scratch,
        compiler_params=PARAMS,
        cost_estimate=pl.CostEstimate(flops=flops, bytes_accessed=1024, transcendentals=0),
    )(*operands)


def sums(kernel, shapes, operands, after=None, flops=1):
    reads = len(operands)
    specs = [VMEM] * reads

    def body(*refs):
        kernel(refs[:reads], refs[len(specs):])

    if after is not None:
        operands = [*operands, after]
        specs.append(ANY)
    return call(body, operands, specs, [jax.ShapeDtypeStruct(shape, jnp.float32) for shape in shapes], (), flops)


def arrange(slots, first, second):
    wide, rows, size = first.shape[1:]
    more = second.shape[0]

    def kernel(refs, outs):
        way = 1 - lax.axis_index("lsec") if more < slots else 0
        skip = 1 - skipped(slots, more) if more < slots else 0
        for l in range(slots):
            outs[0][way, l] = refs[0][l]
        for j in range(more):
            outs[0][1 - way, j + skip] = refs[1][j]

    return sums(kernel, [(2, slots, wide, rows, size)], [first, second], None, ARRANGE_COST)[0]


def settle(arranged, first, second):
    slots = first.shape[0]
    rows, size = first.shape[2:]
    more = second.shape[0]
    widths = [value.shape[2] for value in arranged] + [first.shape[1]]
    across = sum(widths)
    n_left, n_right = lax.axis_size("lsec"), lax.axis_size("rsec")

    def kernel(*refs):
        out, every, ready, sems = refs[-4:]
        mine_l, mine_r = lax.axis_index("lsec"), lax.axis_index("rsec")
        first_l, last_l = (mine_l == 0).astype(jnp.int32), (mine_l == n_left - 1).astype(jnp.int32)
        first_r, last_r = (mine_r == 0).astype(jnp.int32), (mine_r == n_right - 1).astype(jnp.int32)
        steps = ((first_l, -last_r), (-last_l, first_r))
        start = 0
        for i, wide in enumerate(widths[:-1]):
            every[:, :, start:start + wide] = refs[i][...]
            start += wide
        way = 1 - mine_l if more < slots else 0
        skip = 1 - skipped(slots, more) if more < slots else 0
        a, b = refs[len(arranged):len(arranged) + 2]
        for l in range(slots):
            every[way, l, start:] = a[l]
        for j in range(more):
            every[1 - way, j + skip, start:] = b[j]
        copies = []
        for l in range(slots):
            for r in range(across):
                block = jnp.zeros((rows, size), jnp.float32)
                for side, (step_l, step_r) in enumerate(steps):
                    from_l, from_r = l - step_l, r - step_r
                    inside = (from_l >= 0) & (from_l < slots) & (from_r >= 0) & (from_r < across)
                    part = every[side, jnp.clip(from_l, 0, slots - 1), jnp.clip(from_r, 0, across - 1)]
                    block = block + jnp.where(inside, part, 0.0)
                ready[l, r] = block
            copies.append(pltpu.make_async_copy(ready.at[l], out.at[l], sems.at[l]))
            copies[-1].start()
        for copy in copies:
            copy.wait()

    operands = [*arranged, first, second]
    shape = (slots, across, rows, size)
    return pl.pallas_call(
        kernel,
        in_specs=[VMEM] * len(operands),
        out_specs=HBM,
        out_shape=jax.ShapeDtypeStruct(shape, jnp.float32),
        scratch_shapes=[
            pltpu.VMEM((2, *shape), jnp.float32),
            pltpu.VMEM(shape, jnp.float32),
            pltpu.SemaphoreType.DMA((slots,)),
        ],
        compiler_params=PARAMS,
    )(*operands)


def shards(wavefn, left_ops, right_ops, term_shift):
    n_op, n_left, n_right = (lax.axis_size(axis) for axis in ("op", "lsec", "rsec"))
    across = wavefn.shape[1]
    terms, slots, size, _ = left_ops.shape
    ny = n_op // CORES
    share = size // ny
    others = (ny - 1) * share
    rows = size // n_op
    second = slots - 1 if n_left == 2 else slots
    f32, bf16 = jnp.float32, jnp.bfloat16

    def permute(value, target):
        def place(o, l, r):
            return (o % n_op * n_left + l % n_left) * n_right + r % n_right

        perm = [
            (place(o, l, r), place(*target(o, l, r)))
            for o in range(n_op) for l in range(n_left) for r in range(n_right)
        ]
        return lax.ppermute(value, ("op", "lsec", "rsec"), perm)

    def swap(value):
        return permute(value, lambda o, l, r: (o ^ 1, l, r))

    def ahead(value, by):
        return permute(value, lambda o, l, r: (o + CORES * by, l, r))

    def sectors(value, way):
        def target(o, l, r):
            up = way == (l if second < slots else 0)
            return (o, l + 1, r - 1) if up else (o, l - 1, r + 1)

        return permute(value, target)

    def blocks(wide):
        return (slots + second) * wide

    def result(chips, wide):
        return jax.ShapeDtypeStruct((chips, blocks(wide), rows, size), f32)

    def work(many):
        return [
            pltpu.VMEM((terms, slots * many, 2 * size), bf16),
            pltpu.VMEM((2, slots * many // 8, 8, size), f32),
        ]

    def add_cores(refs, outs):
        for at, out in enumerate(outs):
            if len(refs) == 2:
                out[...] = refs[0][at] + refs[1][at]
            else:
                wide = len(refs) - 1
                for block in range(out.shape[0]):
                    out[block] = refs[0][at, block] + refs[1 + block % wide][at, block // wide]

    def add_all(refs, outs):
        total = refs[0][...]
        for ref in refs[1:]:
            total = total + ref[...].reshape(total.shape)
        total = total.reshape(-1, rows, size)
        start = 0
        for out in outs:
            count = 1
            for length in out.shape[:-2]:
                count *= length
            out[...] = total[start:start + count].reshape(out.shape)
            start += count

    widths = WIDTHS if sum(WIDTHS) == across else (across,)
    starts = [sum(widths[:i]) for i in range(len(widths))]
    count = len(widths)
    pieces, own_kept, own_arrived, arrived, kept = [], [], [], [], []

    arguments = (term_shift, wavefn, left_ops, right_ops)
    wide = widths[0]
    send, keep, left, right, chosen, lops, psi, rops = call(
        first_others,
        [pltpu.with_memory_space_constraint(value, pltpu.HBM) for value in arguments],
        [HBM] * 4,
        [result(ny - 1, wide)] * 2 + [
            jax.ShapeDtypeStruct((slots, terms * others, 2 * size), bf16),
            jax.ShapeDtypeStruct((wide, terms, 2 * size, size), bf16),
            jax.ShapeDtypeStruct((terms, 2, 8, size), f32),
            jax.ShapeDtypeStruct((terms, slots, share, size), f32),
            jax.ShapeDtypeStruct(wavefn.shape, f32),
            jax.ShapeDtypeStruct((terms, max(across - wide, 1), size, size), f32),
        ],
        [
            pltpu.SMEM(term_shift.shape, jnp.int32),
            pltpu.VMEM((terms, slots, others, size), f32),
            pltpu.VMEM((terms, wide, size, size), f32),
            *work(others),
            pltpu.SemaphoreType.DMA((slots + 4,)),
            pltpu.SemaphoreType.DMA((ny, slots)),
        ],
    )
    kept.append(keep)
    arrived.append(swap(send))
    pieces.append(sums(add_cores, [(blocks(wide), rows, size)] * (ny - 1), [kept[0], arrived[0]]))
    send, keep, own = call(
        first_own,
        [lops, psi, right, chosen, pieces[0][0]],
        [VMEM] * 4 + [ANY],
        [result(1, wide)] * 2 + [jax.ShapeDtypeStruct((slots, terms * share, 2 * size), bf16)],
        work(share),
    )
    own_kept.append(keep)
    own_arrived.append(swap(send))
    for start, wide in zip(starts[1:], widths[1:]):
        *send, keep, right = call(
            functools.partial(later_others, start, widths[0]),
            [left, psi, rops, chosen, own_kept[-1]],
            [VMEM] * 4 + [ANY],
            [result(ny - 1, 1)] * wide + [
                result(ny - 1, wide), jax.ShapeDtypeStruct((wide, terms, 2 * size, size), bf16)
            ],
            work(others),
        )
        arrived.append([swap(value) for value in send])
        kept.append(keep)
        send, keep = call(
            functools.partial(later_own, start),
            [own, psi, right, chosen, keep],
            [VMEM] * 4 + [ANY],
            [result(1, wide)] * 2,
            work(share),
        )
        own_kept.append(keep)
        own_arrived.append(swap(send))
        pieces.append(sums(
            add_cores, [(blocks(wide), rows, size)] * (ny - 1), [kept[-1], *arrived[-1]], own_kept[-1]
        ))
    arranged = []
    for i, (wide, keep, came) in enumerate(zip(widths, own_kept, own_arrived)):
        landed = [ahead(value, by) for by, value in enumerate(pieces[i], 1)]
        before, after = ([keep, *landed], [came]) if i == 0 else ([keep, came], landed)
        total = sums(add_all, [keep.shape], before, pieces[i + 1][0] if i + 1 < count else None)[0]
        value = sums(add_all, [(slots, wide, rows, size), (second, wide, rows, size)], [total, *after], None, ADD_COST if i == 0 else 1)
        value = [sectors(part, way) for way, part in enumerate(value)]
        if i + 1 < count:
            arranged.append(arrange(slots, *value))
    return settle(arranged, *value)


def solution(mesh):
    placed = (
        P("lsec", "rsec", None, None),
        P("op", "lsec", None, None),
        P("op", "rsec", None, None),
        P("op"),
    )
    return jax.shard_map(
        shards, mesh=mesh, in_specs=placed, out_specs=P("lsec", "rsec", "op", None), check_vma=False
    )
```

```python
import functools

import jax
import jax.numpy as jnp
from jax import lax
from jax.experimental import pallas as pl
from jax.experimental.pallas import tpu as pltpu
from jax.sharding import PartitionSpec as P

CORES = 2
ARRANGE_COST = 10 ** 9
LAST_COST = 10 ** 9
COSTS = ((1, 10 ** 10), (1, 1))
LIMIT = 32 * 1024 * 1024
NT = (((1,), (1,)), ((), ()))
PARAMS = pltpu.CompilerParams(vmem_limit_bytes=LIMIT)
HBM = pl.BlockSpec(memory_space=pltpu.HBM)
VMEM = pl.BlockSpec(memory_space=pltpu.VMEM)
ANY = pl.BlockSpec(memory_space=pl.ANY)


def split(value):
    high = value.astype(jnp.bfloat16)
    low = (value - high.astype(jnp.float32)).astype(jnp.bfloat16)
    return high, low


def choose_rows(lops, left, l):
    terms, _, many, _ = lops.shape
    for t in range(terms):
        left[l, t * many:(t + 1) * many, :] = jnp.concatenate(split(lops[t, l]), axis=1)


def lines(many, rows, slots, second):
    core = lax.rem(lax.axis_index("op"), CORES)
    return core * (rows // 8), (1 - core) * (rows // 8), skipped(slots, second) * (many // 8)


def products(left, psi, right, chosen, inner, total, send, keep, start, begins, lops=None, rops=None, ready=()):
    slots, height, twice = left.shape
    size = twice // 2
    wide, terms = right.shape[:2]
    many = height // terms
    chips, blocks, rows, _ = keep.shape
    second = blocks // wide - slots
    here, there, skip = begins
    for r in range(wide):
        for l in range(slots):
            if r == 0 and lops is not None:
                choose_rows(lops, left, l)
            both = jnp.concatenate(split(psi[l, start + r]), axis=1)
            out = jnp.dot(left[l], jnp.concatenate([both, both], axis=0), preferred_element_type=jnp.float32)
            for t in range(terms):
                block = out[t * many:(t + 1) * many]
                parts = split(block[:, :size] + block[:, size:])
                inner[t, l * many:(l + 1) * many, :] = jnp.concatenate(parts, axis=1)
        if r == 0:
            for copy in ready:
                copy.wait()
        for t in range(terms):
            if rops is not None:
                right[r, t] = jnp.concatenate(split(rops[t, r]), axis=0)
            both = right[r, t]
            out = lax.dot_general(
                inner[t], jnp.concatenate([both, both], axis=1), NT, preferred_element_type=jnp.float32
            )
            out = (out[:, :size] + out[:, size:]).reshape(-1, 8, size)
            for way in range(2):
                mine = out * chosen[t, way]
                total[way] = mine if t == 0 else total[way] + mine
        for chip in range(chips):
            for at in range(slots + second):
                way = 0 if at < slots else 1
                l = at if at < slots else at - slots
                for ref, begin in ((keep, here), (send, there)):
                    line = begin + (l * many + chip * CORES * rows) // 8 + (skip if way else 0)
                    block = total[way, pl.ds(line, rows // 8)].reshape(rows, size)
                    if isinstance(ref, (list, tuple)):
                        ref[2 * r + way][chip, at - way * slots] = block
                    else:
                        ref[chip, at * wide + r] = block


def skipped(slots, second):
    return 0 if second == slots else 1 - lax.axis_index("lsec")


def first_others(shift, psi, lops, rops, send, keep, left, right, chosen, lops_own, psi_all, rops_rest, *refs):
    bits, lops_now, rops_now, inner, total, sems, lsems = refs
    terms, slots, size, _ = lops.shape
    wide = right.shape[0]
    ny = lax.axis_size("op") // CORES
    mine = lax.div(lax.axis_index("op"), CORES)
    share = size // ny

    def rows(ahead, target):
        at = pl.multiple_of(lax.rem(mine + ahead, ny) * share, share)
        return pltpu.make_async_copy(lops.at[:, :, pl.ds(at, share)], target, lsems.at[ahead])

    copies = [rows(ahead, lops_now.at[:, :, pl.ds((ahead - 1) * share, share)]) for ahead in range(1, ny)] + [
        pltpu.make_async_copy(psi.at[:, :wide], psi_all.at[:, :wide], sems.at[0]),
        pltpu.make_async_copy(shift, bits, sems.at[1]),
    ]
    ready = [pltpu.make_async_copy(rops.at[:, :wide], rops_now, sems.at[2])]
    later = [rows(0, lops_own)]
    if wide < rops.shape[1]:
        later += [
            pltpu.make_async_copy(psi.at[:, wide:], psi_all.at[:, wide:], sems.at[3]),
            pltpu.make_async_copy(rops.at[:, wide:], rops_rest, sems.at[4]),
        ]
    for copy in copies + ready:
        copy.start()
    second = keep.shape[1] // wide - slots
    begins = lines(lops_now.shape[2], keep.shape[2], slots, second)
    flip = lax.axis_index("lsec") if second < slots else 0
    for copy in copies:
        copy.wait()
    for copy in later:
        copy.start()
    for t in range(terms):
        kept = jnp.where(flip == 1, 1 - bits[t], bits[t]).astype(jnp.float32)
        chosen[t, 0] = jnp.full((8, size), kept, jnp.float32)
        chosen[t, 1] = jnp.full((8, size), 1.0 - kept, jnp.float32)
    products(
        left, psi_all, right, chosen, inner, total, send, keep, 0, begins, lops_now, rops_now, ready
    )
    for copy in later:
        copy.wait()


def find(left, keep, right):
    slots, height, _ = left.shape
    wide, terms = right.shape[:2]
    return lines(height // terms, keep.shape[2], slots, keep.shape[1] // wide - slots)


def first_own(lops, psi, right, chosen, send, keep, left, inner, total):
    products(left, psi, right, chosen, inner, total, send, keep, 0, find(left, keep, right), lops)


def later_others(start, skip, left, psi, rops, chosen, after, *refs):
    *send, keep, right, inner, total = refs
    products(
        left, psi, right, chosen, inner, total, send, keep, start, find(left, keep, right),
        rops=rops.at[:, start - skip:],
    )


def later_own(start, left, psi, right, chosen, after, send, keep, inner, total):
    products(left, psi, right, chosen, inner, total, send, keep, start, find(left, keep, right))


def call(kernel, operands, in_specs, out_shape, scratch=(), flops=1):
    return pl.pallas_call(
        kernel,
        in_specs=in_specs,
        out_specs=[VMEM] * len(out_shape),
        out_shape=out_shape,
        scratch_shapes=scratch,
        compiler_params=PARAMS,
        cost_estimate=pl.CostEstimate(flops=flops, bytes_accessed=1024, transcendentals=0),
    )(*operands)


def sums(kernel, shapes, operands, after=None, flops=1):
    reads = len(operands)
    specs = [VMEM] * reads

    def body(*refs):
        kernel(refs[:reads], refs[len(specs):])

    if after is not None:
        operands = [*operands, after]
        specs.append(ANY)
    return call(body, operands, specs, [jax.ShapeDtypeStruct(shape, jnp.float32) for shape in shapes], (), flops)


def arrange(slots, first, second):
    wide, rows, size = first.shape[1:]
    more = second.shape[0]

    def kernel(refs, outs):
        way = 1 - lax.axis_index("lsec") if more < slots else 0
        skip = 1 - skipped(slots, more) if more < slots else 0
        for l in range(slots):
            outs[0][way, l] = refs[0][l]
        for j in range(more):
            outs[0][1 - way, j + skip] = refs[1][j]

    return sums(kernel, [(2, slots, wide, rows, size)], [first, second], None, ARRANGE_COST)[0]


def settle(arranged, first, second):
    slots = first.shape[0]
    rows, size = first.shape[2:]
    more = second.shape[0]
    widths = [value.shape[2] for value in arranged] + [first.shape[1]]
    across = sum(widths)
    n_left, n_right = lax.axis_size("lsec"), lax.axis_size("rsec")

    def kernel(*refs):
        out, every = refs[-2:]
        mine_l, mine_r = lax.axis_index("lsec"), lax.axis_index("rsec")
        first_l, last_l = (mine_l == 0).astype(jnp.int32), (mine_l == n_left - 1).astype(jnp.int32)
        first_r, last_r = (mine_r == 0).astype(jnp.int32), (mine_r == n_right - 1).astype(jnp.int32)
        steps = ((first_l, -last_r), (-last_l, first_r))
        start = 0
        for i, wide in enumerate(widths[:-1]):
            every[:, :, start:start + wide] = refs[i][...]
            start += wide
        way = 1 - mine_l if more < slots else 0
        skip = 1 - skipped(slots, more) if more < slots else 0
        a, b = refs[len(arranged):len(arranged) + 2]
        for l in range(slots):
            every[way, l, start:] = a[l]
        for j in range(more):
            every[1 - way, j + skip, start:] = b[j]
        for l in range(slots):
            for r in range(across):
                block = jnp.zeros((rows, size), jnp.float32)
                for side, (step_l, step_r) in enumerate(steps):
                    from_l, from_r = l - step_l, r - step_r
                    inside = (from_l >= 0) & (from_l < slots) & (from_r >= 0) & (from_r < across)
                    part = every[side, jnp.clip(from_l, 0, slots - 1), jnp.clip(from_r, 0, across - 1)]
                    block = block + jnp.where(inside, part, 0.0)
                out[l, r] = block

    operands = [*arranged, first, second]
    return call(
        kernel, operands, [VMEM] * len(operands),
        [jax.ShapeDtypeStruct((slots, across, rows, size), jnp.float32)],
        [pltpu.VMEM((2, slots, across, rows, size), jnp.float32)],
    )[0]


def shards(wavefn, left_ops, right_ops, term_shift):
    n_op, n_left, n_right = (lax.axis_size(axis) for axis in ("op", "lsec", "rsec"))
    across = wavefn.shape[1]
    terms, slots, size, _ = left_ops.shape
    ny = n_op // CORES
    share = size // ny
    others = (ny - 1) * share
    rows = size // n_op
    second = slots - 1 if n_left == 2 else slots
    f32, bf16 = jnp.float32, jnp.bfloat16

    def permute(value, target):
        def place(o, l, r):
            return (o % n_op * n_left + l % n_left) * n_right + r % n_right

        perm = [
            (place(o, l, r), place(*target(o, l, r)))
            for o in range(n_op) for l in range(n_left) for r in range(n_right)
        ]
        return lax.ppermute(value, ("op", "lsec", "rsec"), perm)

    def swap(value):
        return permute(value, lambda o, l, r: (o ^ 1, l, r))

    def ahead(value, by):
        return permute(value, lambda o, l, r: (o + CORES * by, l, r))

    def sectors(value, way):
        def target(o, l, r):
            up = way == (l if second < slots else 0)
            return (o, l + 1, r - 1) if up else (o, l - 1, r + 1)

        return permute(value, target)

    def blocks(wide):
        return (slots + second) * wide

    def result(chips, wide):
        return jax.ShapeDtypeStruct((chips, blocks(wide), rows, size), f32)

    def work(many):
        return [
            pltpu.VMEM((terms, slots * many, 2 * size), bf16),
            pltpu.VMEM((2, slots * many // 8, 8, size), f32),
        ]

    def add_cores(refs, outs):
        for at in range(ny - 1):
            first, then = outs[2 * at:2 * at + 2]
            if len(refs) == 2:
                low = first.shape[0]
                first[...] = refs[0][at, :low] + refs[1][at, :low]
                then[...] = refs[0][at, low:] + refs[1][at, low:]
            else:
                wide = len(refs) // 2
                for s in range(slots + second):
                    way = 0 if s < slots else 1
                    for r in range(wide):
                        block = refs[0][at, s * wide + r] + refs[1 + 2 * r + way][at, s - way * slots]
                        outs[2 * at + way][(s - way * slots) * wide + r] = block

    def cores(i, after):
        shapes = [(number * widths[i], rows, size) for number in (slots, second)] * (ny - 1)
        value = sums(add_cores, shapes, [kept[i], *arrived[i]], after)
        return [[ahead(part, by) for by, part in enumerate(value[group::2], 1)] for group in range(2)], value[0]

    def chips(i, after, order):
        def add_own(refs, outs):
            outs[0][...] = refs[0][0] + refs[1][0]

        total = sums(add_own, [(blocks(widths[i]), rows, size)], [own_kept[i], own_arrived[i]], after)[0]
        values = []
        for group in order:
            number = (slots, second)[group]
            low = group * slots * widths[i]

            def add_landed(refs, outs):
                block = refs[0][low:low + number * widths[i]]
                for ref in refs[1:]:
                    block = block + ref[...]
                outs[0][...] = block.reshape(outs[0].shape)

            value = sums(
                add_landed, [(number, widths[i], rows, size)], [total, *landed[i][group]],
                values[-1] if values else None, COSTS[i][group],
            )[0]
            values.append(value)
        return [sectors(values[order.index(group)], group) for group in range(2)], values[-1]

    widths = (across // 2, across - across // 2)
    own_kept, own_arrived, arrived, kept, landed = [], [], [], [], []

    arguments = (term_shift, wavefn, left_ops, right_ops)
    wide = widths[0]
    send, keep, left, right, chosen, lops, psi, rops = call(
        first_others,
        [pltpu.with_memory_space_constraint(value, pltpu.HBM) for value in arguments],
        [HBM] * 4,
        [result(ny - 1, wide)] * 2 + [
            jax.ShapeDtypeStruct((slots, terms * others, 2 * size), bf16),
            jax.ShapeDtypeStruct((wide, terms, 2 * size, size), bf16),
            jax.ShapeDtypeStruct((terms, 2, 8, size), f32),
            jax.ShapeDtypeStruct((terms, slots, share, size), f32),
            jax.ShapeDtypeStruct(wavefn.shape, f32),
            jax.ShapeDtypeStruct((terms, max(across - wide, 1), size, size), f32),
        ],
        [
            pltpu.SMEM(term_shift.shape, jnp.int32),
            pltpu.VMEM((terms, slots, others, size), f32),
            pltpu.VMEM((terms, wide, size, size), f32),
            *work(others),
            pltpu.SemaphoreType.DMA((5,)),
            pltpu.SemaphoreType.DMA((ny,)),
        ],
    )
    kept.append(keep)
    arrived.append([swap(send)])
    send, keep, own = call(
        first_own,
        [lops, psi, right, chosen],
        [VMEM] * 4,
        [result(1, wide)] * 2 + [jax.ShapeDtypeStruct((slots, terms * share, 2 * size), bf16)],
        work(share),
    )
    own_kept.append(keep)
    own_arrived.append(swap(send))
    came, ready = cores(0, keep)
    landed.append(came)
    start, wide = widths
    *send, keep, right = call(
        functools.partial(later_others, start, start),
        [left, psi, rops, chosen, ready],
        [VMEM] * 4 + [ANY],
        [jax.ShapeDtypeStruct((ny - 1, number, rows, size), f32) for number in (slots, second)] * wide + [
            result(ny - 1, wide), jax.ShapeDtypeStruct((wide, terms, 2 * size, size), bf16)
        ],
        work(others),
    )
    arrived.append([swap(value) for value in send])
    kept.append(keep)
    send, keep = call(
        functools.partial(later_own, start),
        [own, psi, right, chosen, keep],
        [VMEM] * 4 + [ANY],
        [result(1, wide)] * 2,
        work(share),
    )
    own_kept.append(keep)
    own_arrived.append(swap(send))
    came, ready = cores(1, keep)
    landed.append(came)
    shifted, ready = chips(0, ready, (0, 1))
    arranged = [arrange(slots, *shifted)]
    (first, last), _ = chips(1, ready, (1, 0))

    def keep_near(refs, outs):
        outs[0][...] = refs[0][...]

    return settle(arranged, first, sums(keep_near, [last.shape], [last], None, LAST_COST)[0])


def solution(mesh):
    placed = (
        P("lsec", "rsec", None, None),
        P("op", "lsec", None, None),
        P("op", "rsec", None, None),
        P("op"),
    )
    return jax.shard_map(
        shards, mesh=mesh, in_specs=placed, out_specs=P("lsec", "rsec", "op", None), check_vma=False
    )
```

```python
import functools

import jax
import jax.numpy as jnp
from jax import lax
from jax.experimental import pallas as pl
from jax.experimental.pallas import tpu as pltpu
from jax.sharding import PartitionSpec as P

WIDTHS = (2, 2)
CORES = 2
ARRANGE_COST = 10 ** 9
ADD_COST = 10 ** 9
LANDED_COST = 10 ** 9
LIMIT = 32 * 1024 * 1024
NT = (((1,), (1,)), ((), ()))
PARAMS = pltpu.CompilerParams(vmem_limit_bytes=LIMIT)
HBM = pl.BlockSpec(memory_space=pltpu.HBM)
VMEM = pl.BlockSpec(memory_space=pltpu.VMEM)
ANY = pl.BlockSpec(memory_space=pl.ANY)


def split(value):
    high = value.astype(jnp.bfloat16)
    low = (value - high.astype(jnp.float32)).astype(jnp.bfloat16)
    return high, low


def choose_rows(lops, left, l):
    terms, _, many, _ = lops.shape
    for t in range(terms):
        left[l, t * many:(t + 1) * many, :] = jnp.concatenate(split(lops[t, l]), axis=1)


def lines(many, rows, slots, second):
    core = lax.rem(lax.axis_index("op"), CORES)
    return core * (rows // 8), (1 - core) * (rows // 8), skipped(slots, second) * (many // 8)


def products(left, psi, right, chosen, inner, total, send, keep, start, begins, lops=None, rops=None, ready=()):
    slots, height, twice = left.shape
    size = twice // 2
    wide, terms = right.shape[:2]
    many = height // terms
    chips, blocks, rows, _ = keep.shape
    second = blocks // wide - slots
    here, there, skip = begins
    for r in range(wide):
        for l in range(slots):
            if r == 0 and lops is not None:
                choose_rows(lops, left, l)
            both = jnp.concatenate(split(psi[l, start + r]), axis=1)
            out = jnp.dot(left[l], jnp.concatenate([both, both], axis=0), preferred_element_type=jnp.float32)
            for t in range(terms):
                block = out[t * many:(t + 1) * many]
                parts = split(block[:, :size] + block[:, size:])
                inner[t, l * many:(l + 1) * many, :] = jnp.concatenate(parts, axis=1)
        if r == 0:
            for copy in ready:
                copy.wait()
        for t in range(terms):
            if rops is not None:
                right[r, t] = jnp.concatenate(split(rops[t, r]), axis=0)
            both = right[r, t]
            out = lax.dot_general(
                inner[t], jnp.concatenate([both, both], axis=1), NT, preferred_element_type=jnp.float32
            )
            out = (out[:, :size] + out[:, size:]).reshape(-1, 8, size)
            for way in range(2):
                mine = out * chosen[t, way]
                total[way] = mine if t == 0 else total[way] + mine
        for chip in range(chips):
            for at in range(slots + second):
                way = 0 if at < slots else 1
                l = at if at < slots else at - slots
                for ref, begin in ((keep, here), (send, there)):
                    line = begin + (l * many + chip * CORES * rows) // 8 + (skip if way else 0)
                    block = total[way, pl.ds(line, rows // 8)].reshape(rows, size)
                    if isinstance(ref, (list, tuple)):
                        ref[r][chip, at] = block
                    else:
                        ref[chip, at * wide + r] = block


def skipped(slots, second):
    return 0 if second == slots else 1 - lax.axis_index("lsec")


def first_others(shift, psi, lops, rops, send, keep, left, right, chosen, lops_own, psi_all, rops_rest, *refs):
    bits, lops_now, rops_now, inner, total, sems, lsems = refs
    terms, slots, size, _ = lops.shape
    wide = right.shape[0]
    ny = lax.axis_size("op") // CORES
    mine = lax.div(lax.axis_index("op"), CORES)
    share = size // ny

    def rows(ahead, target):
        at = pl.multiple_of(lax.rem(mine + ahead, ny) * share, share)
        return pltpu.make_async_copy(lops.at[:, :, pl.ds(at, share)], target, lsems.at[ahead])

    copies = [rows(ahead, lops_now.at[:, :, pl.ds((ahead - 1) * share, share)]) for ahead in range(1, ny)] + [
        pltpu.make_async_copy(psi.at[:, :wide], psi_all.at[:, :wide], sems.at[0]),
        pltpu.make_async_copy(shift, bits, sems.at[1]),
    ]
    ready = [pltpu.make_async_copy(rops.at[:, :wide], rops_now, sems.at[2])]
    later = [rows(0, lops_own)]
    if wide < rops.shape[1]:
        later += [
            pltpu.make_async_copy(psi.at[:, wide:], psi_all.at[:, wide:], sems.at[3]),
            pltpu.make_async_copy(rops.at[:, wide:], rops_rest, sems.at[4]),
        ]
    for copy in copies + ready:
        copy.start()
    second = keep.shape[1] // wide - slots
    begins = lines(lops_now.shape[2], keep.shape[2], slots, second)
    flip = lax.axis_index("lsec") if second < slots else 0
    for copy in copies:
        copy.wait()
    for copy in later:
        copy.start()
    for t in range(terms):
        kept = jnp.where(flip == 1, 1 - bits[t], bits[t]).astype(jnp.float32)
        chosen[t, 0] = jnp.full((8, size), kept, jnp.float32)
        chosen[t, 1] = jnp.full((8, size), 1.0 - kept, jnp.float32)
    products(
        left, psi_all, right, chosen, inner, total, send, keep, 0, begins, lops_now, rops_now, ready
    )
    for copy in later:
        copy.wait()


def find(left, keep, right):
    slots, height, _ = left.shape
    wide, terms = right.shape[:2]
    return lines(height // terms, keep.shape[2], slots, keep.shape[1] // wide - slots)


def first_own(lops, psi, right, chosen, send, keep, left, inner, total):
    products(left, psi, right, chosen, inner, total, send, keep, 0, find(left, keep, right), lops)


def later_others(start, skip, left, psi, rops, chosen, after, *refs):
    wide = refs[-3].shape[0]
    send, (keep, right, inner, total) = refs[:wide], refs[wide:]
    products(
        left, psi, right, chosen, inner, total, send, keep, start, find(left, keep, right),
        rops=rops.at[:, start - skip:],
    )


def later_own(start, left, psi, right, chosen, after, send, keep, inner, total):
    products(left, psi, right, chosen, inner, total, send, keep, start, find(left, keep, right))


def call(kernel, operands, in_specs, out_shape, scratch=(), flops=1):
    return pl.pallas_call(
        kernel,
        in_specs=in_specs,
        out_specs=[VMEM] * len(out_shape),
        out_shape=out_shape,
        scratch_shapes=scratch,
        compiler_params=PARAMS,
        cost_estimate=pl.CostEstimate(flops=flops, bytes_accessed=1024, transcendentals=0),
    )(*operands)


def sums(kernel, shapes, operands, after=None, flops=1):
    reads = len(operands)
    specs = [VMEM] * reads

    def body(*refs):
        kernel(refs[:reads], refs[len(specs):])

    if after is not None:
        operands = [*operands, after]
        specs.append(ANY)
    return call(body, operands, specs, [jax.ShapeDtypeStruct(shape, jnp.float32) for shape in shapes], (), flops)


def arrange(slots, first, second):
    wide, rows, size = first.shape[1:]
    more = second.shape[0]

    def kernel(refs, outs):
        way = 1 - lax.axis_index("lsec") if more < slots else 0
        skip = 1 - skipped(slots, more) if more < slots else 0
        for l in range(slots):
            outs[0][way, l] = refs[0][l]
        for j in range(more):
            outs[0][1 - way, j + skip] = refs[1][j]

    return sums(kernel, [(2, slots, wide, rows, size)], [first, second], None, ARRANGE_COST)[0]


def settle(arranged, first, second):
    slots = first.shape[0]
    rows, size = first.shape[2:]
    more = second.shape[0]
    widths = [value.shape[2] for value in arranged] + [first.shape[1]]
    across = sum(widths)
    n_left, n_right = lax.axis_size("lsec"), lax.axis_size("rsec")

    def kernel(*refs):
        out, every = refs[-2:]
        mine_l, mine_r = lax.axis_index("lsec"), lax.axis_index("rsec")
        first_l, last_l = (mine_l == 0).astype(jnp.int32), (mine_l == n_left - 1).astype(jnp.int32)
        first_r, last_r = (mine_r == 0).astype(jnp.int32), (mine_r == n_right - 1).astype(jnp.int32)
        steps = ((first_l, -last_r), (-last_l, first_r))
        start = 0
        for i, wide in enumerate(widths[:-1]):
            every[:, :, start:start + wide] = refs[i][...]
            start += wide
        way = 1 - mine_l if more < slots else 0
        skip = 1 - skipped(slots, more) if more < slots else 0
        a, b = refs[len(arranged):len(arranged) + 2]
        for l in range(slots):
            every[way, l, start:] = a[l]
        for j in range(more):
            every[1 - way, j + skip, start:] = b[j]
        for l in range(slots):
            for r in range(across):
                block = jnp.zeros((rows, size), jnp.float32)
                for side, (step_l, step_r) in enumerate(steps):
                    from_l, from_r = l - step_l, r - step_r
                    inside = (from_l >= 0) & (from_l < slots) & (from_r >= 0) & (from_r < across)
                    part = every[side, jnp.clip(from_l, 0, slots - 1), jnp.clip(from_r, 0, across - 1)]
                    block = block + jnp.where(inside, part, 0.0)
                out[l, r] = block

    operands = [*arranged, first, second]
    return call(
        kernel, operands, [VMEM] * len(operands),
        [jax.ShapeDtypeStruct((slots, across, rows, size), jnp.float32)],
        [pltpu.VMEM((2, slots, across, rows, size), jnp.float32)],
    )[0]


def shards(wavefn, left_ops, right_ops, term_shift):
    n_op, n_left, n_right = (lax.axis_size(axis) for axis in ("op", "lsec", "rsec"))
    across = wavefn.shape[1]
    terms, slots, size, _ = left_ops.shape
    ny = n_op // CORES
    share = size // ny
    others = (ny - 1) * share
    rows = size // n_op
    second = slots - 1 if n_left == 2 else slots
    f32, bf16 = jnp.float32, jnp.bfloat16

    def permute(value, target):
        def place(o, l, r):
            return (o % n_op * n_left + l % n_left) * n_right + r % n_right

        perm = [
            (place(o, l, r), place(*target(o, l, r)))
            for o in range(n_op) for l in range(n_left) for r in range(n_right)
        ]
        return lax.ppermute(value, ("op", "lsec", "rsec"), perm)

    def swap(value):
        return permute(value, lambda o, l, r: (o ^ 1, l, r))

    def ahead(value, by):
        return permute(value, lambda o, l, r: (o + CORES * by, l, r))

    def sectors(value, way):
        def target(o, l, r):
            up = way == (l if second < slots else 0)
            return (o, l + 1, r - 1) if up else (o, l - 1, r + 1)

        return permute(value, target)

    def blocks(wide):
        return (slots + second) * wide

    def result(chips, wide):
        return jax.ShapeDtypeStruct((chips, blocks(wide), rows, size), f32)

    def work(many):
        return [
            pltpu.VMEM((terms, slots * many, 2 * size), bf16),
            pltpu.VMEM((2, slots * many // 8, 8, size), f32),
        ]

    def add_cores(refs, outs):
        for at, out in enumerate(outs):
            if len(refs) == 2:
                out[...] = refs[0][at] + refs[1][at]
            else:
                wide = len(refs) - 1
                for block in range(out.shape[0]):
                    out[block] = refs[0][at, block] + refs[1 + block % wide][at, block // wide]

    def add_all(refs, outs):
        total = refs[0][...]
        for ref in refs[1:]:
            total = total + ref[...].reshape(total.shape)
        total = total.reshape(-1, rows, size)
        start = 0
        for out in outs:
            count = 1
            for length in out.shape[:-2]:
                count *= length
            out[...] = total[start:start + count].reshape(out.shape)
            start += count

    def landed_first(refs, outs):
        outs[0][...] = refs[0][...]

    widths = WIDTHS if sum(WIDTHS) == across else (across,)
    starts = [sum(widths[:i]) for i in range(len(widths))]
    count = len(widths)
    pieces, own_kept, own_arrived, arrived, kept = [], [], [], [], []

    arguments = (term_shift, wavefn, left_ops, right_ops)
    wide = widths[0]
    send, keep, left, right, chosen, lops, psi, rops = call(
        first_others,
        [pltpu.with_memory_space_constraint(value, pltpu.HBM) for value in arguments],
        [HBM] * 4,
        [result(ny - 1, wide)] * 2 + [
            jax.ShapeDtypeStruct((slots, terms * others, 2 * size), bf16),
            jax.ShapeDtypeStruct((wide, terms, 2 * size, size), bf16),
            jax.ShapeDtypeStruct((terms, 2, 8, size), f32),
            jax.ShapeDtypeStruct((terms, slots, share, size), f32),
            jax.ShapeDtypeStruct(wavefn.shape, f32),
            jax.ShapeDtypeStruct((terms, max(across - wide, 1), size, size), f32),
        ],
        [
            pltpu.SMEM(term_shift.shape, jnp.int32),
            pltpu.VMEM((terms, slots, others, size), f32),
            pltpu.VMEM((terms, wide, size, size), f32),
            *work(others),
            pltpu.SemaphoreType.DMA((5,)),
            pltpu.SemaphoreType.DMA((ny,)),
        ],
    )
    kept.append(keep)
    arrived.append(swap(send))
    send, keep, own = call(
        first_own,
        [lops, psi, right, chosen],
        [VMEM] * 4,
        [result(1, wide)] * 2 + [jax.ShapeDtypeStruct((slots, terms * share, 2 * size), bf16)],
        work(share),
    )
    own_kept.append(keep)
    own_arrived.append(swap(send))
    pieces.append(sums(add_cores, [(blocks(wide), rows, size)] * (ny - 1), [kept[0], arrived[0]], keep))
    for start, wide in zip(starts[1:], widths[1:]):
        *send, keep, right = call(
            functools.partial(later_others, start, widths[0]),
            [left, psi, rops, chosen, pieces[-1][0]],
            [VMEM] * 4 + [ANY],
            [result(ny - 1, 1)] * wide + [
                result(ny - 1, wide), jax.ShapeDtypeStruct((wide, terms, 2 * size, size), bf16)
            ],
            work(others),
        )
        arrived.append([swap(value) for value in send])
        kept.append(keep)
        send, keep = call(
            functools.partial(later_own, start),
            [own, psi, right, chosen, keep],
            [VMEM] * 4 + [ANY],
            [result(1, wide)] * 2,
            work(share),
        )
        own_kept.append(keep)
        own_arrived.append(swap(send))
        pieces.append(sums(
            add_cores, [(blocks(wide), rows, size)] * (ny - 1), [kept[-1], *arrived[-1]], own_kept[-1]
        ))
    arranged = []
    for i, (wide, keep, came) in enumerate(zip(widths, own_kept, own_arrived)):
        landed = [ahead(value, by) for by, value in enumerate(pieces[i], 1)]
        before, after = ([keep, *landed], [came]) if i == 0 else ([keep, came], landed)
        total = sums(add_all, [keep.shape], before, pieces[i + 1][0] if i + 1 < count else None)[0]
        value = sums(add_all, [(slots, wide, rows, size), (second, wide, rows, size)], [total, *after], None, ADD_COST if i == 0 else 1)
        value = [sectors(part, way) for way, part in enumerate(value)]
        value[1] = sums(landed_first, [value[1].shape], [value[1]], None, LANDED_COST)[0]
        if i + 1 < count:
            arranged.append(arrange(slots, *value))
    return settle(arranged, *value)


def solution(mesh):
    placed = (
        P("lsec", "rsec", None, None),
        P("op", "lsec", None, None),
        P("op", "rsec", None, None),
        P("op"),
    )
    return jax.shard_map(
        shards, mesh=mesh, in_specs=placed, out_specs=P("lsec", "rsec", "op", None), check_vma=False
    )
```

```python
import functools

import jax
import jax.numpy as jnp
from jax import lax
from jax.experimental import pallas as pl
from jax.experimental.pallas import tpu as pltpu
from jax.sharding import PartitionSpec as P

WIDTHS = (2, 2)
CORES = 2
ARRANGE_COST = 1
ADD_COST = 2 * 10 ** 9
LANDED_COST = 6 * 10 ** 8
LIMIT = 32 * 1024 * 1024
NT = (((1,), (1,)), ((), ()))
PARAMS = pltpu.CompilerParams(vmem_limit_bytes=LIMIT)
HBM = pl.BlockSpec(memory_space=pltpu.HBM)
VMEM = pl.BlockSpec(memory_space=pltpu.VMEM)
ANY = pl.BlockSpec(memory_space=pl.ANY)


def split(value):
    high = value.astype(jnp.bfloat16)
    low = (value - high.astype(jnp.float32)).astype(jnp.bfloat16)
    return high, low


def choose_rows(lops, left, l):
    terms, _, many, _ = lops.shape
    for t in range(terms):
        left[l, t * many:(t + 1) * many, :] = jnp.concatenate(split(lops[t, l]), axis=1)


def lines(many, rows, slots, second):
    core = lax.rem(lax.axis_index("op"), CORES)
    return core * (rows // 8), (1 - core) * (rows // 8), skipped(slots, second) * (many // 8)


def products(left, psi, right, chosen, inner, total, send, keep, start, begins, lops=None, rops=None, ready=()):
    slots, height, twice = left.shape
    size = twice // 2
    wide, terms = right.shape[:2]
    many = height // terms
    chips, blocks, rows, _ = keep.shape
    second = blocks // wide - slots
    here, there, skip = begins
    for r in range(wide):
        for l in range(slots):
            if r == 0 and lops is not None:
                choose_rows(lops, left, l)
            both = jnp.concatenate(split(psi[l, start + r]), axis=1)
            out = jnp.dot(left[l], jnp.concatenate([both, both], axis=0), preferred_element_type=jnp.float32)
            for t in range(terms):
                block = out[t * many:(t + 1) * many]
                parts = split(block[:, :size] + block[:, size:])
                inner[t, l * many:(l + 1) * many, :] = jnp.concatenate(parts, axis=1)
        if r == 0:
            for copy in ready:
                copy.wait()
        for t in range(terms):
            if rops is not None:
                right[r, t] = jnp.concatenate(split(rops[t, r]), axis=0)
            both = right[r, t]
            out = lax.dot_general(
                inner[t], jnp.concatenate([both, both], axis=1), NT, preferred_element_type=jnp.float32
            )
            out = (out[:, :size] + out[:, size:]).reshape(-1, 8, size)
            for way in range(2):
                mine = out * chosen[t, way]
                total[way] = mine if t == 0 else total[way] + mine
        for chip in range(chips):
            for at in range(slots + second):
                way = 0 if at < slots else 1
                l = at if at < slots else at - slots
                for ref, begin in ((keep, here), (send, there)):
                    line = begin + (l * many + chip * CORES * rows) // 8 + (skip if way else 0)
                    block = total[way, pl.ds(line, rows // 8)].reshape(rows, size)
                    if isinstance(ref, (list, tuple)):
                        ref[r][chip, at] = block
                    else:
                        ref[chip, at * wide + r] = block


def skipped(slots, second):
    return 0 if second == slots else 1 - lax.axis_index("lsec")


def first_others(shift, psi, lops, rops, send, keep, left, right, chosen, lops_own, psi_all, rops_rest, *refs):
    bits, lops_now, rops_now, inner, total, sems, lsems = refs
    terms, slots, size, _ = lops.shape
    wide = right.shape[0]
    ny = lax.axis_size("op") // CORES
    mine = lax.div(lax.axis_index("op"), CORES)
    share = size // ny

    def rows(ahead, target):
        at = pl.multiple_of(lax.rem(mine + ahead, ny) * share, share)
        return pltpu.make_async_copy(lops.at[:, :, pl.ds(at, share)], target, lsems.at[ahead])

    copies = [rows(ahead, lops_now.at[:, :, pl.ds((ahead - 1) * share, share)]) for ahead in range(1, ny)] + [
        pltpu.make_async_copy(psi.at[:, :wide], psi_all.at[:, :wide], sems.at[0]),
        pltpu.make_async_copy(shift, bits, sems.at[1]),
    ]
    ready = [pltpu.make_async_copy(rops.at[:, :wide], rops_now, sems.at[2])]
    later = [rows(0, lops_own)]
    if wide < rops.shape[1]:
        later += [
            pltpu.make_async_copy(psi.at[:, wide:], psi_all.at[:, wide:], sems.at[3]),
            pltpu.make_async_copy(rops.at[:, wide:], rops_rest, sems.at[4]),
        ]
    for copy in copies + ready:
        copy.start()
    second = keep.shape[1] // wide - slots
    begins = lines(lops_now.shape[2], keep.shape[2], slots, second)
    flip = lax.axis_index("lsec") if second < slots else 0
    for copy in copies:
        copy.wait()
    for copy in later:
        copy.start()
    for t in range(terms):
        kept = jnp.where(flip == 1, 1 - bits[t], bits[t]).astype(jnp.float32)
        chosen[t, 0] = jnp.full((8, size), kept, jnp.float32)
        chosen[t, 1] = jnp.full((8, size), 1.0 - kept, jnp.float32)
    products(
        left, psi_all, right, chosen, inner, total, send, keep, 0, begins, lops_now, rops_now, ready
    )
    for copy in later:
        copy.wait()


def find(left, keep, right):
    slots, height, _ = left.shape
    wide, terms = right.shape[:2]
    return lines(height // terms, keep.shape[2], slots, keep.shape[1] // wide - slots)


def first_own(lops, psi, right, chosen, send, keep, left, inner, total):
    products(left, psi, right, chosen, inner, total, send, keep, 0, find(left, keep, right), lops)


def later_others(start, skip, left, psi, rops, chosen, after, *refs):
    wide = refs[-3].shape[0]
    send, (keep, right, inner, total) = refs[:wide], refs[wide:]
    products(
        left, psi, right, chosen, inner, total, send, keep, start, find(left, keep, right),
        rops=rops.at[:, start - skip:],
    )


def later_own(start, left, psi, right, chosen, after, send, keep, inner, total):
    products(left, psi, right, chosen, inner, total, send, keep, start, find(left, keep, right))


def call(kernel, operands, in_specs, out_shape, scratch=(), flops=1):
    return pl.pallas_call(
        kernel,
        in_specs=in_specs,
        out_specs=[VMEM] * len(out_shape),
        out_shape=out_shape,
        scratch_shapes=scratch,
        compiler_params=PARAMS,
        cost_estimate=pl.CostEstimate(flops=flops, bytes_accessed=1024, transcendentals=0),
    )(*operands)


def sums(kernel, shapes, operands, after=None, flops=1):
    reads = len(operands)
    specs = [VMEM] * reads

    def body(*refs):
        kernel(refs[:reads], refs[len(specs):])

    if after is not None:
        operands = [*operands, after]
        specs.append(ANY)
    return call(body, operands, specs, [jax.ShapeDtypeStruct(shape, jnp.float32) for shape in shapes], (), flops)


def arrange(slots, first, second):
    wide, rows, size = first.shape[1:]
    more = second.shape[0]

    def kernel(refs, outs):
        way = 1 - lax.axis_index("lsec") if more < slots else 0
        skip = 1 - skipped(slots, more) if more < slots else 0
        for l in range(slots):
            outs[0][way, l] = refs[0][l]
        for j in range(more):
            outs[0][1 - way, j + skip] = refs[1][j]

    return sums(kernel, [(2, slots, wide, rows, size)], [first, second], None, ARRANGE_COST)[0]


def settle(arranged, first, second):
    slots = first.shape[0]
    rows, size = first.shape[2:]
    more = second.shape[0]
    widths = [value.shape[2] for value in arranged] + [first.shape[1]]
    across = sum(widths)
    n_left, n_right = lax.axis_size("lsec"), lax.axis_size("rsec")

    def kernel(*refs):
        out, every = refs[-2:]
        mine_l, mine_r = lax.axis_index("lsec"), lax.axis_index("rsec")
        first_l, last_l = (mine_l == 0).astype(jnp.int32), (mine_l == n_left - 1).astype(jnp.int32)
        first_r, last_r = (mine_r == 0).astype(jnp.int32), (mine_r == n_right - 1).astype(jnp.int32)
        steps = ((first_l, -last_r), (-last_l, first_r))
        start = 0
        for i, wide in enumerate(widths[:-1]):
            every[:, :, start:start + wide] = refs[i][...]
            start += wide
        way = 1 - mine_l if more < slots else 0
        skip = 1 - skipped(slots, more) if more < slots else 0
        a, b = refs[len(arranged):len(arranged) + 2]
        for l in range(slots):
            every[way, l, start:] = a[l]
        for j in range(more):
            every[1 - way, j + skip, start:] = b[j]
        for l in range(slots):
            for r in range(across):
                block = jnp.zeros((rows, size), jnp.float32)
                for side, (step_l, step_r) in enumerate(steps):
                    from_l, from_r = l - step_l, r - step_r
                    inside = (from_l >= 0) & (from_l < slots) & (from_r >= 0) & (from_r < across)
                    part = every[side, jnp.clip(from_l, 0, slots - 1), jnp.clip(from_r, 0, across - 1)]
                    block = block + jnp.where(inside, part, 0.0)
                out[l, r] = block

    operands = [*arranged, first, second]
    return call(
        kernel, operands, [VMEM] * len(operands),
        [jax.ShapeDtypeStruct((slots, across, rows, size), jnp.float32)],
        [pltpu.VMEM((2, slots, across, rows, size), jnp.float32)],
    )[0]


def shards(wavefn, left_ops, right_ops, term_shift):
    n_op, n_left, n_right = (lax.axis_size(axis) for axis in ("op", "lsec", "rsec"))
    across = wavefn.shape[1]
    terms, slots, size, _ = left_ops.shape
    ny = n_op // CORES
    share = size // ny
    others = (ny - 1) * share
    rows = size // n_op
    second = slots - 1 if n_left == 2 else slots
    f32, bf16 = jnp.float32, jnp.bfloat16

    def permute(value, target):
        def place(o, l, r):
            return (o % n_op * n_left + l % n_left) * n_right + r % n_right

        perm = [
            (place(o, l, r), place(*target(o, l, r)))
            for o in range(n_op) for l in range(n_left) for r in range(n_right)
        ]
        return lax.ppermute(value, ("op", "lsec", "rsec"), perm)

    def swap(value):
        return permute(value, lambda o, l, r: (o ^ 1, l, r))

    def ahead(value, by):
        return permute(value, lambda o, l, r: (o + CORES * by, l, r))

    def sectors(value, way):
        def target(o, l, r):
            up = way == (l if second < slots else 0)
            return (o, l + 1, r - 1) if up else (o, l - 1, r + 1)

        return permute(value, target)

    def blocks(wide):
        return (slots + second) * wide

    def result(chips, wide):
        return jax.ShapeDtypeStruct((chips, blocks(wide), rows, size), f32)

    def work(many):
        return [
            pltpu.VMEM((terms, slots * many, 2 * size), bf16),
            pltpu.VMEM((2, slots * many // 8, 8, size), f32),
        ]

    def add_cores(refs, outs):
        for at, out in enumerate(outs):
            if len(refs) == 2:
                out[...] = refs[0][at] + refs[1][at]
            else:
                wide = len(refs) - 1
                for block in range(out.shape[0]):
                    out[block] = refs[0][at, block] + refs[1 + block % wide][at, block // wide]

    def add_all(refs, outs):
        total = refs[0][...]
        for ref in refs[1:]:
            total = total + ref[...].reshape(total.shape)
        total = total.reshape(-1, rows, size)
        start = 0
        for out in outs:
            count = 1
            for length in out.shape[:-2]:
                count *= length
            out[...] = total[start:start + count].reshape(out.shape)
            start += count

    def landed_first(refs, outs):
        outs[0][...] = refs[0][...]

    widths = WIDTHS if sum(WIDTHS) == across else (across,)
    starts = [sum(widths[:i]) for i in range(len(widths))]
    count = len(widths)
    pieces, own_kept, own_arrived, arrived, kept = [], [], [], [], []

    arguments = (term_shift, wavefn, left_ops, right_ops)
    wide = widths[0]
    send, keep, left, right, chosen, lops, psi, rops = call(
        first_others,
        [pltpu.with_memory_space_constraint(value, pltpu.HBM) for value in arguments],
        [HBM] * 4,
        [result(ny - 1, wide)] * 2 + [
            jax.ShapeDtypeStruct((slots, terms * others, 2 * size), bf16),
            jax.ShapeDtypeStruct((wide, terms, 2 * size, size), bf16),
            jax.ShapeDtypeStruct((terms, 2, 8, size), f32),
            jax.ShapeDtypeStruct((terms, slots, share, size), f32),
            jax.ShapeDtypeStruct(wavefn.shape, f32),
            jax.ShapeDtypeStruct((terms, max(across - wide, 1), size, size), f32),
        ],
        [
            pltpu.SMEM(term_shift.shape, jnp.int32),
            pltpu.VMEM((terms, slots, others, size), f32),
            pltpu.VMEM((terms, wide, size, size), f32),
            *work(others),
            pltpu.SemaphoreType.DMA((5,)),
            pltpu.SemaphoreType.DMA((ny,)),
        ],
    )
    kept.append(keep)
    arrived.append(swap(send))
    send, keep, own = call(
        first_own,
        [lops, psi, right, chosen],
        [VMEM] * 4,
        [result(1, wide)] * 2 + [jax.ShapeDtypeStruct((slots, terms * share, 2 * size), bf16)],
        work(share),
    )
    own_kept.append(keep)
    own_arrived.append(swap(send))
    pieces.append(sums(add_cores, [(blocks(wide), rows, size)] * (ny - 1), [kept[0], arrived[0]], keep))
    for start, wide in zip(starts[1:], widths[1:]):
        *send, keep, right = call(
            functools.partial(later_others, start, widths[0]),
            [left, psi, rops, chosen, pieces[-1][0]],
            [VMEM] * 4 + [ANY],
            [result(ny - 1, 1)] * wide + [
                result(ny - 1, wide), jax.ShapeDtypeStruct((wide, terms, 2 * size, size), bf16)
            ],
            work(others),
        )
        arrived.append([swap(value) for value in send])
        kept.append(keep)
        send, keep = call(
            functools.partial(later_own, start),
            [own, psi, right, chosen, keep],
            [VMEM] * 4 + [ANY],
            [result(1, wide)] * 2,
            work(share),
        )
        own_kept.append(keep)
        own_arrived.append(swap(send))
        pieces.append(sums(
            add_cores, [(blocks(wide), rows, size)] * (ny - 1), [kept[-1], *arrived[-1]], own_kept[-1]
        ))
    arranged = []
    for i, (wide, keep, came) in enumerate(zip(widths, own_kept, own_arrived)):
        landed = [ahead(value, by) for by, value in enumerate(pieces[i], 1)]
        before, after = ([keep, *landed], [came]) if i == 0 else ([keep, came], landed)
        total = sums(add_all, [keep.shape], before, pieces[i + 1][0] if i + 1 < count else None)[0]
        value = sums(add_all, [(slots, wide, rows, size), (second, wide, rows, size)], [total, *after], None, ADD_COST if i == 0 else 1)
        value = [sectors(part, way) for way, part in enumerate(value)]
        value[1] = sums(landed_first, [value[1].shape], [value[1]], None, LANDED_COST)[0]
        if i + 1 < count:
            arranged.append(arrange(slots, *value))
    return settle(arranged, *value)


def solution(mesh):
    placed = (
        P("lsec", "rsec", None, None),
        P("op", "lsec", None, None),
        P("op", "rsec", None, None),
        P("op"),
    )
    return jax.shard_map(
        shards, mesh=mesh, in_specs=placed, out_specs=P("lsec", "rsec", "op", None), check_vma=False
    )
```

```python
import functools

import jax
import jax.numpy as jnp
from jax import lax
from jax.experimental import pallas as pl
from jax.experimental.pallas import tpu as pltpu
from jax.sharding import PartitionSpec as P

CORES = 2
ARRANGE_COST = 1
ADD_COST = 2 * 10 ** 9
LANDED_COST = 6 * 10 ** 8
LIMIT = 32 * 1024 * 1024
NT = (((1,), (1,)), ((), ()))
PARAMS = pltpu.CompilerParams(vmem_limit_bytes=LIMIT)
HBM = pl.BlockSpec(memory_space=pltpu.HBM)
VMEM = pl.BlockSpec(memory_space=pltpu.VMEM)
ANY = pl.BlockSpec(memory_space=pl.ANY)


def split(value):
    high = value.astype(jnp.bfloat16)
    low = (value - high.astype(jnp.float32)).astype(jnp.bfloat16)
    return high, low


def choose_rows(lops, left, l):
    terms, _, many, _ = lops.shape
    for t in range(terms):
        left[l, t * many:(t + 1) * many, :] = jnp.concatenate(split(lops[t, l]), axis=1)


def lines(many, rows, slots, second):
    core = lax.rem(lax.axis_index("op"), CORES)
    return core * (rows // 8), (1 - core) * (rows // 8), skipped(slots, second) * (many // 8)


def products(left, psi, right, chosen, inner, total, send, keep, start, begins, lops=None, rops=None, ready=()):
    slots, height, twice = left.shape
    size = twice // 2
    wide, terms = right.shape[:2]
    many = height // terms
    chips, blocks, rows, _ = keep.shape
    second = blocks // wide - slots
    here, there, skip = begins
    for r in range(wide):
        for l in range(slots):
            if r == 0 and lops is not None:
                choose_rows(lops, left, l)
            both = jnp.concatenate(split(psi[l, start + r]), axis=1)
            out = jnp.dot(left[l], jnp.concatenate([both, both], axis=0), preferred_element_type=jnp.float32)
            for t in range(terms):
                block = out[t * many:(t + 1) * many]
                parts = split(block[:, :size] + block[:, size:])
                inner[t, l * many:(l + 1) * many, :] = jnp.concatenate(parts, axis=1)
        if r == 0:
            for copy in ready:
                copy.wait()
        for t in range(terms):
            if rops is not None:
                right[r, t] = jnp.concatenate(split(rops[t, r]), axis=0)
            both = right[r, t]
            out = lax.dot_general(
                inner[t], jnp.concatenate([both, both], axis=1), NT, preferred_element_type=jnp.float32
            )
            out = (out[:, :size] + out[:, size:]).reshape(-1, 8, size)
            for way in range(2):
                mine = out * chosen[t, way]
                total[way] = mine if t == 0 else total[way] + mine
        for chip in range(chips):
            for at in range(slots + second):
                way = 0 if at < slots else 1
                l = at if at < slots else at - slots
                for ref, begin in ((keep, here), (send, there)):
                    line = begin + (l * many + chip * CORES * rows) // 8 + (skip if way else 0)
                    block = total[way, pl.ds(line, rows // 8)].reshape(rows, size)
                    if isinstance(ref, (list, tuple)):
                        ref[r][chip, at] = block
                    else:
                        ref[chip, at * wide + r] = block


def skipped(slots, second):
    return 0 if second == slots else 1 - lax.axis_index("lsec")


def first_others(shift, psi, lops, rops, send, keep, left, right, chosen, lops_own, psi_all, rops_rest, *refs):
    bits, lops_now, rops_now, inner, total, sems, lsems = refs
    terms, slots, size, _ = lops.shape
    wide = right.shape[0]
    ny = lax.axis_size("op") // CORES
    mine = lax.div(lax.axis_index("op"), CORES)
    share = size // ny

    def rows(ahead, target):
        at = pl.multiple_of(lax.rem(mine + ahead, ny) * share, share)
        return pltpu.make_async_copy(lops.at[:, :, pl.ds(at, share)], target, lsems.at[ahead])

    copies = [rows(ahead, lops_now.at[:, :, pl.ds((ahead - 1) * share, share)]) for ahead in range(1, ny)] + [
        pltpu.make_async_copy(psi.at[:, :wide], psi_all.at[:, :wide], sems.at[0]),
        pltpu.make_async_copy(shift, bits, sems.at[1]),
    ]
    ready = [pltpu.make_async_copy(rops.at[:, :wide], rops_now, sems.at[2])]
    later = [rows(0, lops_own)]
    if wide < rops.shape[1]:
        later += [
            pltpu.make_async_copy(psi.at[:, wide:], psi_all.at[:, wide:], sems.at[3]),
            pltpu.make_async_copy(rops.at[:, wide:], rops_rest, sems.at[4]),
        ]
    for copy in copies + ready:
        copy.start()
    second = keep.shape[1] // wide - slots
    begins = lines(lops_now.shape[2], keep.shape[2], slots, second)
    flip = lax.axis_index("lsec") if second < slots else 0
    for copy in copies:
        copy.wait()
    for copy in later:
        copy.start()
    for t in range(terms):
        kept = jnp.where(flip == 1, 1 - bits[t], bits[t]).astype(jnp.float32)
        chosen[t, 0] = jnp.full((8, size), kept, jnp.float32)
        chosen[t, 1] = jnp.full((8, size), 1.0 - kept, jnp.float32)
    products(
        left, psi_all, right, chosen, inner, total, send, keep, 0, begins, lops_now, rops_now, ready
    )
    for copy in later:
        copy.wait()


def find(left, keep, right):
    slots, height, _ = left.shape
    wide, terms = right.shape[:2]
    return lines(height // terms, keep.shape[2], slots, keep.shape[1] // wide - slots)


def first_own(lops, psi, right, chosen, send, keep, left, inner, total):
    products(left, psi, right, chosen, inner, total, send, keep, 0, find(left, keep, right), lops)


def later_others(start, skip, left, psi, rops, chosen, after, *refs):
    wide = refs[-3].shape[0]
    send, (keep, right, inner, total) = refs[:wide], refs[wide:]
    products(
        left, psi, right, chosen, inner, total, send, keep, start, find(left, keep, right),
        rops=rops.at[:, start - skip:],
    )


def later_own(start, left, psi, right, chosen, after, send, keep, inner, total):
    products(left, psi, right, chosen, inner, total, send, keep, start, find(left, keep, right))


def call(kernel, operands, in_specs, out_shape, scratch=(), flops=1):
    return pl.pallas_call(
        kernel,
        in_specs=in_specs,
        out_specs=[VMEM] * len(out_shape),
        out_shape=out_shape,
        scratch_shapes=scratch,
        compiler_params=PARAMS,
        cost_estimate=pl.CostEstimate(flops=flops, bytes_accessed=1024, transcendentals=0),
    )(*operands)


def sums(kernel, shapes, operands, after=None, flops=1):
    reads = len(operands)
    specs = [VMEM] * reads

    def body(*refs):
        kernel(refs[:reads], refs[len(specs):])

    if after is not None:
        operands = [*operands, after]
        specs.append(ANY)
    return call(body, operands, specs, [jax.ShapeDtypeStruct(shape, jnp.float32) for shape in shapes], (), flops)


def arrange(slots, first, second):
    wide, rows, size = first.shape[1:]
    more = second.shape[0]

    def kernel(refs, outs):
        way = 1 - lax.axis_index("lsec") if more < slots else 0
        skip = 1 - skipped(slots, more) if more < slots else 0
        for l in range(slots):
            outs[0][way, l] = refs[0][l]
        for j in range(more):
            outs[0][1 - way, j + skip] = refs[1][j]

    return sums(kernel, [(2, slots, wide, rows, size)], [first, second], None, ARRANGE_COST)[0]


def settle(arranged, first, second):
    slots = first.shape[0]
    rows, size = first.shape[2:]
    more = second.shape[0]
    widths = [value.shape[2] for value in arranged] + [first.shape[1]]
    across = sum(widths)
    n_left, n_right = lax.axis_size("lsec"), lax.axis_size("rsec")

    def kernel(*refs):
        out, every = refs[-2:]
        mine_l, mine_r = lax.axis_index("lsec"), lax.axis_index("rsec")
        first_l, last_l = (mine_l == 0).astype(jnp.int32), (mine_l == n_left - 1).astype(jnp.int32)
        first_r, last_r = (mine_r == 0).astype(jnp.int32), (mine_r == n_right - 1).astype(jnp.int32)
        steps = ((first_l, -last_r), (-last_l, first_r))
        start = 0
        for i, wide in enumerate(widths[:-1]):
            every[:, :, start:start + wide] = refs[i][...]
            start += wide
        way = 1 - mine_l if more < slots else 0
        skip = 1 - skipped(slots, more) if more < slots else 0
        a, b = refs[len(arranged):len(arranged) + 2]
        for l in range(slots):
            every[way, l, start:] = a[l]
        for j in range(more):
            every[1 - way, j + skip, start:] = b[j]
        for l in range(slots):
            for r in range(across):
                block = jnp.zeros((rows, size), jnp.float32)
                for side, (step_l, step_r) in enumerate(steps):
                    from_l, from_r = l - step_l, r - step_r
                    inside = (from_l >= 0) & (from_l < slots) & (from_r >= 0) & (from_r < across)
                    part = every[side, jnp.clip(from_l, 0, slots - 1), jnp.clip(from_r, 0, across - 1)]
                    block = block + jnp.where(inside, part, 0.0)
                out[l, r] = block

    operands = [*arranged, first, second]
    return call(
        kernel, operands, [VMEM] * len(operands),
        [jax.ShapeDtypeStruct((slots, across, rows, size), jnp.float32)],
        [pltpu.VMEM((2, slots, across, rows, size), jnp.float32)],
    )[0]


def shards(wavefn, left_ops, right_ops, term_shift):
    n_op, n_left, n_right = (lax.axis_size(axis) for axis in ("op", "lsec", "rsec"))
    across = wavefn.shape[1]
    terms, slots, size, _ = left_ops.shape
    ny = n_op // CORES
    share = size // ny
    others = (ny - 1) * share
    rows = size // n_op
    second = slots - 1 if n_left == 2 else slots
    f32, bf16 = jnp.float32, jnp.bfloat16

    def permute(value, target):
        def place(o, l, r):
            return (o % n_op * n_left + l % n_left) * n_right + r % n_right

        perm = [
            (place(o, l, r), place(*target(o, l, r)))
            for o in range(n_op) for l in range(n_left) for r in range(n_right)
        ]
        return lax.ppermute(value, ("op", "lsec", "rsec"), perm)

    def swap(value):
        return permute(value, lambda o, l, r: (o ^ 1, l, r))

    def ahead(value, by):
        return permute(value, lambda o, l, r: (o + CORES * by, l, r))

    def sectors(value, way):
        def target(o, l, r):
            up = way == (l if second < slots else 0)
            return (o, l + 1, r - 1) if up else (o, l - 1, r + 1)

        return permute(value, target)

    def blocks(wide):
        return (slots + second) * wide

    def result(chips, wide):
        return jax.ShapeDtypeStruct((chips, blocks(wide), rows, size), f32)

    def work(many):
        return [
            pltpu.VMEM((terms, slots * many, 2 * size), bf16),
            pltpu.VMEM((2, slots * many // 8, 8, size), f32),
        ]

    def add_cores(refs, outs):
        for at, out in enumerate(outs):
            if len(refs) == 2:
                out[...] = refs[0][at] + refs[1][at]
            else:
                wide = len(refs) - 1
                first = 0 if at % 2 else slots * wide
                for block in range(first, first + out.shape[0]):
                    out[block - first] = refs[0][at // 2, block] + refs[1 + block % wide][at // 2, block // wide]

    def add_all(refs, outs):
        total = refs[0][...]
        for ref in refs[1:]:
            total = total + ref[...].reshape(total.shape)
        total = total.reshape(-1, rows, size)
        start = 0
        for out in outs:
            count = 1
            for length in out.shape[:-2]:
                count *= length
            out[...] = total[start:start + count].reshape(out.shape)
            start += count

    def landed_first(refs, outs):
        outs[0][...] = refs[0][...]

    widths = (across // 2, across - across // 2)
    starts = [sum(widths[:i]) for i in range(len(widths))]
    pieces, own_kept, own_arrived, arrived, kept = [], [], [], [], []

    arguments = (term_shift, wavefn, left_ops, right_ops)
    wide = widths[0]
    send, keep, left, right, chosen, lops, psi, rops = call(
        first_others,
        [pltpu.with_memory_space_constraint(value, pltpu.HBM) for value in arguments],
        [HBM] * 4,
        [result(ny - 1, wide)] * 2 + [
            jax.ShapeDtypeStruct((slots, terms * others, 2 * size), bf16),
            jax.ShapeDtypeStruct((wide, terms, 2 * size, size), bf16),
            jax.ShapeDtypeStruct((terms, 2, 8, size), f32),
            jax.ShapeDtypeStruct((terms, slots, share, size), f32),
            jax.ShapeDtypeStruct(wavefn.shape, f32),
            jax.ShapeDtypeStruct((terms, max(across - wide, 1), size, size), f32),
        ],
        [
            pltpu.SMEM(term_shift.shape, jnp.int32),
            pltpu.VMEM((terms, slots, others, size), f32),
            pltpu.VMEM((terms, wide, size, size), f32),
            *work(others),
            pltpu.SemaphoreType.DMA((5,)),
            pltpu.SemaphoreType.DMA((ny,)),
        ],
    )
    kept.append(keep)
    arrived.append(swap(send))
    send, keep, own = call(
        first_own,
        [lops, psi, right, chosen],
        [VMEM] * 4,
        [result(1, wide)] * 2 + [jax.ShapeDtypeStruct((slots, terms * share, 2 * size), bf16)],
        work(share),
    )
    own_kept.append(keep)
    own_arrived.append(swap(send))
    pieces.append(sums(add_cores, [(blocks(wide), rows, size)] * (ny - 1), [kept[0], arrived[0]], keep))
    for start, wide in zip(starts[1:], widths[1:]):
        *send, keep, right = call(
            functools.partial(later_others, start, widths[0]),
            [left, psi, rops, chosen, pieces[-1][0]],
            [VMEM] * 4 + [ANY],
            [result(ny - 1, 1)] * wide + [
                result(ny - 1, wide), jax.ShapeDtypeStruct((wide, terms, 2 * size, size), bf16)
            ],
            work(others),
        )
        arrived.append([swap(value) for value in send])
        kept.append(keep)
        send, keep = call(
            functools.partial(later_own, start),
            [own, psi, right, chosen, keep],
            [VMEM] * 4 + [ANY],
            [result(1, wide)] * 2,
            work(share),
        )
        own_kept.append(keep)
        own_arrived.append(swap(send))
        groups = [(number * wide, rows, size) for number in (second, slots)]
        pieces.append(sums(add_cores, groups * (ny - 1), [kept[-1], *arrived[-1]], own_kept[-1]))

    def land(values):
        return [ahead(value, by) for by, value in enumerate(values, 1)]

    wide = widths[0]
    total = sums(add_all, [own_kept[0].shape], [own_kept[0], *land(pieces[0])], pieces[1][0])[0]
    value = sums(
        add_all, [(slots, wide, rows, size), (second, wide, rows, size)], [total, own_arrived[0]], None, ADD_COST
    )
    ready = value[1]
    value = [sectors(part, way) for way, part in enumerate(value)]
    value[1] = sums(landed_first, [value[1].shape], [value[1]], None, LANDED_COST)[0]
    arranged = [arrange(slots, *value)]

    wide = widths[1]
    total = sums(add_all, [(blocks(wide), rows, size)], [own_kept[1], own_arrived[1]], ready)[0]

    def add_group(refs, outs):
        block = refs[0][first:first + refs[1].shape[0]]
        for ref in refs[1:]:
            block = block + ref[...]
        outs[0][...] = block.reshape(outs[0].shape)

    value = []
    for way, number, first in ((1, second, slots * wide), (0, slots, 0)):
        came = land(pieces[1][1 - way::2])
        ready = sums(add_group, [(number, wide, rows, size)], [total, *came], ready)[0]
        value.append(sectors(ready, way))
    value[0] = sums(landed_first, [value[0].shape], [value[0]], arranged[0], LANDED_COST)[0]
    return settle(arranged, value[1], value[0])


def solution(mesh):
    placed = (
        P("lsec", "rsec", None, None),
        P("op", "lsec", None, None),
        P("op", "rsec", None, None),
        P("op"),
    )
    return jax.shard_map(
        shards, mesh=mesh, in_specs=placed, out_specs=P("lsec", "rsec", "op", None), check_vma=False
    )
```

```python
import functools

import jax
import jax.numpy as jnp
from jax import lax
from jax.experimental import pallas as pl
from jax.experimental.pallas import tpu as pltpu
from jax.sharding import PartitionSpec as P

CORES = 2
ARRANGE_COST = 1
ADD_COST = 2 * 10 ** 9
LANDED_COST = 6 * 10 ** 8
LIMIT = 32 * 1024 * 1024
NT = (((1,), (1,)), ((), ()))
PARAMS = pltpu.CompilerParams(vmem_limit_bytes=LIMIT)
HBM = pl.BlockSpec(memory_space=pltpu.HBM)
VMEM = pl.BlockSpec(memory_space=pltpu.VMEM)
ANY = pl.BlockSpec(memory_space=pl.ANY)


def split(value):
    high = value.astype(jnp.bfloat16)
    low = (value - high.astype(jnp.float32)).astype(jnp.bfloat16)
    return high, low


def choose_rows(lops, left, l):
    terms, _, many, _ = lops.shape
    for t in range(terms):
        left[l, t * many:(t + 1) * many, :] = jnp.concatenate(split(lops[t, l]), axis=1)


def lines(many, rows, slots, second):
    core = lax.rem(lax.axis_index("op"), CORES)
    return core * (rows // 8), (1 - core) * (rows // 8), skipped(slots, second) * (many // 8)


def products(left, psi, right, way_of, inner, total, send, keep, start, begins, lops=None, rops=None, ready=()):
    slots, height, twice = left.shape
    size = twice // 2
    wide, terms = right.shape[:2]
    many = height // terms
    chips, blocks, rows, _ = keep.shape
    second = blocks // wide - slots
    here, there, skip = begins
    for r in range(wide):
        for l in range(slots):
            if r == 0 and lops is not None:
                choose_rows(lops, left, l)
            both = jnp.concatenate(split(psi[l, start + r]), axis=1)
            out = jnp.dot(left[l], jnp.concatenate([both, both], axis=0), preferred_element_type=jnp.float32)
            for t in range(terms):
                block = out[t * many:(t + 1) * many]
                parts = split(block[:, :size] + block[:, size:])
                inner[t, l * many:(l + 1) * many, :] = jnp.concatenate(parts, axis=1)
        if r == 0:
            for copy in ready:
                copy.wait()
        total[...] = jnp.zeros_like(total)
        for t in range(terms):
            if rops is not None:
                right[r, t] = jnp.concatenate(split(rops[t, r]), axis=0)
            both = right[r, t]
            out = lax.dot_general(
                inner[t], jnp.concatenate([both, both], axis=1), NT, preferred_element_type=jnp.float32
            )
            out = (out[:, :size] + out[:, size:]).reshape(-1, 8, size)
            way = way_of(t)
            total[way] = total[way] + out
        for chip in range(chips):
            for at in range(slots + second):
                way = 0 if at < slots else 1
                l = at if at < slots else at - slots
                for ref, begin in ((keep, here), (send, there)):
                    line = begin + (l * many + chip * CORES * rows) // 8 + (skip if way else 0)
                    block = total[way, pl.ds(line, rows // 8)].reshape(rows, size)
                    if isinstance(ref, (list, tuple)):
                        ref[r][chip, at] = block
                    else:
                        ref[chip, at * wide + r] = block


def skipped(slots, second):
    return 0 if second == slots else 1 - lax.axis_index("lsec")


def first_others(shift, psi, lops, rops, send, keep, left, right, lops_own, psi_all, rops_rest, *refs):
    bits, lops_now, rops_now, inner, total, sems, lsems = refs
    terms, slots, size, _ = lops.shape
    wide = right.shape[0]
    ny = lax.axis_size("op") // CORES
    mine = lax.div(lax.axis_index("op"), CORES)
    share = size // ny

    def rows(ahead, target):
        at = pl.multiple_of(lax.rem(mine + ahead, ny) * share, share)
        return pltpu.make_async_copy(lops.at[:, :, pl.ds(at, share)], target, lsems.at[ahead])

    copies = [rows(ahead, lops_now.at[:, :, pl.ds((ahead - 1) * share, share)]) for ahead in range(1, ny)] + [
        pltpu.make_async_copy(psi.at[:, :wide], psi_all.at[:, :wide], sems.at[0]),
        pltpu.make_async_copy(shift, bits, sems.at[1]),
    ]
    ready = [pltpu.make_async_copy(rops.at[:, :wide], rops_now, sems.at[2])]
    later = [rows(0, lops_own)]
    if wide < rops.shape[1]:
        later += [
            pltpu.make_async_copy(psi.at[:, wide:], psi_all.at[:, wide:], sems.at[3]),
            pltpu.make_async_copy(rops.at[:, wide:], rops_rest, sems.at[4]),
        ]
    for copy in copies + ready:
        copy.start()
    second = keep.shape[1] // wide - slots
    begins = lines(lops_now.shape[2], keep.shape[2], slots, second)
    way_of = classes(bits, second < slots)
    for copy in copies:
        copy.wait()
    for copy in later:
        copy.start()
    products(
        left, psi_all, right, way_of, inner, total, send, keep, 0, begins, lops_now, rops_now, ready
    )
    for copy in later:
        copy.wait()


def find(left, keep, right):
    slots, height, _ = left.shape
    wide, terms = right.shape[:2]
    return lines(height // terms, keep.shape[2], slots, keep.shape[1] // wide - slots)


def classes(bits, paired):
    flip = lax.axis_index("lsec") if paired else 0
    return lambda t: jnp.where(flip == 1, bits[t], 1 - bits[t])


def again(shift, left, psi, right, inner, total, bits, sem, send, keep, start, **extra):
    copy = pltpu.make_async_copy(shift, bits, sem.at[0])
    copy.start()
    paired = keep.shape[1] < 2 * right.shape[0] * left.shape[0]
    products(
        left, psi, right, classes(bits, paired), inner, total, send, keep, start, find(left, keep, right),
        ready=[copy], **extra,
    )


def first_own(shift, lops, psi, right, send, keep, left, inner, total, bits, sem):
    again(shift, left, psi, right, inner, total, bits, sem, send, keep, 0, lops=lops)


def later_others(start, skip, shift, left, psi, rops, after, *refs):
    wide = refs[-5].shape[0]
    send, (keep, right, inner, total, bits, sem) = refs[:wide], refs[wide:]
    again(shift, left, psi, right, inner, total, bits, sem, send, keep, start, rops=rops.at[:, start - skip:])


def later_own(start, shift, left, psi, right, after, send, keep, inner, total, bits, sem):
    again(shift, left, psi, right, inner, total, bits, sem, send, keep, start)


def call(kernel, operands, in_specs, out_shape, scratch=(), flops=1):
    return pl.pallas_call(
        kernel,
        in_specs=in_specs,
        out_specs=[VMEM] * len(out_shape),
        out_shape=out_shape,
        scratch_shapes=scratch,
        compiler_params=PARAMS,
        cost_estimate=pl.CostEstimate(flops=flops, bytes_accessed=1024, transcendentals=0),
    )(*operands)


def sums(kernel, shapes, operands, after=None, flops=1):
    reads = len(operands)
    specs = [VMEM] * reads

    def body(*refs):
        kernel(refs[:reads], refs[len(specs):])

    if after is not None:
        operands = [*operands, after]
        specs.append(ANY)
    return call(body, operands, specs, [jax.ShapeDtypeStruct(shape, jnp.float32) for shape in shapes], (), flops)


def arrange(slots, first, second):
    wide, rows, size = first.shape[1:]
    more = second.shape[0]

    def kernel(refs, outs):
        way = 1 - lax.axis_index("lsec") if more < slots else 0
        skip = 1 - skipped(slots, more) if more < slots else 0
        for l in range(slots):
            outs[0][way, l] = refs[0][l]
        for j in range(more):
            outs[0][1 - way, j + skip] = refs[1][j]

    return sums(kernel, [(2, slots, wide, rows, size)], [first, second], None, ARRANGE_COST)[0]


def settle(arranged, first, second):
    slots = first.shape[0]
    rows, size = first.shape[2:]
    more = second.shape[0]
    widths = [value.shape[2] for value in arranged] + [first.shape[1]]
    across = sum(widths)
    n_left, n_right = lax.axis_size("lsec"), lax.axis_size("rsec")

    def kernel(*refs):
        out, every = refs[-2:]
        mine_l, mine_r = lax.axis_index("lsec"), lax.axis_index("rsec")
        first_l, last_l = (mine_l == 0).astype(jnp.int32), (mine_l == n_left - 1).astype(jnp.int32)
        first_r, last_r = (mine_r == 0).astype(jnp.int32), (mine_r == n_right - 1).astype(jnp.int32)
        steps = ((first_l, -last_r), (-last_l, first_r))
        start = 0
        for i, wide in enumerate(widths[:-1]):
            every[:, :, start:start + wide] = refs[i][...]
            start += wide
        way = 1 - mine_l if more < slots else 0
        skip = 1 - skipped(slots, more) if more < slots else 0
        a, b = refs[len(arranged):len(arranged) + 2]
        for l in range(slots):
            every[way, l, start:] = a[l]
        for j in range(more):
            every[1 - way, j + skip, start:] = b[j]
        for l in range(slots):
            for r in range(across):
                block = jnp.zeros((rows, size), jnp.float32)
                for side, (step_l, step_r) in enumerate(steps):
                    from_l, from_r = l - step_l, r - step_r
                    inside = (from_l >= 0) & (from_l < slots) & (from_r >= 0) & (from_r < across)
                    part = every[side, jnp.clip(from_l, 0, slots - 1), jnp.clip(from_r, 0, across - 1)]
                    block = block + jnp.where(inside, part, 0.0)
                out[l, r] = block

    operands = [*arranged, first, second]
    return call(
        kernel, operands, [VMEM] * len(operands),
        [jax.ShapeDtypeStruct((slots, across, rows, size), jnp.float32)],
        [pltpu.VMEM((2, slots, across, rows, size), jnp.float32)],
    )[0]


def shards(wavefn, left_ops, right_ops, term_shift):
    n_op, n_left, n_right = (lax.axis_size(axis) for axis in ("op", "lsec", "rsec"))
    across = wavefn.shape[1]
    terms, slots, size, _ = left_ops.shape
    ny = n_op // CORES
    share = size // ny
    others = (ny - 1) * share
    rows = size // n_op
    second = slots - 1 if n_left == 2 else slots
    f32, bf16 = jnp.float32, jnp.bfloat16

    def permute(value, target):
        def place(o, l, r):
            return (o % n_op * n_left + l % n_left) * n_right + r % n_right

        perm = [
            (place(o, l, r), place(*target(o, l, r)))
            for o in range(n_op) for l in range(n_left) for r in range(n_right)
        ]
        return lax.ppermute(value, ("op", "lsec", "rsec"), perm)

    def swap(value):
        return permute(value, lambda o, l, r: (o ^ 1, l, r))

    def ahead(value, by):
        return permute(value, lambda o, l, r: (o + CORES * by, l, r))

    def sectors(value, way):
        def target(o, l, r):
            up = way == (l if second < slots else 0)
            return (o, l + 1, r - 1) if up else (o, l - 1, r + 1)

        return permute(value, target)

    def blocks(wide):
        return (slots + second) * wide

    def result(chips, wide):
        return jax.ShapeDtypeStruct((chips, blocks(wide), rows, size), f32)

    def work(many):
        return [
            pltpu.VMEM((terms, slots * many, 2 * size), bf16),
            pltpu.VMEM((2, slots * many // 8, 8, size), f32),
        ]

    def add_cores(refs, outs):
        for at, out in enumerate(outs):
            if len(refs) == 2:
                out[...] = refs[0][at] + refs[1][at]
            else:
                wide = len(refs) - 1
                first = 0 if at % 2 else slots * wide
                for block in range(first, first + out.shape[0]):
                    out[block - first] = refs[0][at // 2, block] + refs[1 + block % wide][at // 2, block // wide]

    def add_all(refs, outs):
        total = refs[0][...]
        for ref in refs[1:]:
            total = total + ref[...].reshape(total.shape)
        total = total.reshape(-1, rows, size)
        start = 0
        for out in outs:
            count = 1
            for length in out.shape[:-2]:
                count *= length
            out[...] = total[start:start + count].reshape(out.shape)
            start += count

    def landed_first(refs, outs):
        outs[0][...] = refs[0][...]

    widths = (across // 2, across - across // 2)
    starts = [sum(widths[:i]) for i in range(len(widths))]
    pieces, own_kept, own_arrived, arrived, kept = [], [], [], [], []

    fetch = [pltpu.SMEM(term_shift.shape, jnp.int32), pltpu.SemaphoreType.DMA((1,))]
    arguments = [
        pltpu.with_memory_space_constraint(value, pltpu.HBM)
        for value in (term_shift, wavefn, left_ops, right_ops)
    ]
    wide = widths[0]
    send, keep, left, right, lops, psi, rops = call(
        first_others,
        arguments,
        [HBM] * 4,
        [result(ny - 1, wide)] * 2 + [
            jax.ShapeDtypeStruct((slots, terms * others, 2 * size), bf16),
            jax.ShapeDtypeStruct((wide, terms, 2 * size, size), bf16),
            jax.ShapeDtypeStruct((terms, slots, share, size), f32),
            jax.ShapeDtypeStruct(wavefn.shape, f32),
            jax.ShapeDtypeStruct((terms, max(across - wide, 1), size, size), f32),
        ],
        [
            pltpu.SMEM(term_shift.shape, jnp.int32),
            pltpu.VMEM((terms, slots, others, size), f32),
            pltpu.VMEM((terms, wide, size, size), f32),
            *work(others),
            pltpu.SemaphoreType.DMA((5,)),
            pltpu.SemaphoreType.DMA((ny,)),
        ],
    )
    kept.append(keep)
    arrived.append(swap(send))
    send, keep, own = call(
        first_own,
        [arguments[0], lops, psi, right],
        [HBM] + [VMEM] * 3,
        [result(1, wide)] * 2 + [jax.ShapeDtypeStruct((slots, terms * share, 2 * size), bf16)],
        work(share) + fetch,
    )
    own_kept.append(keep)
    own_arrived.append(swap(send))
    pieces.append(sums(add_cores, [(blocks(wide), rows, size)] * (ny - 1), [kept[0], arrived[0]], keep))
    for start, wide in zip(starts[1:], widths[1:]):
        *send, keep, right = call(
            functools.partial(later_others, start, widths[0]),
            [arguments[0], left, psi, rops, pieces[-1][0]],
            [HBM] + [VMEM] * 3 + [ANY],
            [result(ny - 1, 1)] * wide + [
                result(ny - 1, wide), jax.ShapeDtypeStruct((wide, terms, 2 * size, size), bf16)
            ],
            work(others) + fetch,
        )
        arrived.append([swap(value) for value in send])
        kept.append(keep)
        send, keep = call(
            functools.partial(later_own, start),
            [arguments[0], own, psi, right, keep],
            [HBM] + [VMEM] * 3 + [ANY],
            [result(1, wide)] * 2,
            work(share) + fetch,
        )
        own_kept.append(keep)
        own_arrived.append(swap(send))
        groups = [(number * wide, rows, size) for number in (second, slots)]
        pieces.append(sums(add_cores, groups * (ny - 1), [kept[-1], *arrived[-1]], own_kept[-1]))

    def land(values):
        return [ahead(value, by) for by, value in enumerate(values, 1)]

    wide = widths[0]
    total = sums(add_all, [own_kept[0].shape], [own_kept[0], *land(pieces[0])], pieces[1][0])[0]
    value = sums(
        add_all, [(slots, wide, rows, size), (second, wide, rows, size)], [total, own_arrived[0]], None, ADD_COST
    )
    ready = value[1]
    value = [sectors(part, way) for way, part in enumerate(value)]
    arranged = [arrange(slots, *value)]

    wide = widths[1]
    total = sums(add_all, [(blocks(wide), rows, size)], [own_kept[1], own_arrived[1]], ready)[0]

    def add_group(refs, outs):
        block = refs[0][first:first + refs[1].shape[0]]
        for ref in refs[1:]:
            block = block + ref[...]
        outs[0][...] = block.reshape(outs[0].shape)

    value = []
    for way, number, first in ((1, second, slots * wide), (0, slots, 0)):
        came = land(pieces[1][1 - way::2])
        ready = sums(add_group, [(number, wide, rows, size)], [total, *came], ready)[0]
        value.append(sectors(ready, way))
    value[0] = sums(landed_first, [value[0].shape], [value[0]], arranged[0], LANDED_COST)[0]
    return settle(arranged, value[1], value[0])


def solution(mesh):
    placed = (
        P("lsec", "rsec", None, None),
        P("op", "lsec", None, None),
        P("op", "rsec", None, None),
        P("op"),
    )
    return jax.shard_map(
        shards, mesh=mesh, in_specs=placed, out_specs=P("lsec", "rsec", "op", None), check_vma=False
    )
```

```python
import functools

import jax
import jax.numpy as jnp
from jax import lax
from jax.experimental import pallas as pl
from jax.experimental.pallas import tpu as pltpu
from jax.sharding import PartitionSpec as P

CORES = 2
ARRANGE_COST = 1
ADD_COST = 2 * 10 ** 9
LANDED_COST = 6 * 10 ** 8
LIMIT = 32 * 1024 * 1024
NT = (((1,), (1,)), ((), ()))
PARAMS = pltpu.CompilerParams(vmem_limit_bytes=LIMIT)
HBM = pl.BlockSpec(memory_space=pltpu.HBM)
VMEM = pl.BlockSpec(memory_space=pltpu.VMEM)
ANY = pl.BlockSpec(memory_space=pl.ANY)


def split(value):
    high = value.astype(jnp.bfloat16)
    low = (value - high.astype(jnp.float32)).astype(jnp.bfloat16)
    return high, low


def choose_rows(lops, left, l):
    terms, _, many, _ = lops.shape
    for t in range(terms):
        left[l, t * many:(t + 1) * many, :] = jnp.concatenate(split(lops[t, l]), axis=1)


def lines(many, rows, slots, second):
    core = lax.rem(lax.axis_index("op"), CORES)
    return core * (rows // 8), (1 - core) * (rows // 8), skipped(slots, second) * (many // 8)


def products(left, psi, right, chosen, inner, total, send, keep, start, begins, lops=None, rops=None, ready=()):
    slots, height, twice = left.shape
    size = twice // 2
    wide, terms = right.shape[:2]
    many = height // terms
    chips, blocks, rows, _ = keep.shape
    second = blocks // wide - slots
    here, there, skip = begins

    def first(r, l):
        if r == 0 and lops is not None:
            choose_rows(lops, left, l)
        both = jnp.concatenate(split(psi[l, start + r]), axis=1)
        out = jnp.dot(left[l], jnp.concatenate([both, both], axis=0), preferred_element_type=jnp.float32)
        for t in range(terms):
            block = out[t * many:(t + 1) * many]
            parts = split(block[:, :size] + block[:, size:])
            inner[r, t, l * many:(l + 1) * many, :] = jnp.concatenate(parts, axis=1)

    def then(r, t):
        if rops is not None:
            right[r, t] = jnp.concatenate(split(rops[t, r]), axis=0)
        both = right[r, t]
        out = lax.dot_general(
            inner[r, t], jnp.concatenate([both, both], axis=1), NT, preferred_element_type=jnp.float32
        )
        out = (out[:, :size] + out[:, size:]).reshape(-1, 8, size)
        for way in range(2):
            mine = out * chosen[t, way]
            total[r, way] = mine if t == 0 else total[r, way] + mine

    def put(r):
        for chip in range(chips):
            for at in range(slots + second):
                way = 0 if at < slots else 1
                l = at if at < slots else at - slots
                for ref, begin in ((keep, here), (send, there)):
                    line = begin + (l * many + chip * CORES * rows) // 8 + (skip if way else 0)
                    block = total[r, way, pl.ds(line, rows // 8)].reshape(rows, size)
                    if isinstance(ref, (list, tuple)):
                        ref[r][chip, at] = block
                    else:
                        ref[chip, at * wide + r] = block

    for l in range(slots):
        first(0, l)
    for copy in ready:
        copy.wait()
    for r in range(wide):
        done = 0
        for t in range(terms):
            if r + 1 < wide and done < slots and t * slots >= done * terms:
                first(r + 1, done)
                done += 1
            then(r, t)
        for l in range(done, slots if r + 1 < wide else 0):
            first(r + 1, l)
        put(r)


def skipped(slots, second):
    return 0 if second == slots else 1 - lax.axis_index("lsec")


def first_others(shift, psi, lops, rops, send, keep, left, right, chosen, lops_own, psi_all, rops_rest, *refs):
    bits, lops_now, rops_now, inner, total, sems, lsems = refs
    terms, slots, size, _ = lops.shape
    wide = right.shape[0]
    ny = lax.axis_size("op") // CORES
    mine = lax.div(lax.axis_index("op"), CORES)
    share = size // ny

    def rows(ahead, target):
        at = pl.multiple_of(lax.rem(mine + ahead, ny) * share, share)
        return pltpu.make_async_copy(lops.at[:, :, pl.ds(at, share)], target, lsems.at[ahead])

    copies = [rows(ahead, lops_now.at[:, :, pl.ds((ahead - 1) * share, share)]) for ahead in range(1, ny)] + [
        pltpu.make_async_copy(psi.at[:, :wide], psi_all.at[:, :wide], sems.at[0]),
        pltpu.make_async_copy(shift, bits, sems.at[1]),
    ]
    ready = [pltpu.make_async_copy(rops.at[:, :wide], rops_now, sems.at[2])]
    later = [rows(0, lops_own)]
    if wide < rops.shape[1]:
        later += [
            pltpu.make_async_copy(psi.at[:, wide:], psi_all.at[:, wide:], sems.at[3]),
            pltpu.make_async_copy(rops.at[:, wide:], rops_rest, sems.at[4]),
        ]
    for copy in copies + ready:
        copy.start()
    second = keep.shape[1] // wide - slots
    begins = lines(lops_now.shape[2], keep.shape[2], slots, second)
    flip = lax.axis_index("lsec") if second < slots else 0
    for copy in copies:
        copy.wait()
    for copy in later:
        copy.start()
    for t in range(terms):
        kept = jnp.where(flip == 1, 1 - bits[t], bits[t]).astype(jnp.float32)
        chosen[t, 0] = jnp.full((8, size), kept, jnp.float32)
        chosen[t, 1] = jnp.full((8, size), 1.0 - kept, jnp.float32)
    products(
        left, psi_all, right, chosen, inner, total, send, keep, 0, begins, lops_now, rops_now, ready
    )
    for copy in later:
        copy.wait()


def find(left, keep, right):
    slots, height, _ = left.shape
    wide, terms = right.shape[:2]
    return lines(height // terms, keep.shape[2], slots, keep.shape[1] // wide - slots)


def first_own(lops, psi, right, chosen, send, keep, left, inner, total):
    products(left, psi, right, chosen, inner, total, send, keep, 0, find(left, keep, right), lops)


def later_others(start, skip, left, psi, rops, chosen, after, *refs):
    wide = refs[-3].shape[0]
    send, (keep, right, inner, total) = refs[:wide], refs[wide:]
    products(
        left, psi, right, chosen, inner, total, send, keep, start, find(left, keep, right),
        rops=rops.at[:, start - skip:],
    )


def later_own(start, left, psi, right, chosen, after, send, keep, inner, total):
    products(left, psi, right, chosen, inner, total, send, keep, start, find(left, keep, right))


def call(kernel, operands, in_specs, out_shape, scratch=(), flops=1):
    return pl.pallas_call(
        kernel,
        in_specs=in_specs,
        out_specs=[VMEM] * len(out_shape),
        out_shape=out_shape,
        scratch_shapes=scratch,
        compiler_params=PARAMS,
        cost_estimate=pl.CostEstimate(flops=flops, bytes_accessed=1024, transcendentals=0),
    )(*operands)


def sums(kernel, shapes, operands, after=None, flops=1):
    reads = len(operands)
    specs = [VMEM] * reads

    def body(*refs):
        kernel(refs[:reads], refs[len(specs):])

    if after is not None:
        operands = [*operands, after]
        specs.append(ANY)
    return call(body, operands, specs, [jax.ShapeDtypeStruct(shape, jnp.float32) for shape in shapes], (), flops)


def arrange(slots, first, second):
    wide, rows, size = first.shape[1:]
    more = second.shape[0]

    def kernel(refs, outs):
        way = 1 - lax.axis_index("lsec") if more < slots else 0
        skip = 1 - skipped(slots, more) if more < slots else 0
        for l in range(slots):
            outs[0][way, l] = refs[0][l]
        for j in range(more):
            outs[0][1 - way, j + skip] = refs[1][j]

    return sums(kernel, [(2, slots, wide, rows, size)], [first, second], None, ARRANGE_COST)[0]


def settle(arranged, first, second):
    slots = first.shape[0]
    rows, size = first.shape[2:]
    more = second.shape[0]
    widths = [value.shape[2] for value in arranged] + [first.shape[1]]
    across = sum(widths)
    n_left, n_right = lax.axis_size("lsec"), lax.axis_size("rsec")

    def kernel(*refs):
        out, every = refs[-2:]
        mine_l, mine_r = lax.axis_index("lsec"), lax.axis_index("rsec")
        first_l, last_l = (mine_l == 0).astype(jnp.int32), (mine_l == n_left - 1).astype(jnp.int32)
        first_r, last_r = (mine_r == 0).astype(jnp.int32), (mine_r == n_right - 1).astype(jnp.int32)
        steps = ((first_l, -last_r), (-last_l, first_r))
        start = 0
        for i, wide in enumerate(widths[:-1]):
            every[:, :, start:start + wide] = refs[i][...]
            start += wide
        way = 1 - mine_l if more < slots else 0
        skip = 1 - skipped(slots, more) if more < slots else 0
        a, b = refs[len(arranged):len(arranged) + 2]
        for l in range(slots):
            every[way, l, start:] = a[l]
        for j in range(more):
            every[1 - way, j + skip, start:] = b[j]
        for l in range(slots):
            for r in range(across):
                block = jnp.zeros((rows, size), jnp.float32)
                for side, (step_l, step_r) in enumerate(steps):
                    from_l, from_r = l - step_l, r - step_r
                    inside = (from_l >= 0) & (from_l < slots) & (from_r >= 0) & (from_r < across)
                    part = every[side, jnp.clip(from_l, 0, slots - 1), jnp.clip(from_r, 0, across - 1)]
                    block = block + jnp.where(inside, part, 0.0)
                out[l, r] = block

    operands = [*arranged, first, second]
    return call(
        kernel, operands, [VMEM] * len(operands),
        [jax.ShapeDtypeStruct((slots, across, rows, size), jnp.float32)],
        [pltpu.VMEM((2, slots, across, rows, size), jnp.float32)],
    )[0]


def shards(wavefn, left_ops, right_ops, term_shift):
    n_op, n_left, n_right = (lax.axis_size(axis) for axis in ("op", "lsec", "rsec"))
    across = wavefn.shape[1]
    terms, slots, size, _ = left_ops.shape
    ny = n_op // CORES
    share = size // ny
    others = (ny - 1) * share
    rows = size // n_op
    second = slots - 1 if n_left == 2 else slots
    f32, bf16 = jnp.float32, jnp.bfloat16

    def permute(value, target):
        def place(o, l, r):
            return (o % n_op * n_left + l % n_left) * n_right + r % n_right

        perm = [
            (place(o, l, r), place(*target(o, l, r)))
            for o in range(n_op) for l in range(n_left) for r in range(n_right)
        ]
        return lax.ppermute(value, ("op", "lsec", "rsec"), perm)

    def swap(value):
        return permute(value, lambda o, l, r: (o ^ 1, l, r))

    def ahead(value, by):
        return permute(value, lambda o, l, r: (o + CORES * by, l, r))

    def sectors(value, way):
        def target(o, l, r):
            up = way == (l if second < slots else 0)
            return (o, l + 1, r - 1) if up else (o, l - 1, r + 1)

        return permute(value, target)

    def blocks(wide):
        return (slots + second) * wide

    def result(chips, wide):
        return jax.ShapeDtypeStruct((chips, blocks(wide), rows, size), f32)

    def work(many):
        return [
            pltpu.VMEM((across // 2, terms, slots * many, 2 * size), bf16),
            pltpu.VMEM((across // 2, 2, slots * many // 8, 8, size), f32),
        ]

    def add_cores(refs, outs):
        for at, out in enumerate(outs):
            if len(refs) == 2:
                out[...] = refs[0][at] + refs[1][at]
            else:
                wide = len(refs) - 1
                first = 0 if at % 2 else slots * wide
                for block in range(first, first + out.shape[0]):
                    out[block - first] = refs[0][at // 2, block] + refs[1 + block % wide][at // 2, block // wide]

    def add_all(refs, outs):
        total = refs[0][...]
        for ref in refs[1:]:
            total = total + ref[...].reshape(total.shape)
        total = total.reshape(-1, rows, size)
        start = 0
        for out in outs:
            count = 1
            for length in out.shape[:-2]:
                count *= length
            out[...] = total[start:start + count].reshape(out.shape)
            start += count

    def landed_first(refs, outs):
        outs[0][...] = refs[0][...]

    widths = (across // 2, across - across // 2)
    starts = [sum(widths[:i]) for i in range(len(widths))]
    pieces, own_kept, own_arrived, arrived, kept = [], [], [], [], []

    arguments = (term_shift, wavefn, left_ops, right_ops)
    wide = widths[0]
    send, keep, left, right, chosen, lops, psi, rops = call(
        first_others,
        [pltpu.with_memory_space_constraint(value, pltpu.HBM) for value in arguments],
        [HBM] * 4,
        [result(ny - 1, wide)] * 2 + [
            jax.ShapeDtypeStruct((slots, terms * others, 2 * size), bf16),
            jax.ShapeDtypeStruct((wide, terms, 2 * size, size), bf16),
            jax.ShapeDtypeStruct((terms, 2, 8, size), f32),
            jax.ShapeDtypeStruct((terms, slots, share, size), f32),
            jax.ShapeDtypeStruct(wavefn.shape, f32),
            jax.ShapeDtypeStruct((terms, max(across - wide, 1), size, size), f32),
        ],
        [
            pltpu.SMEM(term_shift.shape, jnp.int32),
            pltpu.VMEM((terms, slots, others, size), f32),
            pltpu.VMEM((terms, wide, size, size), f32),
            *work(others),
            pltpu.SemaphoreType.DMA((5,)),
            pltpu.SemaphoreType.DMA((ny,)),
        ],
    )
    kept.append(keep)
    arrived.append(swap(send))
    send, keep, own = call(
        first_own,
        [lops, psi, right, chosen],
        [VMEM] * 4,
        [result(1, wide)] * 2 + [jax.ShapeDtypeStruct((slots, terms * share, 2 * size), bf16)],
        work(share),
    )
    own_kept.append(keep)
    own_arrived.append(swap(send))
    pieces.append(sums(add_cores, [(blocks(wide), rows, size)] * (ny - 1), [kept[0], arrived[0]], keep))
    for start, wide in zip(starts[1:], widths[1:]):
        *send, keep, right = call(
            functools.partial(later_others, start, widths[0]),
            [left, psi, rops, chosen, pieces[-1][0]],
            [VMEM] * 4 + [ANY],
            [result(ny - 1, 1)] * wide + [
                result(ny - 1, wide), jax.ShapeDtypeStruct((wide, terms, 2 * size, size), bf16)
            ],
            work(others),
        )
        arrived.append([swap(value) for value in send])
        kept.append(keep)
        send, keep = call(
            functools.partial(later_own, start),
            [own, psi, right, chosen, keep],
            [VMEM] * 4 + [ANY],
            [result(1, wide)] * 2,
            work(share),
        )
        own_kept.append(keep)
        own_arrived.append(swap(send))
        groups = [(number * wide, rows, size) for number in (second, slots)]
        pieces.append(sums(add_cores, groups * (ny - 1), [kept[-1], *arrived[-1]], own_kept[-1]))

    def land(values):
        return [ahead(value, by) for by, value in enumerate(values, 1)]

    wide = widths[0]
    total = sums(add_all, [own_kept[0].shape], [own_kept[0], *land(pieces[0])], pieces[1][0])[0]
    value = sums(
        add_all, [(slots, wide, rows, size), (second, wide, rows, size)], [total, own_arrived[0]], None, ADD_COST
    )
    ready = value[1]
    value = [sectors(part, way) for way, part in enumerate(value)]
    value[1] = sums(landed_first, [value[1].shape], [value[1]], None, LANDED_COST)[0]
    arranged = [arrange(slots, *value)]

    wide = widths[1]
    total = sums(add_all, [(blocks(wide), rows, size)], [own_kept[1], own_arrived[1]], ready)[0]

    def add_group(refs, outs):
        block = refs[0][first:first + refs[1].shape[0]]
        for ref in refs[1:]:
            block = block + ref[...]
        outs[0][...] = block.reshape(outs[0].shape)

    value = []
    for way, number, first in ((1, second, slots * wide), (0, slots, 0)):
        came = land(pieces[1][1 - way::2])
        ready = sums(add_group, [(number, wide, rows, size)], [total, *came], ready)[0]
        value.append(sectors(ready, way))
    value[0] = sums(landed_first, [value[0].shape], [value[0]], arranged[0], LANDED_COST)[0]
    return settle(arranged, value[1], value[0])


def solution(mesh):
    placed = (
        P("lsec", "rsec", None, None),
        P("op", "lsec", None, None),
        P("op", "rsec", None, None),
        P("op"),
    )
    return jax.shard_map(
        shards, mesh=mesh, in_specs=placed, out_specs=P("lsec", "rsec", "op", None), check_vma=False
    )
```

```python
import functools

import jax
import jax.numpy as jnp
from jax import lax
from jax.experimental import pallas as pl
from jax.experimental.pallas import tpu as pltpu
from jax.sharding import PartitionSpec as P

CORES = 2
ARRANGE_COST = 1
ADD_COST = 2 * 10 ** 9
LANDED_COST = 6 * 10 ** 8
LIMIT = 32 * 1024 * 1024
NT = (((1,), (1,)), ((), ()))
PARAMS = pltpu.CompilerParams(vmem_limit_bytes=LIMIT)
HBM = pl.BlockSpec(memory_space=pltpu.HBM)
VMEM = pl.BlockSpec(memory_space=pltpu.VMEM)
ANY = pl.BlockSpec(memory_space=pl.ANY)


def split(value):
    high = value.astype(jnp.bfloat16)
    low = (value - high.astype(jnp.float32)).astype(jnp.bfloat16)
    return high, low


def choose_rows(lops, left, l):
    terms, _, many, _ = lops.shape
    for t in range(terms):
        left[l, t * many:(t + 1) * many, :] = jnp.concatenate(split(lops[t, l]), axis=1)


def lines(many, rows, slots, second):
    core = lax.rem(lax.axis_index("op"), CORES)
    return core * (rows // 8), (1 - core) * (rows // 8), skipped(slots, second) * (many // 8)


def products(left, psi, right, chosen, inner, total, send, keep, start, begins, lops=None, rops=None, ready=()):
    slots, height, twice = left.shape
    size = twice // 2
    wide, terms = right.shape[:2]
    many = height // terms
    chips, blocks, rows, _ = keep.shape
    second = blocks // wide - slots
    here, there, skip = begins
    for r in range(wide):
        for l in range(slots):
            if r == 0 and lops is not None:
                choose_rows(lops, left, l)
            both = jnp.concatenate(split(psi[l, start + r]), axis=1)
            out = jnp.dot(left[l], jnp.concatenate([both, both], axis=0), preferred_element_type=jnp.float32)
            for t in range(terms):
                block = out[t * many:(t + 1) * many]
                parts = split(block[:, :size] + block[:, size:])
                inner[t, l * many:(l + 1) * many, :] = jnp.concatenate(parts, axis=1)
        if r == 0:
            for copy in ready:
                copy.wait()
        for t in range(terms):
            if rops is not None:
                right[r, t] = jnp.concatenate(split(rops[t, r]), axis=0)
            both = right[r, t]
            out = lax.dot_general(
                inner[t], jnp.concatenate([both, both], axis=1), NT, preferred_element_type=jnp.float32
            )
            out = (out[:, :size] + out[:, size:]).reshape(-1, 8, size)
            for way in range(2):
                mine = out * chosen[t, way]
                total[way] = mine if t == 0 else total[way] + mine
        for chip in range(chips):
            for at in range(slots + second):
                way = 0 if at < slots else 1
                l = at if at < slots else at - slots
                for ref, begin in ((keep, here), (send, there)):
                    line = begin + (l * many + chip * CORES * rows) // 8 + (skip if way else 0)
                    block = total[way, pl.ds(line, rows // 8)].reshape(rows, size)
                    if isinstance(ref, (list, tuple)):
                        ref[r][chip, at] = block
                    else:
                        ref[chip, at * wide + r] = block


def skipped(slots, second):
    return 0 if second == slots else 1 - lax.axis_index("lsec")


def first_others(shift, psi, lops, rops, send, keep, left, right, chosen, lops_own, psi_all, rops_rest, *refs):
    bits, lops_now, rops_now, inner, total, sems, lsems = refs
    terms, slots, size, _ = lops.shape
    wide = right.shape[0]
    ny = lax.axis_size("op") // CORES
    mine = lax.div(lax.axis_index("op"), CORES)
    share = size // ny

    def rows(ahead, target, low, high):
        at = pl.multiple_of(lax.rem(mine + ahead, ny) * share, share)
        return pltpu.make_async_copy(lops.at[low:high, :, pl.ds(at, share)], target, lsems.at[ahead, low])

    half = terms // 2
    copies = [
        rows(ahead, lops_now.at[low:high, :, pl.ds((ahead - 1) * share, share)], low, high)
        for ahead in range(1, ny) for low, high in ((0, half), (half, terms))
    ] + [
        pltpu.make_async_copy(psi.at[:slots // 2, :wide], psi_all.at[:slots // 2, :wide], sems.at[0]),
        pltpu.make_async_copy(psi.at[slots // 2:, :wide], psi_all.at[slots // 2:, :wide], sems.at[5]),
        pltpu.make_async_copy(shift, bits, sems.at[1]),
    ]
    ready = [pltpu.make_async_copy(rops.at[:, :wide], rops_now, sems.at[2])]
    later = [rows(0, lops_own, 0, terms)]
    if wide < rops.shape[1]:
        later += [
            pltpu.make_async_copy(psi.at[:, wide:], psi_all.at[:, wide:], sems.at[3]),
            pltpu.make_async_copy(rops.at[:, wide:], rops_rest, sems.at[4]),
        ]
    for copy in copies + ready:
        copy.start()
    second = keep.shape[1] // wide - slots
    begins = lines(lops_now.shape[2], keep.shape[2], slots, second)
    flip = lax.axis_index("lsec") if second < slots else 0
    for copy in copies:
        copy.wait()
    for copy in later:
        copy.start()
    for t in range(terms):
        kept = jnp.where(flip == 1, 1 - bits[t], bits[t]).astype(jnp.float32)
        chosen[t, 0] = jnp.full((8, size), kept, jnp.float32)
        chosen[t, 1] = jnp.full((8, size), 1.0 - kept, jnp.float32)
    products(
        left, psi_all, right, chosen, inner, total, send, keep, 0, begins, lops_now, rops_now, ready
    )
    for copy in later:
        copy.wait()


def find(left, keep, right):
    slots, height, _ = left.shape
    wide, terms = right.shape[:2]
    return lines(height // terms, keep.shape[2], slots, keep.shape[1] // wide - slots)


def first_own(lops, psi, right, chosen, send, keep, left, inner, total):
    products(left, psi, right, chosen, inner, total, send, keep, 0, find(left, keep, right), lops)


def later_others(start, skip, left, psi, rops, chosen, after, *refs):
    wide = refs[-3].shape[0]
    send, (keep, right, inner, total) = refs[:wide], refs[wide:]
    products(
        left, psi, right, chosen, inner, total, send, keep, start, find(left, keep, right),
        rops=rops.at[:, start - skip:],
    )


def later_own(start, left, psi, right, chosen, after, send, keep, inner, total):
    products(left, psi, right, chosen, inner, total, send, keep, start, find(left, keep, right))


def call(kernel, operands, in_specs, out_shape, scratch=(), flops=1):
    return pl.pallas_call(
        kernel,
        in_specs=in_specs,
        out_specs=[VMEM] * len(out_shape),
        out_shape=out_shape,
        scratch_shapes=scratch,
        compiler_params=PARAMS,
        cost_estimate=pl.CostEstimate(flops=flops, bytes_accessed=1024, transcendentals=0),
    )(*operands)


def sums(kernel, shapes, operands, after=None, flops=1):
    reads = len(operands)
    specs = [VMEM] * reads

    def body(*refs):
        kernel(refs[:reads], refs[len(specs):])

    if after is not None:
        operands = [*operands, after]
        specs.append(ANY)
    return call(body, operands, specs, [jax.ShapeDtypeStruct(shape, jnp.float32) for shape in shapes], (), flops)


def arrange(slots, first, second):
    wide, rows, size = first.shape[1:]
    more = second.shape[0]

    def kernel(refs, outs):
        way = 1 - lax.axis_index("lsec") if more < slots else 0
        skip = 1 - skipped(slots, more) if more < slots else 0
        for l in range(slots):
            outs[0][way, l] = refs[0][l]
        for j in range(more):
            outs[0][1 - way, j + skip] = refs[1][j]

    return sums(kernel, [(2, slots, wide, rows, size)], [first, second], None, ARRANGE_COST)[0]


def settle(arranged, first, second):
    slots = first.shape[0]
    rows, size = first.shape[2:]
    more = second.shape[0]
    widths = [value.shape[2] for value in arranged] + [first.shape[1]]
    across = sum(widths)
    n_left, n_right = lax.axis_size("lsec"), lax.axis_size("rsec")

    def kernel(*refs):
        out, every = refs[-2:]
        mine_l, mine_r = lax.axis_index("lsec"), lax.axis_index("rsec")
        first_l, last_l = (mine_l == 0).astype(jnp.int32), (mine_l == n_left - 1).astype(jnp.int32)
        first_r, last_r = (mine_r == 0).astype(jnp.int32), (mine_r == n_right - 1).astype(jnp.int32)
        steps = ((first_l, -last_r), (-last_l, first_r))
        start = 0
        for i, wide in enumerate(widths[:-1]):
            every[:, :, start:start + wide] = refs[i][...]
            start += wide
        way = 1 - mine_l if more < slots else 0
        skip = 1 - skipped(slots, more) if more < slots else 0
        a, b = refs[len(arranged):len(arranged) + 2]
        for l in range(slots):
            every[way, l, start:] = a[l]
        for j in range(more):
            every[1 - way, j + skip, start:] = b[j]
        places = []
        for step_l, step_r in steps:
            froms = [[at - step for at in range(count)] for step, count in ((step_l, slots), (step_r, across))]
            places.append([
                [((at >= 0) & (at < count), jnp.clip(at, 0, count - 1)) for at in several]
                for several, count in zip(froms, (slots, across))
            ])
        for l in range(slots):
            for r in range(across):
                block = jnp.zeros((rows, size), jnp.float32)
                for side, (lefts, rights) in enumerate(places):
                    (ok_l, from_l), (ok_r, from_r) = lefts[l], rights[r]
                    block = block + jnp.where(ok_l & ok_r, every[side, from_l, from_r], 0.0)
                out[l, r] = block

    operands = [*arranged, first, second]
    return call(
        kernel, operands, [VMEM] * len(operands),
        [jax.ShapeDtypeStruct((slots, across, rows, size), jnp.float32)],
        [pltpu.VMEM((2, slots, across, rows, size), jnp.float32)],
    )[0]


def shards(wavefn, left_ops, right_ops, term_shift):
    n_op, n_left, n_right = (lax.axis_size(axis) for axis in ("op", "lsec", "rsec"))
    across = wavefn.shape[1]
    terms, slots, size, _ = left_ops.shape
    ny = n_op // CORES
    share = size // ny
    others = (ny - 1) * share
    rows = size // n_op
    second = slots - 1 if n_left == 2 else slots
    f32, bf16 = jnp.float32, jnp.bfloat16

    def permute(value, target):
        def place(o, l, r):
            return (o % n_op * n_left + l % n_left) * n_right + r % n_right

        perm = [
            (place(o, l, r), place(*target(o, l, r)))
            for o in range(n_op) for l in range(n_left) for r in range(n_right)
        ]
        return lax.ppermute(value, ("op", "lsec", "rsec"), perm)

    def swap(value):
        return permute(value, lambda o, l, r: (o ^ 1, l, r))

    def ahead(value, by):
        return permute(value, lambda o, l, r: (o + CORES * by, l, r))

    def sectors(value, way):
        def target(o, l, r):
            up = way == (l if second < slots else 0)
            return (o, l + 1, r - 1) if up else (o, l - 1, r + 1)

        return permute(value, target)

    def blocks(wide):
        return (slots + second) * wide

    def result(chips, wide):
        return jax.ShapeDtypeStruct((chips, blocks(wide), rows, size), f32)

    def work(many):
        return [
            pltpu.VMEM((terms, slots * many, 2 * size), bf16),
            pltpu.VMEM((2, slots * many // 8, 8, size), f32),
        ]

    def add_cores(refs, outs):
        for at, out in enumerate(outs):
            if len(refs) == 2:
                out[...] = refs[0][at] + refs[1][at]
            else:
                wide = len(refs) - 1
                first = 0 if at % 2 else slots * wide
                for block in range(first, first + out.shape[0]):
                    out[block - first] = refs[0][at // 2, block] + refs[1 + block % wide][at // 2, block // wide]

    def add_all(refs, outs):
        total = refs[0][...]
        for ref in refs[1:]:
            total = total + ref[...].reshape(total.shape)
        total = total.reshape(-1, rows, size)
        start = 0
        for out in outs:
            count = 1
            for length in out.shape[:-2]:
                count *= length
            out[...] = total[start:start + count].reshape(out.shape)
            start += count

    def landed_first(refs, outs):
        outs[0][...] = refs[0][...]

    widths = (across // 2, across - across // 2)
    starts = [sum(widths[:i]) for i in range(len(widths))]
    pieces, own_kept, own_arrived, arrived, kept = [], [], [], [], []

    arguments = (term_shift, wavefn, left_ops, right_ops)
    wide = widths[0]
    send, keep, left, right, chosen, lops, psi, rops = call(
        first_others,
        [pltpu.with_memory_space_constraint(value, pltpu.HBM) for value in arguments],
        [HBM] * 4,
        [result(ny - 1, wide)] * 2 + [
            jax.ShapeDtypeStruct((slots, terms * others, 2 * size), bf16),
            jax.ShapeDtypeStruct((wide, terms, 2 * size, size), bf16),
            jax.ShapeDtypeStruct((terms, 2, 8, size), f32),
            jax.ShapeDtypeStruct((terms, slots, share, size), f32),
            jax.ShapeDtypeStruct(wavefn.shape, f32),
            jax.ShapeDtypeStruct((terms, max(across - wide, 1), size, size), f32),
        ],
        [
            pltpu.SMEM(term_shift.shape, jnp.int32),
            pltpu.VMEM((terms, slots, others, size), f32),
            pltpu.VMEM((terms, wide, size, size), f32),
            *work(others),
            pltpu.SemaphoreType.DMA((6,)),
            pltpu.SemaphoreType.DMA((ny, terms)),
        ],
    )
    kept.append(keep)
    arrived.append(swap(send))
    send, keep, own = call(
        first_own,
        [lops, psi, right, chosen],
        [VMEM] * 4,
        [result(1, wide)] * 2 + [jax.ShapeDtypeStruct((slots, terms * share, 2 * size), bf16)],
        work(share),
    )
    own_kept.append(keep)
    own_arrived.append(swap(send))
    pieces.append(sums(add_cores, [(blocks(wide), rows, size)] * (ny - 1), [kept[0], arrived[0]], keep))
    for start, wide in zip(starts[1:], widths[1:]):
        *send, keep, right = call(
            functools.partial(later_others, start, widths[0]),
            [left, psi, rops, chosen, pieces[-1][0]],
            [VMEM] * 4 + [ANY],
            [result(ny - 1, 1)] * wide + [
                result(ny - 1, wide), jax.ShapeDtypeStruct((wide, terms, 2 * size, size), bf16)
            ],
            work(others),
        )
        arrived.append([swap(value) for value in send])
        kept.append(keep)
        send, keep = call(
            functools.partial(later_own, start),
            [own, psi, right, chosen, keep],
            [VMEM] * 4 + [ANY],
            [result(1, wide)] * 2,
            work(share),
        )
        own_kept.append(keep)
        own_arrived.append(swap(send))
        groups = [(number * wide, rows, size) for number in (second, slots)]
        pieces.append(sums(add_cores, groups * (ny - 1), [kept[-1], *arrived[-1]], own_kept[-1]))

    def land(values):
        return [ahead(value, by) for by, value in enumerate(values, 1)]

    wide = widths[0]
    total = sums(add_all, [own_kept[0].shape], [own_kept[0], *land(pieces[0])], pieces[1][0])[0]
    value = sums(
        add_all, [(slots, wide, rows, size), (second, wide, rows, size)], [total, own_arrived[0]], None, ADD_COST
    )
    ready = value[1]
    value = [sectors(part, way) for way, part in enumerate(value)]
    value[1] = sums(landed_first, [value[1].shape], [value[1]], None, LANDED_COST)[0]
    arranged = [arrange(slots, *value)]

    wide = widths[1]
    total = sums(add_all, [(blocks(wide), rows, size)], [own_kept[1], own_arrived[1]], ready)[0]

    def add_group(refs, outs):
        block = refs[0][first:first + refs[1].shape[0]]
        for ref in refs[1:]:
            block = block + ref[...]
        outs[0][...] = block.reshape(outs[0].shape)

    value = []
    for way, number, first in ((1, second, slots * wide), (0, slots, 0)):
        came = land(pieces[1][1 - way::2])
        ready = sums(add_group, [(number, wide, rows, size)], [total, *came], ready)[0]
        value.append(sectors(ready, way))
    value[0] = sums(landed_first, [value[0].shape], [value[0]], arranged[0], LANDED_COST)[0]
    return settle(arranged, value[1], value[0])


def solution(mesh):
    placed = (
        P("lsec", "rsec", None, None),
        P("op", "lsec", None, None),
        P("op", "rsec", None, None),
        P("op"),
    )
    return jax.shard_map(
        shards, mesh=mesh, in_specs=placed, out_specs=P("lsec", "rsec", "op", None), check_vma=False
    )
```

```python
import functools

import jax
import jax.numpy as jnp
from jax import lax
from jax.experimental import pallas as pl
from jax.experimental.pallas import tpu as pltpu
from jax.sharding import PartitionSpec as P

CORES = 2
ARRANGE_COST = 1
ADD_COST = 2 * 10 ** 9
LANDED_COST = 6 * 10 ** 8
LIMIT = 32 * 1024 * 1024
NT = (((1,), (1,)), ((), ()))
PARAMS = pltpu.CompilerParams(vmem_limit_bytes=LIMIT)
HBM = pl.BlockSpec(memory_space=pltpu.HBM)
VMEM = pl.BlockSpec(memory_space=pltpu.VMEM)
ANY = pl.BlockSpec(memory_space=pl.ANY)


def split(value):
    high = value.astype(jnp.bfloat16)
    low = (value - high.astype(jnp.float32)).astype(jnp.bfloat16)
    return high, low


def choose_rows(lops, left, l):
    terms, _, many, _ = lops.shape
    for t in range(terms):
        left[l, t * many:(t + 1) * many, :] = jnp.concatenate(split(lops[t, l]), axis=1)


def lines(many, rows, slots, second):
    core = lax.rem(lax.axis_index("op"), CORES)
    return core * (rows // 8), (1 - core) * (rows // 8), skipped(slots, second) * (many // 8)


def products(left, psi, right, chosen, inner, total, send, keep, start, begins, lops=None, rops=None, ready=()):
    slots, height, twice = left.shape
    size = twice // 2
    wide, terms = right.shape[:2]
    many = height // terms
    chips, blocks, rows, _ = keep.shape
    second = blocks // wide - slots
    here, there, skip = begins
    for r in range(wide):
        for l in range(slots):
            if r == 0 and lops is not None:
                choose_rows(lops, left, l)
            both = jnp.concatenate(split(psi[l, start + r]), axis=1)
            out = jnp.dot(left[l], jnp.concatenate([both, both], axis=0), preferred_element_type=jnp.float32)
            for t in range(terms):
                block = out[t * many:(t + 1) * many]
                parts = split(block[:, :size] + block[:, size:])
                inner[t, l * many:(l + 1) * many, :] = jnp.concatenate(parts, axis=1)
        if r == 0:
            for copy in ready:
                copy.wait()
        for t in range(terms):
            if rops is not None:
                right[r, t] = jnp.concatenate(split(rops[t, r]), axis=0)
            both = right[r, t]
            out = lax.dot_general(
                inner[t], jnp.concatenate([both, both], axis=1), NT, preferred_element_type=jnp.float32
            )
            out = (out[:, :size] + out[:, size:]).reshape(-1, 8, size)
            for way in range(2):
                mine = out * chosen[t, way]
                total[way] = mine if t == 0 else total[way] + mine
        for chip in range(chips):
            for at in range(slots + second):
                way = 0 if at < slots else 1
                l = at if at < slots else at - slots
                for ref, begin in ((keep, here), (send, there)):
                    line = begin + (l * many + chip * CORES * rows) // 8 + (skip if way else 0)
                    block = total[way, pl.ds(line, rows // 8)].reshape(rows, size)
                    if isinstance(ref, (list, tuple)):
                        ref[r][chip, at] = block
                    else:
                        ref[chip, at * wide + r] = block


def skipped(slots, second):
    return 0 if second == slots else 1 - lax.axis_index("lsec")


def first_others(shift, psi, lops, rops, send, keep, left, right, chosen, lops_own, psi_all, rops_rest, *refs):
    bits, lops_now, rops_now, inner, total, sems, lsems = refs
    terms, slots, size, _ = lops.shape
    wide = right.shape[0]
    ny = lax.axis_size("op") // CORES
    mine = lax.div(lax.axis_index("op"), CORES)
    share = size // ny

    def rows(ahead, target):
        at = pl.multiple_of(lax.rem(mine + ahead, ny) * share, share)
        return pltpu.make_async_copy(lops.at[:, :, pl.ds(at, share)], target, lsems.at[ahead])

    copies = [rows(ahead, lops_now.at[:, :, pl.ds((ahead - 1) * share, share)]) for ahead in range(1, ny)] + [
        pltpu.make_async_copy(psi.at[:, :wide], psi_all.at[:, :wide], sems.at[0]),
        pltpu.make_async_copy(shift, bits, sems.at[1]),
    ]
    ready = [pltpu.make_async_copy(rops.at[:, :wide], rops_now, sems.at[2])]
    later = [rows(0, lops_own)]
    if wide < rops.shape[1]:
        later += [
            pltpu.make_async_copy(psi.at[:, wide:], psi_all.at[:, wide:], sems.at[3]),
            pltpu.make_async_copy(rops.at[:, wide:], rops_rest, sems.at[4]),
        ]
    for copy in copies + ready:
        copy.start()
    second = keep.shape[1] // wide - slots
    begins = lines(lops_now.shape[2], keep.shape[2], slots, second)
    flip = lax.axis_index("lsec") if second < slots else 0
    for copy in copies:
        copy.wait()
    for copy in later:
        copy.start()
    for t in range(terms):
        kept = jnp.where(flip == 1, 1 - bits[t], bits[t]).astype(jnp.float32)
        chosen[t, 0] = jnp.full((8, size), kept, jnp.float32)
        chosen[t, 1] = jnp.full((8, size), 1.0 - kept, jnp.float32)
    products(
        left, psi_all, right, chosen, inner, total, send, keep, 0, begins, lops_now, rops_now, ready
    )
    for copy in later:
        copy.wait()


def find(left, keep, right):
    slots, height, _ = left.shape
    wide, terms = right.shape[:2]
    return lines(height // terms, keep.shape[2], slots, keep.shape[1] // wide - slots)


def first_own(lops, psi, right, chosen, send, keep, left, inner, total):
    products(left, psi, right, chosen, inner, total, send, keep, 0, find(left, keep, right), lops)


def later_others(start, skip, left, psi, rops, chosen, after, *refs):
    wide = refs[-3].shape[0]
    send, (keep, right, inner, total) = refs[:wide], refs[wide:]
    products(
        left, psi, right, chosen, inner, total, send, keep, start, find(left, keep, right),
        rops=rops.at[:, start - skip:],
    )


def later_own(start, left, psi, right, chosen, after, send, keep, inner, total):
    products(left, psi, right, chosen, inner, total, send, keep, start, find(left, keep, right))


def call(kernel, operands, in_specs, out_shape, scratch=(), flops=1):
    return pl.pallas_call(
        kernel,
        in_specs=in_specs,
        out_specs=[VMEM] * len(out_shape),
        out_shape=out_shape,
        scratch_shapes=scratch,
        compiler_params=PARAMS,
        cost_estimate=pl.CostEstimate(flops=flops, bytes_accessed=1024, transcendentals=0),
    )(*operands)


def sums(kernel, shapes, operands, after=None, flops=1):
    reads = len(operands)
    specs = [VMEM] * reads

    def body(*refs):
        kernel(refs[:reads], refs[len(specs):])

    if after is not None:
        operands = [*operands, after]
        specs.append(ANY)
    return call(body, operands, specs, [jax.ShapeDtypeStruct(shape, jnp.float32) for shape in shapes], (), flops)


def arrange(slots, first, second):
    wide, rows, size = first.shape[1:]
    more = second.shape[0]

    def kernel(refs, outs):
        way = 1 - lax.axis_index("lsec") if more < slots else 0
        skip = 1 - skipped(slots, more) if more < slots else 0
        for l in range(slots):
            outs[0][way, l] = refs[0][l]
        for j in range(more):
            outs[0][1 - way, j + skip] = refs[1][j]

    return sums(kernel, [(2, slots, wide, rows, size)], [first, second], None, ARRANGE_COST)[0]


def settle(arranged, first, second):
    slots = first.shape[0]
    rows, size = first.shape[2:]
    more = second.shape[0]
    widths = [value.shape[2] for value in arranged] + [first.shape[1]]
    across = sum(widths)
    n_left, n_right = lax.axis_size("lsec"), lax.axis_size("rsec")

    def kernel(*refs):
        out, every = refs[-2:]
        mine_l, mine_r = lax.axis_index("lsec"), lax.axis_index("rsec")
        first_l, last_l = (mine_l == 0).astype(jnp.int32), (mine_l == n_left - 1).astype(jnp.int32)
        first_r, last_r = (mine_r == 0).astype(jnp.int32), (mine_r == n_right - 1).astype(jnp.int32)
        steps = ((first_l, -last_r), (-last_l, first_r))
        start = 0
        for i, wide in enumerate(widths[:-1]):
            every[:, :, start:start + wide] = refs[i][...]
            start += wide
        way = 1 - mine_l if more < slots else 0
        skip = 1 - skipped(slots, more) if more < slots else 0
        a, b = refs[len(arranged):len(arranged) + 2]
        for l in range(slots):
            every[way, l, start:] = a[l]
        for j in range(more):
            every[1 - way, j + skip, start:] = b[j]
        for l in range(slots):
            for r in range(across):
                block = jnp.zeros((rows, size), jnp.float32)
                for side, (step_l, step_r) in enumerate(steps):
                    from_l, from_r = l - step_l, r - step_r
                    inside = (from_l >= 0) & (from_l < slots) & (from_r >= 0) & (from_r < across)
                    part = every[side, jnp.clip(from_l, 0, slots - 1), jnp.clip(from_r, 0, across - 1)]
                    block = block + jnp.where(inside, part, 0.0)
                out[l, r] = block

    operands = [*arranged, first, second]
    return call(
        kernel, operands, [VMEM] * len(operands),
        [jax.ShapeDtypeStruct((slots, across, rows, size), jnp.float32)],
        [pltpu.VMEM((2, slots, across, rows, size), jnp.float32)],
    )[0]


def shards(wavefn, left_ops, right_ops, term_shift):
    n_op, n_left, n_right = (lax.axis_size(axis) for axis in ("op", "lsec", "rsec"))
    across = wavefn.shape[1]
    terms, slots, size, _ = left_ops.shape
    ny = n_op // CORES
    share = size // ny
    others = (ny - 1) * share
    rows = size // n_op
    second = slots - 1 if n_left == 2 else slots
    f32, bf16 = jnp.float32, jnp.bfloat16

    def permute(value, target):
        def place(o, l, r):
            return (o % n_op * n_left + l % n_left) * n_right + r % n_right

        perm = [
            (place(o, l, r), place(*target(o, l, r)))
            for o in range(n_op) for l in range(n_left) for r in range(n_right)
        ]
        return lax.ppermute(value, ("op", "lsec", "rsec"), perm)

    def swap(value):
        return permute(value, lambda o, l, r: (o ^ 1, l, r))

    def ahead(value, by):
        return permute(value, lambda o, l, r: (o + CORES * by, l, r))

    def sectors(value, way):
        def target(o, l, r):
            up = way == (l if second < slots else 0)
            return (o, l + 1, r - 1) if up else (o, l - 1, r + 1)

        return permute(value, target)

    def blocks(wide):
        return (slots + second) * wide

    def result(chips, wide):
        return jax.ShapeDtypeStruct((chips, blocks(wide), rows, size), f32)

    def work(many):
        return [
            pltpu.VMEM((terms, slots * many, 2 * size), bf16),
            pltpu.VMEM((2, slots * many // 8, 8, size), f32),
        ]

    def add_cores(refs, outs):
        for at, out in enumerate(outs):
            if len(refs) == 2:
                out[...] = refs[0][at] + refs[1][at]
            else:
                wide = len(refs) - 1
                first = 0 if at % 2 else slots * wide
                for block in range(first, first + out.shape[0]):
                    out[block - first] = refs[0][at // 2, block] + refs[1 + block % wide][at // 2, block // wide]

    def add_all(refs, outs):
        total = refs[0][...]
        for ref in refs[1:]:
            total = total + ref[...].reshape(total.shape)
        total = total.reshape(-1, rows, size)
        start = 0
        for out in outs:
            count = 1
            for length in out.shape[:-2]:
                count *= length
            out[...] = total[start:start + count].reshape(out.shape)
            start += count

    def landed_first(refs, outs):
        outs[0][...] = refs[0][...]

    widths = (across // 2, across - across // 2)
    starts = [sum(widths[:i]) for i in range(len(widths))]
    pieces, own_kept, own_arrived, arrived, kept = [], [], [], [], []

    arguments = (term_shift, wavefn, left_ops, right_ops)
    wide = widths[0]
    send, keep, left, right, chosen, lops, psi, rops = call(
        first_others,
        [pltpu.with_memory_space_constraint(value, pltpu.HBM) for value in arguments],
        [HBM] * 4,
        [result(ny - 1, wide)] * 2 + [
            jax.ShapeDtypeStruct((slots, terms * others, 2 * size), bf16),
            jax.ShapeDtypeStruct((wide, terms, 2 * size, size), bf16),
            jax.ShapeDtypeStruct((terms, 2, 8, size), f32),
            jax.ShapeDtypeStruct((terms, slots, share, size), f32),
            jax.ShapeDtypeStruct(wavefn.shape, f32),
            jax.ShapeDtypeStruct((terms, max(across - wide, 1), size, size), f32),
        ],
        [
            pltpu.SMEM(term_shift.shape, jnp.int32),
            pltpu.VMEM((terms, slots, others, size), f32),
            pltpu.VMEM((terms, wide, size, size), f32),
            *work(others),
            pltpu.SemaphoreType.DMA((5,)),
            pltpu.SemaphoreType.DMA((ny,)),
        ],
    )
    kept.append(keep)
    arrived.append(swap(send))
    send, keep, own = call(
        first_own,
        [lops, psi, right, chosen],
        [VMEM] * 4,
        [result(1, wide)] * 2 + [jax.ShapeDtypeStruct((slots, terms * share, 2 * size), bf16)],
        work(share),
    )
    own_kept.append(keep)
    own_arrived.append(swap(send))
    pieces.append(sums(add_cores, [(blocks(wide), rows, size)] * (ny - 1), [kept[0], arrived[0]], keep))
    for start, wide in zip(starts[1:], widths[1:]):
        *send, keep, right = call(
            functools.partial(later_others, start, widths[0]),
            [left, psi, rops, chosen, pieces[-1][0]],
            [VMEM] * 4 + [ANY],
            [result(ny - 1, 1)] * wide + [
                result(ny - 1, wide), jax.ShapeDtypeStruct((wide, terms, 2 * size, size), bf16)
            ],
            work(others),
        )
        arrived.append([swap(value) for value in send])
        kept.append(keep)
        send, keep = call(
            functools.partial(later_own, start),
            [own, psi, right, chosen, keep],
            [VMEM] * 4 + [ANY],
            [result(1, wide)] * 2,
            work(share),
        )
        own_kept.append(keep)
        own_arrived.append(swap(send))
        groups = [(number * wide, rows, size) for number in (second, slots)]
        pieces.append(sums(add_cores, groups * (ny - 1), [kept[-1], *arrived[-1]], own_kept[-1]))

    def land(values):
        return [ahead(value, by) for by, value in enumerate(values, 1)]

    wide = widths[0]
    total = sums(add_all, [own_kept[0].shape], [own_kept[0], *land(pieces[0])], pieces[1][0])[0]
    value = sums(
        add_all, [(slots, wide, rows, size), (second, wide, rows, size)], [total, own_arrived[0]], None, ADD_COST
    )
    ready = value[1]
    value = [sectors(part, way) for way, part in enumerate(value)]
    arranged = [arrange(slots, *value)]

    wide = widths[1]
    total = sums(add_all, [(blocks(wide), rows, size)], [own_kept[1], own_arrived[1]], ready)[0]

    def add_group(refs, outs):
        block = refs[0][first:first + refs[1].shape[0]]
        for ref in refs[1:]:
            block = block + ref[...]
        outs[0][...] = block.reshape(outs[0].shape)

    value = []
    for way, number, first in ((1, second, slots * wide), (0, slots, 0)):
        came = land(pieces[1][1 - way::2])
        ready = sums(add_group, [(number, wide, rows, size)], [total, *came], ready)[0]
        value.append(sectors(ready, way))
    value[0] = sums(landed_first, [value[0].shape], [value[0]], arranged[0], LANDED_COST)[0]
    return settle(arranged, value[1], value[0])


def solution(mesh):
    placed = (
        P("lsec", "rsec", None, None),
        P("op", "lsec", None, None),
        P("op", "rsec", None, None),
        P("op"),
    )
    return jax.shard_map(
        shards, mesh=mesh, in_specs=placed, out_specs=P("lsec", "rsec", "op", None), check_vma=False
    )
```

```python
import jax
import jax.numpy as jnp
from jax import lax
from jax.experimental import pallas as pl
from jax.experimental.pallas import tpu as pltpu
from jax.sharding import PartitionSpec as P

CORES = 2
ARRANGE_COST = 1
ADD_COST = 2 * 10 ** 9
LANDED_COST = 6 * 10 ** 8
LIMIT = 32 * 1024 * 1024
NT = (((1,), (1,)), ((), ()))
PARAMS = pltpu.CompilerParams(vmem_limit_bytes=LIMIT)
HBM = pl.BlockSpec(memory_space=pltpu.HBM)
VMEM = pl.BlockSpec(memory_space=pltpu.VMEM)
ANY = pl.BlockSpec(memory_space=pl.ANY)


def split(value):
    high = value.astype(jnp.bfloat16)
    low = (value - high.astype(jnp.float32)).astype(jnp.bfloat16)
    return high, low


def choose_rows(lops, left, l):
    terms, _, many, _ = lops.shape
    for t in range(terms):
        left[l, t * many:(t + 1) * many, :] = jnp.concatenate(split(lops[t, l]), axis=1)


def lines(many, rows, slots, second):
    core = lax.rem(lax.axis_index("op"), CORES)
    return core * (rows // 8), (1 - core) * (rows // 8), skipped(slots, second) * (many // 8)


def products(left, psi, right, chosen, inner, total, send, keep, start, begins, lops=None, rops=None, ready=()):
    slots, height, twice = left.shape
    size = twice // 2
    wide, terms = right.shape[:2]
    many = height // terms
    chips, blocks, rows, _ = keep.shape
    second = blocks // wide - slots
    here, there, skip = begins
    for r in range(wide):
        for l in range(slots):
            if r == 0 and lops is not None:
                choose_rows(lops, left, l)
            both = jnp.concatenate(split(psi[l, start + r]), axis=1)
            out = jnp.dot(left[l], jnp.concatenate([both, both], axis=0), preferred_element_type=jnp.float32)
            for t in range(terms):
                block = out[t * many:(t + 1) * many]
                parts = split(block[:, :size] + block[:, size:])
                inner[t, l * many:(l + 1) * many, :] = jnp.concatenate(parts, axis=1)
        if r == 0:
            for copy in ready:
                copy.wait()
        for t in range(terms):
            if rops is not None:
                right[r, t] = jnp.concatenate(split(rops[t, r]), axis=0)
            both = right[r, t]
            out = lax.dot_general(
                inner[t], jnp.concatenate([both, both], axis=1), NT, preferred_element_type=jnp.float32
            )
            out = (out[:, :size] + out[:, size:]).reshape(-1, 8, size)
            for way in range(2):
                mine = out * chosen[t, way]
                total[way] = mine if t == 0 else total[way] + mine
        for chip in range(chips):
            for at in range(slots + second):
                way = 0 if at < slots else 1
                l = at if at < slots else at - slots
                for ref, begin in ((keep, here), (send, there)):
                    line = begin + (l * many + chip * CORES * rows) // 8 + (skip if way else 0)
                    block = total[way, pl.ds(line, rows // 8)].reshape(rows, size)
                    if isinstance(ref, (list, tuple)):
                        ref[r][chip, at] = block
                    else:
                        ref[chip, at * wide + r] = block


def skipped(slots, second):
    return 0 if second == slots else 1 - lax.axis_index("lsec")


def first_others(shift, psi, lops, rops, send, keep, left, right, chosen, lops_own, psi_now, *refs):
    bits, lops_now, rops_now, inner, total, sems, lsems = refs
    terms, slots, size, _ = lops.shape
    wide = right.shape[0]
    ny = lax.axis_size("op") // CORES
    mine = lax.div(lax.axis_index("op"), CORES)
    share = size // ny

    def rows(ahead, target):
        at = pl.multiple_of(lax.rem(mine + ahead, ny) * share, share)
        return pltpu.make_async_copy(lops.at[:, :, pl.ds(at, share)], target, lsems.at[ahead])

    copies = [rows(ahead, lops_now.at[:, :, pl.ds((ahead - 1) * share, share)]) for ahead in range(1, ny)] + [
        pltpu.make_async_copy(psi.at[:, :wide], psi_now, sems.at[0]),
        pltpu.make_async_copy(shift, bits, sems.at[1]),
    ]
    ready = [pltpu.make_async_copy(rops.at[:, :wide], rops_now, sems.at[2])]
    later = [rows(0, lops_own)]
    for copy in copies + ready:
        copy.start()
    second = keep.shape[1] // wide - slots
    begins = lines(lops_now.shape[2], keep.shape[2], slots, second)
    flip = lax.axis_index("lsec") if second < slots else 0
    for copy in copies:
        copy.wait()
    for copy in later:
        copy.start()
    for t in range(terms):
        kept = jnp.where(flip == 1, 1 - bits[t], bits[t]).astype(jnp.float32)
        chosen[t, 0] = jnp.full((8, size), kept, jnp.float32)
        chosen[t, 1] = jnp.full((8, size), 1.0 - kept, jnp.float32)
    products(
        left, psi_now, right, chosen, inner, total, send, keep, 0, begins, lops_now, rops_now, ready
    )
    for copy in later:
        copy.wait()


def find(left, keep, right):
    slots, height, _ = left.shape
    wide, terms = right.shape[:2]
    return lines(height // terms, keep.shape[2], slots, keep.shape[1] // wide - slots)


def first_own(lops, psi, right, chosen, wave, rops, send, keep, left, psi_rest, rops_rest, inner, total, sems):
    wide = right.shape[0]
    copies = [
        pltpu.make_async_copy(wave.at[:, wide:], psi_rest, sems.at[0]),
        pltpu.make_async_copy(rops.at[:, wide:], rops_rest, sems.at[1]),
    ]
    for copy in copies:
        copy.start()
    products(left, psi, right, chosen, inner, total, send, keep, 0, find(left, keep, right), lops)
    for copy in copies:
        copy.wait()


def later_others(left, psi, rops, chosen, after, *refs):
    wide = refs[-3].shape[0]
    send, (keep, right, inner, total) = refs[:wide], refs[wide:]
    products(
        left, psi, right, chosen, inner, total, send, keep, 0, find(left, keep, right), rops=rops,
    )


def later_own(left, psi, right, chosen, after, send, keep, inner, total):
    products(left, psi, right, chosen, inner, total, send, keep, 0, find(left, keep, right))


def call(kernel, operands, in_specs, out_shape, scratch=(), flops=1):
    return pl.pallas_call(
        kernel,
        in_specs=in_specs,
        out_specs=[VMEM] * len(out_shape),
        out_shape=out_shape,
        scratch_shapes=scratch,
        compiler_params=PARAMS,
        cost_estimate=pl.CostEstimate(flops=flops, bytes_accessed=1024, transcendentals=0),
    )(*operands)


def sums(kernel, shapes, operands, after=None, flops=1):
    reads = len(operands)
    specs = [VMEM] * reads

    def body(*refs):
        kernel(refs[:reads], refs[len(specs):])

    if after is not None:
        operands = [*operands, after]
        specs.append(ANY)
    return call(body, operands, specs, [jax.ShapeDtypeStruct(shape, jnp.float32) for shape in shapes], (), flops)


def arrange(slots, first, second):
    wide, rows, size = first.shape[1:]
    more = second.shape[0]

    def kernel(refs, outs):
        way = 1 - lax.axis_index("lsec") if more < slots else 0
        skip = 1 - skipped(slots, more) if more < slots else 0
        for l in range(slots):
            outs[0][way, l] = refs[0][l]
        for j in range(more):
            outs[0][1 - way, j + skip] = refs[1][j]

    return sums(kernel, [(2, slots, wide, rows, size)], [first, second], None, ARRANGE_COST)[0]


def settle(arranged, first, second):
    slots = first.shape[0]
    rows, size = first.shape[2:]
    more = second.shape[0]
    widths = [value.shape[2] for value in arranged] + [first.shape[1]]
    across = sum(widths)
    n_left, n_right = lax.axis_size("lsec"), lax.axis_size("rsec")

    def kernel(*refs):
        out, every = refs[-2:]
        mine_l, mine_r = lax.axis_index("lsec"), lax.axis_index("rsec")
        first_l, last_l = (mine_l == 0).astype(jnp.int32), (mine_l == n_left - 1).astype(jnp.int32)
        first_r, last_r = (mine_r == 0).astype(jnp.int32), (mine_r == n_right - 1).astype(jnp.int32)
        steps = ((first_l, -last_r), (-last_l, first_r))
        start = 0
        for i, wide in enumerate(widths[:-1]):
            every[:, :, start:start + wide] = refs[i][...]
            start += wide
        way = 1 - mine_l if more < slots else 0
        skip = 1 - skipped(slots, more) if more < slots else 0
        a, b = refs[len(arranged):len(arranged) + 2]
        for l in range(slots):
            every[way, l, start:] = a[l]
        for j in range(more):
            every[1 - way, j + skip, start:] = b[j]
        for l in range(slots):
            for r in range(across):
                block = jnp.zeros((rows, size), jnp.float32)
                for side, (step_l, step_r) in enumerate(steps):
                    from_l, from_r = l - step_l, r - step_r
                    inside = (from_l >= 0) & (from_l < slots) & (from_r >= 0) & (from_r < across)
                    part = every[side, jnp.clip(from_l, 0, slots - 1), jnp.clip(from_r, 0, across - 1)]
                    block = block + jnp.where(inside, part, 0.0)
                out[l, r] = block

    operands = [*arranged, first, second]
    return call(
        kernel, operands, [VMEM] * len(operands),
        [jax.ShapeDtypeStruct((slots, across, rows, size), jnp.float32)],
        [pltpu.VMEM((2, slots, across, rows, size), jnp.float32)],
    )[0]


def shards(wavefn, left_ops, right_ops, term_shift):
    n_op, n_left, n_right = (lax.axis_size(axis) for axis in ("op", "lsec", "rsec"))
    across = wavefn.shape[1]
    terms, slots, size, _ = left_ops.shape
    ny = n_op // CORES
    share = size // ny
    others = (ny - 1) * share
    rows = size // n_op
    second = slots - 1 if n_left == 2 else slots
    f32, bf16 = jnp.float32, jnp.bfloat16

    def permute(value, target):
        def place(o, l, r):
            return (o % n_op * n_left + l % n_left) * n_right + r % n_right

        perm = [
            (place(o, l, r), place(*target(o, l, r)))
            for o in range(n_op) for l in range(n_left) for r in range(n_right)
        ]
        return lax.ppermute(value, ("op", "lsec", "rsec"), perm)

    def swap(value):
        return permute(value, lambda o, l, r: (o ^ 1, l, r))

    def ahead(value, by):
        return permute(value, lambda o, l, r: (o + CORES * by, l, r))

    def sectors(value, way):
        def target(o, l, r):
            up = way == (l if second < slots else 0)
            return (o, l + 1, r - 1) if up else (o, l - 1, r + 1)

        return permute(value, target)

    def blocks(wide):
        return (slots + second) * wide

    def result(chips, wide):
        return jax.ShapeDtypeStruct((chips, blocks(wide), rows, size), f32)

    def work(many):
        return [
            pltpu.VMEM((terms, slots * many, 2 * size), bf16),
            pltpu.VMEM((2, slots * many // 8, 8, size), f32),
        ]

    def add_cores(refs, outs):
        for at, out in enumerate(outs):
            if len(refs) == 2:
                out[...] = refs[0][at] + refs[1][at]
            else:
                wide = len(refs) - 1
                first = 0 if at % 2 else slots * wide
                for block in range(first, first + out.shape[0]):
                    out[block - first] = refs[0][at // 2, block] + refs[1 + block % wide][at // 2, block // wide]

    def add_all(refs, outs):
        total = refs[0][...]
        for ref in refs[1:]:
            total = total + ref[...].reshape(total.shape)
        total = total.reshape(-1, rows, size)
        start = 0
        for out in outs:
            count = 1
            for length in out.shape[:-2]:
                count *= length
            out[...] = total[start:start + count].reshape(out.shape)
            start += count

    def landed_first(refs, outs):
        outs[0][...] = refs[0][...]

    widths = (across // 2, across - across // 2)
    starts = [sum(widths[:i]) for i in range(len(widths))]
    pieces, own_kept, own_arrived, arrived, kept = [], [], [], [], []

    arguments = [
        pltpu.with_memory_space_constraint(value, pltpu.HBM)
        for value in (term_shift, wavefn, left_ops, right_ops)
    ]
    wide = widths[0]
    send, keep, left, right, chosen, lops, psi_now = call(
        first_others,
        arguments,
        [HBM] * 4,
        [result(ny - 1, wide)] * 2 + [
            jax.ShapeDtypeStruct((slots, terms * others, 2 * size), bf16),
            jax.ShapeDtypeStruct((wide, terms, 2 * size, size), bf16),
            jax.ShapeDtypeStruct((terms, 2, 8, size), f32),
            jax.ShapeDtypeStruct((terms, slots, share, size), f32),
            jax.ShapeDtypeStruct((slots, wide, size, size), f32),
        ],
        [
            pltpu.SMEM(term_shift.shape, jnp.int32),
            pltpu.VMEM((terms, slots, others, size), f32),
            pltpu.VMEM((terms, wide, size, size), f32),
            *work(others),
            pltpu.SemaphoreType.DMA((3,)),
            pltpu.SemaphoreType.DMA((ny,)),
        ],
    )
    kept.append(keep)
    arrived.append(swap(send))
    send, keep, own, psi, rops = call(
        first_own,
        [lops, psi_now, right, chosen, arguments[1], arguments[3]],
        [VMEM] * 4 + [HBM] * 2,
        [result(1, wide)] * 2 + [
            jax.ShapeDtypeStruct((slots, terms * share, 2 * size), bf16),
            jax.ShapeDtypeStruct((slots, across - wide, size, size), f32),
            jax.ShapeDtypeStruct((terms, across - wide, size, size), f32),
        ],
        work(share) + [pltpu.SemaphoreType.DMA((2,))],
    )
    own_kept.append(keep)
    own_arrived.append(swap(send))
    pieces.append(sums(add_cores, [(blocks(wide), rows, size)] * (ny - 1), [kept[0], arrived[0]], keep))
    for start, wide in zip(starts[1:], widths[1:]):
        *send, keep, right = call(
            later_others,
            [left, psi, rops, chosen, pieces[-1][0]],
            [VMEM] * 4 + [ANY],
            [result(ny - 1, 1)] * wide + [
                result(ny - 1, wide), jax.ShapeDtypeStruct((wide, terms, 2 * size, size), bf16)
            ],
            work(others),
        )
        arrived.append([swap(value) for value in send])
        kept.append(keep)
        send, keep = call(
            later_own,
            [own, psi, right, chosen, keep],
            [VMEM] * 4 + [ANY],
            [result(1, wide)] * 2,
            work(share),
        )
        own_kept.append(keep)
        own_arrived.append(swap(send))
        groups = [(number * wide, rows, size) for number in (second, slots)]
        pieces.append(sums(add_cores, groups * (ny - 1), [kept[-1], *arrived[-1]], own_kept[-1]))

    def land(values):
        return [ahead(value, by) for by, value in enumerate(values, 1)]

    wide = widths[0]
    total = sums(add_all, [own_kept[0].shape], [own_kept[0], *land(pieces[0])], pieces[1][0])[0]
    value = sums(
        add_all, [(slots, wide, rows, size), (second, wide, rows, size)], [total, own_arrived[0]], None, ADD_COST
    )
    ready = value[1]
    value = [sectors(part, way) for way, part in enumerate(value)]
    value[1] = sums(landed_first, [value[1].shape], [value[1]], None, LANDED_COST)[0]
    arranged = [arrange(slots, *value)]

    wide = widths[1]
    total = sums(add_all, [(blocks(wide), rows, size)], [own_kept[1], own_arrived[1]], ready)[0]

    def add_group(refs, outs):
        block = refs[0][first:first + refs[1].shape[0]]
        for ref in refs[1:]:
            block = block + ref[...]
        outs[0][...] = block.reshape(outs[0].shape)

    value = []
    for way, number, first in ((1, second, slots * wide), (0, slots, 0)):
        came = land(pieces[1][1 - way::2])
        ready = sums(add_group, [(number, wide, rows, size)], [total, *came], ready)[0]
        value.append(sectors(ready, way))
    value[0] = sums(landed_first, [value[0].shape], [value[0]], arranged[0], LANDED_COST)[0]
    return settle(arranged, value[1], value[0])


def solution(mesh):
    placed = (
        P("lsec", "rsec", None, None),
        P("op", "lsec", None, None),
        P("op", "rsec", None, None),
        P("op"),
    )
    return jax.shard_map(
        shards, mesh=mesh, in_specs=placed, out_specs=P("lsec", "rsec", "op", None), check_vma=False
    )
```

```python
import functools

import jax
import jax.numpy as jnp
from jax import lax
from jax.experimental import pallas as pl
from jax.experimental.pallas import tpu as pltpu
from jax.sharding import PartitionSpec as P

CORES = 2
ARRANGE_COST = 1
ADD_COST = 2 * 10 ** 9
LANDED_COST = 6 * 10 ** 8
LIMIT = 32 * 1024 * 1024
NT = (((1,), (1,)), ((), ()))
PARAMS = pltpu.CompilerParams(vmem_limit_bytes=LIMIT)
HBM = pl.BlockSpec(memory_space=pltpu.HBM)
VMEM = pl.BlockSpec(memory_space=pltpu.VMEM)
ANY = pl.BlockSpec(memory_space=pl.ANY)


def split(value):
    high = value.astype(jnp.bfloat16)
    low = (value - high.astype(jnp.float32)).astype(jnp.bfloat16)
    return high, low


def choose_rows(lops, left, l):
    terms, _, many, _ = lops.shape
    for t in range(terms):
        left[l, t * many:(t + 1) * many, :] = jnp.concatenate(split(lops[t, l]), axis=1)


def lines(many, rows, slots, second):
    core = lax.rem(lax.axis_index("op"), CORES)
    return core * (rows // 8), (1 - core) * (rows // 8), skipped(slots, second) * (many // 8)


def products(left, psi, right, chosen, inner, total, send, keep, start, begins, lops=None, rops=None, ready=()):
    slots, height, twice = left.shape
    size = twice // 2
    wide, terms = right.shape[:2]
    many = height // terms
    chips, blocks, rows, _ = keep.shape
    second = blocks // wide - slots
    here, there, skip = begins
    for r in range(wide):
        for l in range(slots):
            if r == 0 and lops is not None:
                choose_rows(lops, left, l)
            both = jnp.concatenate(split(psi[l, start + r]), axis=1)
            out = jnp.dot(left[l], jnp.concatenate([both, both], axis=0), preferred_element_type=jnp.float32)
            for t in range(terms):
                block = out[t * many:(t + 1) * many]
                parts = split(block[:, :size] + block[:, size:])
                inner[t, l * many:(l + 1) * many, :] = jnp.concatenate(parts, axis=1)
        if r == 0:
            for copy in ready:
                copy.wait()
        for t in range(terms):
            if rops is not None:
                right[r, t] = jnp.concatenate(split(rops[t, r]), axis=0)
            both = right[r, t]
            out = lax.dot_general(
                inner[t], jnp.concatenate([both, both], axis=1), NT, preferred_element_type=jnp.float32
            )
            out = (out[:, :size] + out[:, size:]).reshape(-1, 8, size)
            for way in range(2):
                mine = out * chosen[t, way]
                total[way] = mine if t == 0 else total[way] + mine
        for chip in range(chips):
            for at in range(slots + second):
                way = 0 if at < slots else 1
                l = at if at < slots else at - slots
                for ref, begin in ((keep, here), (send, there)):
                    line = begin + (l * many + chip * CORES * rows) // 8 + (skip if way else 0)
                    block = total[way, pl.ds(line, rows // 8)].reshape(rows, size)
                    if isinstance(ref, tuple):
                        ref[way][chip, (at - way * slots) * wide + r] = block
                    elif isinstance(ref, list):
                        ref[r][chip, at] = block
                    else:
                        ref[chip, at * wide + r] = block


def skipped(slots, second):
    return 0 if second == slots else 1 - lax.axis_index("lsec")


def first_others(shift, psi, lops, rops, send, keep, left, right, chosen, lops_own, psi_all, rops_rest, *refs):
    bits, lops_now, rops_now, inner, total, sems, lsems = refs
    terms, slots, size, _ = lops.shape
    wide = right.shape[0]
    ny = lax.axis_size("op") // CORES
    mine = lax.div(lax.axis_index("op"), CORES)
    share = size // ny

    def rows(ahead, target):
        at = pl.multiple_of(lax.rem(mine + ahead, ny) * share, share)
        return pltpu.make_async_copy(lops.at[:, :, pl.ds(at, share)], target, lsems.at[ahead])

    copies = [rows(ahead, lops_now.at[:, :, pl.ds((ahead - 1) * share, share)]) for ahead in range(1, ny)] + [
        pltpu.make_async_copy(psi.at[:, :wide], psi_all.at[:, :wide], sems.at[0]),
        pltpu.make_async_copy(shift, bits, sems.at[1]),
    ]
    ready = [pltpu.make_async_copy(rops.at[:, :wide], rops_now, sems.at[2])]
    later = [rows(0, lops_own)]
    if wide < rops.shape[1]:
        later += [
            pltpu.make_async_copy(psi.at[:, wide:], psi_all.at[:, wide:], sems.at[3]),
            pltpu.make_async_copy(rops.at[:, wide:], rops_rest, sems.at[4]),
        ]
    for copy in copies + ready:
        copy.start()
    second = keep.shape[1] // wide - slots
    begins = lines(lops_now.shape[2], keep.shape[2], slots, second)
    flip = lax.axis_index("lsec") if second < slots else 0
    for copy in copies:
        copy.wait()
    for copy in later:
        copy.start()
    for t in range(terms):
        kept = jnp.where(flip == 1, 1 - bits[t], bits[t]).astype(jnp.float32)
        chosen[t, 0] = jnp.full((8, size), kept, jnp.float32)
        chosen[t, 1] = jnp.full((8, size), 1.0 - kept, jnp.float32)
    products(
        left, psi_all, right, chosen, inner, total, send, keep, 0, begins, lops_now, rops_now, ready
    )
    for copy in later:
        copy.wait()


def find(left, keep, right):
    slots, height, _ = left.shape
    wide, terms = right.shape[:2]
    return lines(height // terms, keep.shape[2], slots, keep.shape[1] // wide - slots)


def first_own(lops, psi, right, chosen, after, send, keep, left, inner, total):
    products(left, psi, right, chosen, inner, total, send, keep, 0, find(left, keep, right), lops)


def later_others(start, skip, left, psi, rops, chosen, after, *refs):
    wide = refs[-3].shape[0]
    send, (keep, right, inner, total) = list(refs[:wide]), refs[wide:]
    products(
        left, psi, right, chosen, inner, total, send, keep, start, find(left, keep, right),
        rops=rops.at[:, start - skip:],
    )


def later_own(start, left, psi, right, chosen, after, send, rest, keep, inner, total):
    products(left, psi, right, chosen, inner, total, (send, rest), keep, start, find(left, keep, right))


def call(kernel, operands, in_specs, out_shape, scratch=(), flops=1):
    return pl.pallas_call(
        kernel,
        in_specs=in_specs,
        out_specs=[VMEM] * len(out_shape),
        out_shape=out_shape,
        scratch_shapes=scratch,
        compiler_params=PARAMS,
        cost_estimate=pl.CostEstimate(flops=flops, bytes_accessed=1024, transcendentals=0),
    )(*operands)


def sums(kernel, shapes, operands, after=None, flops=1):
    reads = len(operands)
    specs = [VMEM] * reads

    def body(*refs):
        kernel(refs[:reads], refs[len(specs):])

    if after is not None:
        operands = [*operands, after]
        specs.append(ANY)
    return call(body, operands, specs, [jax.ShapeDtypeStruct(shape, jnp.float32) for shape in shapes], (), flops)


def arrange(slots, first, second):
    wide, rows, size = first.shape[1:]
    more = second.shape[0]

    def kernel(refs, outs):
        way = 1 - lax.axis_index("lsec") if more < slots else 0
        skip = 1 - skipped(slots, more) if more < slots else 0
        for l in range(slots):
            outs[0][way, l] = refs[0][l]
        for j in range(more):
            outs[0][1 - way, j + skip] = refs[1][j]

    return sums(kernel, [(2, slots, wide, rows, size)], [first, second], None, ARRANGE_COST)[0]


def settle(arranged, first, second):
    slots = first.shape[0]
    rows, size = first.shape[2:]
    more = second.shape[0]
    widths = [value.shape[2] for value in arranged] + [first.shape[1]]
    across = sum(widths)
    n_left, n_right = lax.axis_size("lsec"), lax.axis_size("rsec")

    def kernel(*refs):
        out, every = refs[-2:]
        mine_l, mine_r = lax.axis_index("lsec"), lax.axis_index("rsec")
        first_l, last_l = (mine_l == 0).astype(jnp.int32), (mine_l == n_left - 1).astype(jnp.int32)
        first_r, last_r = (mine_r == 0).astype(jnp.int32), (mine_r == n_right - 1).astype(jnp.int32)
        steps = ((first_l, -last_r), (-last_l, first_r))
        start = 0
        for i, wide in enumerate(widths[:-1]):
            every[:, :, start:start + wide] = refs[i][...]
            start += wide
        way = 1 - mine_l if more < slots else 0
        skip = 1 - skipped(slots, more) if more < slots else 0
        a, b = refs[len(arranged):len(arranged) + 2]
        for l in range(slots):
            every[way, l, start:] = a[l]
        for j in range(more):
            every[1 - way, j + skip, start:] = b[j]
        for l in range(slots):
            for r in range(across):
                block = jnp.zeros((rows, size), jnp.float32)
                for side, (step_l, step_r) in enumerate(steps):
                    from_l, from_r = l - step_l, r - step_r
                    inside = (from_l >= 0) & (from_l < slots) & (from_r >= 0) & (from_r < across)
                    part = every[side, jnp.clip(from_l, 0, slots - 1), jnp.clip(from_r, 0, across - 1)]
                    block = block + jnp.where(inside, part, 0.0)
                out[l, r] = block

    operands = [*arranged, first, second]
    return call(
        kernel, operands, [VMEM] * len(operands),
        [jax.ShapeDtypeStruct((slots, across, rows, size), jnp.float32)],
        [pltpu.VMEM((2, slots, across, rows, size), jnp.float32)],
    )[0]


def shards(wavefn, left_ops, right_ops, term_shift):
    n_op, n_left, n_right = (lax.axis_size(axis) for axis in ("op", "lsec", "rsec"))
    across = wavefn.shape[1]
    terms, slots, size, _ = left_ops.shape
    ny = n_op // CORES
    share = size // ny
    others = (ny - 1) * share
    rows = size // n_op
    second = slots - 1 if n_left == 2 else slots
    f32, bf16 = jnp.float32, jnp.bfloat16

    def permute(value, target):
        def place(o, l, r):
            return (o % n_op * n_left + l % n_left) * n_right + r % n_right

        perm = [
            (place(o, l, r), place(*target(o, l, r)))
            for o in range(n_op) for l in range(n_left) for r in range(n_right)
        ]
        return lax.ppermute(value, ("op", "lsec", "rsec"), perm)

    def swap(value):
        return permute(value, lambda o, l, r: (o ^ 1, l, r))

    def ahead(value, by):
        return permute(value, lambda o, l, r: (o + CORES * by, l, r))

    def sectors(value, way):
        def target(o, l, r):
            up = way == (l if second < slots else 0)
            return (o, l + 1, r - 1) if up else (o, l - 1, r + 1)

        return permute(value, target)

    def blocks(wide):
        return (slots + second) * wide

    def result(chips, wide):
        return jax.ShapeDtypeStruct((chips, blocks(wide), rows, size), f32)

    def work(many):
        return [
            pltpu.VMEM((terms, slots * many, 2 * size), bf16),
            pltpu.VMEM((2, slots * many // 8, 8, size), f32),
        ]

    def add_cores(refs, outs):
        for at, out in enumerate(outs):
            if len(refs) == 2:
                out[...] = refs[0][at] + refs[1][at]
            else:
                wide = len(refs) - 1
                first = 0 if at % 2 else slots * wide
                for block in range(first, first + out.shape[0]):
                    out[block - first] = refs[0][at // 2, block] + refs[1 + block % wide][at // 2, block // wide]

    def add_all(refs, outs):
        total = refs[0][...]
        for ref in refs[1:]:
            total = total + ref[...].reshape(total.shape)
        total = total.reshape(-1, rows, size)
        start = 0
        for out in outs:
            count = 1
            for length in out.shape[:-2]:
                count *= length
            out[...] = total[start:start + count].reshape(out.shape)
            start += count

    def landed_first(refs, outs):
        outs[0][...] = refs[0][...]

    widths = (across // 2, across - across // 2)
    starts = [sum(widths[:i]) for i in range(len(widths))]
    pieces, own_kept, own_arrived, arrived, kept = [], [], [], [], []

    arguments = (term_shift, wavefn, left_ops, right_ops)
    wide = widths[0]
    send, keep, left, right, chosen, lops, psi, rops = call(
        first_others,
        [pltpu.with_memory_space_constraint(value, pltpu.HBM) for value in arguments],
        [HBM] * 4,
        [result(ny - 1, wide)] * 2 + [
            jax.ShapeDtypeStruct((slots, terms * others, 2 * size), bf16),
            jax.ShapeDtypeStruct((wide, terms, 2 * size, size), bf16),
            jax.ShapeDtypeStruct((terms, 2, 8, size), f32),
            jax.ShapeDtypeStruct((terms, slots, share, size), f32),
            jax.ShapeDtypeStruct(wavefn.shape, f32),
            jax.ShapeDtypeStruct((terms, max(across - wide, 1), size, size), f32),
        ],
        [
            pltpu.SMEM(term_shift.shape, jnp.int32),
            pltpu.VMEM((terms, slots, others, size), f32),
            pltpu.VMEM((terms, wide, size, size), f32),
            *work(others),
            pltpu.SemaphoreType.DMA((5,)),
            pltpu.SemaphoreType.DMA((ny,)),
        ],
    )
    kept.append(keep)
    arrived.append(swap(send))
    start, more = widths
    *send, keep, last = call(
        functools.partial(later_others, start, start),
        [left, psi, rops, chosen, keep],
        [VMEM] * 4 + [ANY],
        [result(ny - 1, 1)] * more + [
            result(ny - 1, more), jax.ShapeDtypeStruct((more, terms, 2 * size, size), bf16)
        ],
        work(others),
    )
    arrived.append([swap(value) for value in send])
    kept.append(keep)
    pieces.append(sums(add_cores, [(blocks(wide), rows, size)] * (ny - 1), [kept[0], arrived[0]], keep))
    send, keep, own = call(
        first_own,
        [lops, psi, right, chosen, pieces[0][0]],
        [VMEM] * 4 + [ANY],
        [result(1, wide)] * 2 + [jax.ShapeDtypeStruct((slots, terms * share, 2 * size), bf16)],
        work(share),
    )
    own_kept.append(keep)
    own_arrived.append(swap(send))
    groups = [(number * more, rows, size) for number in (second, slots)]
    pieces.append(sums(add_cores, groups * (ny - 1), [kept[1], *arrived[1]], keep))
    *send, keep = call(
        functools.partial(later_own, start),
        [own, psi, last, chosen, pieces[1][0]],
        [VMEM] * 4 + [ANY],
        [jax.ShapeDtypeStruct((1, number * more, rows, size), f32) for number in (slots, second)] + [result(1, more)],
        work(share),
    )
    own_kept.append(keep)
    own_arrived.append([swap(value) for value in send])

    def land(values):
        return [ahead(value, by) for by, value in enumerate(values, 1)]

    wide = widths[0]
    total = sums(add_all, [own_kept[0].shape], [own_kept[0], *land(pieces[0])], own_kept[1])[0]
    value = sums(
        add_all, [(slots, wide, rows, size), (second, wide, rows, size)], [total, own_arrived[0]], None, ADD_COST
    )
    ready = value[1]
    value = [sectors(part, way) for way, part in enumerate(value)]
    value[1] = sums(landed_first, [value[1].shape], [value[1]], None, LANDED_COST)[0]
    arranged = [arrange(slots, *value)]

    wide = widths[1]

    def add_group(refs, outs):
        block = refs[0][0, first:first + refs[1].shape[0]]
        for ref in refs[1:]:
            block = block + ref[...]
        outs[0][...] = block

    def add_swapped(refs, outs):
        outs[0][...] = (refs[0][...] + refs[1][0]).reshape(outs[0].shape)

    value = []
    for way, number, first in ((1, second, slots * wide), (0, slots, 0)):
        came = land(pieces[1][1 - way::2])
        ready = sums(add_group, [(number * wide, rows, size)], [own_kept[1], *came], ready)[0]
        ready = sums(add_swapped, [(number, wide, rows, size)], [ready, own_arrived[1][way]])[0]
        value.append(sectors(ready, way))
    value[0] = sums(landed_first, [value[0].shape], [value[0]], arranged[0], LANDED_COST)[0]
    return settle(arranged, value[1], value[0])


def solution(mesh):
    placed = (
        P("lsec", "rsec", None, None),
        P("op", "lsec", None, None),
        P("op", "rsec", None, None),
        P("op"),
    )
    return jax.shard_map(
        shards, mesh=mesh, in_specs=placed, out_specs=P("lsec", "rsec", "op", None), check_vma=False
    )
```

```python
import functools

import jax
import jax.numpy as jnp
from jax import lax
from jax.experimental import pallas as pl
from jax.experimental.pallas import tpu as pltpu
from jax.sharding import PartitionSpec as P

CORES = 2
ARRANGE_COST = 1
ADD_COST = 2 * 10 ** 9
LANDED_COST = 6 * 10 ** 8
LIMIT = 32 * 1024 * 1024
NT = (((1,), (1,)), ((), ()))
PARAMS = pltpu.CompilerParams(vmem_limit_bytes=LIMIT)
HBM = pl.BlockSpec(memory_space=pltpu.HBM)
VMEM = pl.BlockSpec(memory_space=pltpu.VMEM)
ANY = pl.BlockSpec(memory_space=pl.ANY)


def split(value):
    high = value.astype(jnp.bfloat16)
    low = (value - high.astype(jnp.float32)).astype(jnp.bfloat16)
    return high, low


def choose_rows(lops, left, l):
    terms, _, many, _ = lops.shape
    for t in range(terms):
        left[l, t * many:(t + 1) * many, :] = jnp.concatenate(split(lops[t, l]), axis=1)


def lines(many, rows, slots, second):
    core = lax.rem(lax.axis_index("op"), CORES)
    return core * (rows // 8), (1 - core) * (rows // 8), skipped(slots, second) * (many // 8)


def products(left, psi, right, chosen, inner, total, send, keep, start, begins, lops=None, rops=None, ready=()):
    slots, height, twice = left.shape
    size = twice // 2
    wide, terms = right.shape[:2]
    many = height // terms
    chips, blocks, rows, _ = keep.shape
    second = blocks // wide - slots
    here, there, skip = begins
    for r in range(wide):
        for l in range(slots):
            if r == 0 and lops is not None:
                choose_rows(lops, left, l)
            both = jnp.concatenate(split(psi[l, start + r]), axis=1)
            out = jnp.dot(left[l], jnp.concatenate([both, both], axis=0), preferred_element_type=jnp.float32)
            for t in range(terms):
                block = out[t * many:(t + 1) * many]
                parts = split(block[:, :size] + block[:, size:])
                inner[t, l * many:(l + 1) * many, :] = jnp.concatenate(parts, axis=1)
        if r == 0:
            for copy in ready:
                copy.wait()
        for t in range(terms):
            if rops is not None:
                right[r, t] = jnp.concatenate(split(rops[t, r]), axis=0)
            both = right[r, t]
            out = lax.dot_general(
                inner[t], jnp.concatenate([both, both], axis=1), NT, preferred_element_type=jnp.float32
            )
            out = (out[:, :size] + out[:, size:]).reshape(-1, 8, size)
            for way in range(2):
                mine = out * chosen[t, way]
                total[way] = mine if t == 0 else total[way] + mine
        for chip in range(chips):
            for at in range(slots + second):
                way = 0 if at < slots else 1
                l = at if at < slots else at - slots
                for ref, begin in ((keep, here), (send, there)):
                    line = begin + (l * many + chip * CORES * rows) // 8 + (skip if way else 0)
                    block = total[way, pl.ds(line, rows // 8)].reshape(rows, size)
                    if isinstance(ref, (list, tuple)):
                        ref[r][chip, at] = block
                    else:
                        ref[chip, at * wide + r] = block


def skipped(slots, second):
    return 0 if second == slots else 1 - lax.axis_index("lsec")


def first_others(shift, psi, lops, rops, send, keep, left, right, chosen, lops_own, psi_all, rops_rest, *refs):
    bits, lops_now, rops_now, inner, total, sems, lsems = refs
    terms, slots, size, _ = lops.shape
    wide = right.shape[0]
    ny = lax.axis_size("op") // CORES
    mine = lax.div(lax.axis_index("op"), CORES)
    share = size // ny

    def rows(ahead, target):
        at = pl.multiple_of(lax.rem(mine + ahead, ny) * share, share)
        return pltpu.make_async_copy(lops.at[:, :, pl.ds(at, share)], target, lsems.at[ahead])

    copies = [rows(ahead, lops_now.at[:, :, pl.ds((ahead - 1) * share, share)]) for ahead in range(1, ny)] + [
        pltpu.make_async_copy(psi.at[:, :wide], psi_all.at[:, :wide], sems.at[0]),
        pltpu.make_async_copy(shift, bits, sems.at[1]),
    ]
    ready = [pltpu.make_async_copy(rops.at[:, :wide], rops_now, sems.at[2])]
    later = [rows(0, lops_own)]
    if wide < rops.shape[1]:
        later += [
            pltpu.make_async_copy(psi.at[:, wide:], psi_all.at[:, wide:], sems.at[3]),
            pltpu.make_async_copy(rops.at[:, wide:], rops_rest, sems.at[4]),
        ]
    for copy in copies + ready + later:
        copy.start()
    second = keep.shape[1] // wide - slots
    begins = lines(lops_now.shape[2], keep.shape[2], slots, second)
    flip = lax.axis_index("lsec") if second < slots else 0
    for copy in copies:
        copy.wait()
    for t in range(terms):
        kept = jnp.where(flip == 1, 1 - bits[t], bits[t]).astype(jnp.float32)
        chosen[t, 0] = jnp.full((8, size), kept, jnp.float32)
        chosen[t, 1] = jnp.full((8, size), 1.0 - kept, jnp.float32)
    products(
        left, psi_all, right, chosen, inner, total, send, keep, 0, begins, lops_now, rops_now, ready
    )
    for copy in later:
        copy.wait()


def find(left, keep, right):
    slots, height, _ = left.shape
    wide, terms = right.shape[:2]
    return lines(height // terms, keep.shape[2], slots, keep.shape[1] // wide - slots)


def first_own(lops, psi, right, chosen, send, keep, left, inner, total):
    products(left, psi, right, chosen, inner, total, send, keep, 0, find(left, keep, right), lops)


def later_others(start, skip, left, psi, rops, chosen, after, *refs):
    wide = refs[-3].shape[0]
    send, (keep, right, inner, total) = refs[:wide], refs[wide:]
    products(
        left, psi, right, chosen, inner, total, send, keep, start, find(left, keep, right),
        rops=rops.at[:, start - skip:],
    )


def later_own(start, left, psi, right, chosen, after, send, keep, inner, total):
    products(left, psi, right, chosen, inner, total, send, keep, start, find(left, keep, right))


def call(kernel, operands, in_specs, out_shape, scratch=(), flops=1):
    return pl.pallas_call(
        kernel,
        in_specs=in_specs,
        out_specs=[VMEM] * len(out_shape),
        out_shape=out_shape,
        scratch_shapes=scratch,
        compiler_params=PARAMS,
        cost_estimate=pl.CostEstimate(flops=flops, bytes_accessed=1024, transcendentals=0),
    )(*operands)


def sums(kernel, shapes, operands, after=None, flops=1):
    reads = len(operands)
    specs = [VMEM] * reads

    def body(*refs):
        kernel(refs[:reads], refs[len(specs):])

    if after is not None:
        operands = [*operands, after]
        specs.append(ANY)
    return call(body, operands, specs, [jax.ShapeDtypeStruct(shape, jnp.float32) for shape in shapes], (), flops)


def arrange(slots, first, second):
    wide, rows, size = first.shape[1:]
    more = second.shape[0]

    def kernel(refs, outs):
        way = 1 - lax.axis_index("lsec") if more < slots else 0
        skip = 1 - skipped(slots, more) if more < slots else 0
        for l in range(slots):
            outs[0][way, l] = refs[0][l]
        for j in range(more):
            outs[0][1 - way, j + skip] = refs[1][j]

    return sums(kernel, [(2, slots, wide, rows, size)], [first, second], None, ARRANGE_COST)[0]


def settle(arranged, first, second):
    slots = first.shape[0]
    rows, size = first.shape[2:]
    more = second.shape[0]
    widths = [value.shape[2] for value in arranged] + [first.shape[1]]
    across = sum(widths)
    n_left, n_right = lax.axis_size("lsec"), lax.axis_size("rsec")

    def kernel(*refs):
        out, every = refs[-2:]
        mine_l, mine_r = lax.axis_index("lsec"), lax.axis_index("rsec")
        first_l, last_l = (mine_l == 0).astype(jnp.int32), (mine_l == n_left - 1).astype(jnp.int32)
        first_r, last_r = (mine_r == 0).astype(jnp.int32), (mine_r == n_right - 1).astype(jnp.int32)
        steps = ((first_l, -last_r), (-last_l, first_r))
        start = 0
        for i, wide in enumerate(widths[:-1]):
            every[:, :, start:start + wide] = refs[i][...]
            start += wide
        way = 1 - mine_l if more < slots else 0
        skip = 1 - skipped(slots, more) if more < slots else 0
        a, b = refs[len(arranged):len(arranged) + 2]
        for l in range(slots):
            every[way, l, start:] = a[l]
        for j in range(more):
            every[1 - way, j + skip, start:] = b[j]
        for l in range(slots):
            for r in range(across):
                block = jnp.zeros((rows, size), jnp.float32)
                for side, (step_l, step_r) in enumerate(steps):
                    from_l, from_r = l - step_l, r - step_r
                    inside = (from_l >= 0) & (from_l < slots) & (from_r >= 0) & (from_r < across)
                    part = every[side, jnp.clip(from_l, 0, slots - 1), jnp.clip(from_r, 0, across - 1)]
                    block = block + jnp.where(inside, part, 0.0)
                out[l, r] = block

    operands = [*arranged, first, second]
    return call(
        kernel, operands, [VMEM] * len(operands),
        [jax.ShapeDtypeStruct((slots, across, rows, size), jnp.float32)],
        [pltpu.VMEM((2, slots, across, rows, size), jnp.float32)],
    )[0]


def shards(wavefn, left_ops, right_ops, term_shift):
    n_op, n_left, n_right = (lax.axis_size(axis) for axis in ("op", "lsec", "rsec"))
    across = wavefn.shape[1]
    terms, slots, size, _ = left_ops.shape
    ny = n_op // CORES
    share = size // ny
    others = (ny - 1) * share
    rows = size // n_op
    second = slots - 1 if n_left == 2 else slots
    f32, bf16 = jnp.float32, jnp.bfloat16

    def permute(value, target):
        def place(o, l, r):
            return (o % n_op * n_left + l % n_left) * n_right + r % n_right

        perm = [
            (place(o, l, r), place(*target(o, l, r)))
            for o in range(n_op) for l in range(n_left) for r in range(n_right)
        ]
        return lax.ppermute(value, ("op", "lsec", "rsec"), perm)

    def swap(value):
        return permute(value, lambda o, l, r: (o ^ 1, l, r))

    def ahead(value, by):
        return permute(value, lambda o, l, r: (o + CORES * by, l, r))

    def sectors(value, way):
        def target(o, l, r):
            up = way == (l if second < slots else 0)
            return (o, l + 1, r - 1) if up else (o, l - 1, r + 1)

        return permute(value, target)

    def blocks(wide):
        return (slots + second) * wide

    def result(chips, wide):
        return jax.ShapeDtypeStruct((chips, blocks(wide), rows, size), f32)

    def work(many):
        return [
            pltpu.VMEM((terms, slots * many, 2 * size), bf16),
            pltpu.VMEM((2, slots * many // 8, 8, size), f32),
        ]

    def add_cores(refs, outs):
        for at, out in enumerate(outs):
            if len(refs) == 2:
                out[...] = refs[0][at] + refs[1][at]
            else:
                wide = len(refs) - 1
                first = 0 if at % 2 else slots * wide
                for block in range(first, first + out.shape[0]):
                    out[block - first] = refs[0][at // 2, block] + refs[1 + block % wide][at // 2, block // wide]

    def add_all(refs, outs):
        total = refs[0][...]
        for ref in refs[1:]:
            total = total + ref[...].reshape(total.shape)
        total = total.reshape(-1, rows, size)
        start = 0
        for out in outs:
            count = 1
            for length in out.shape[:-2]:
                count *= length
            out[...] = total[start:start + count].reshape(out.shape)
            start += count

    def landed_first(refs, outs):
        outs[0][...] = refs[0][...]

    widths = (across // 2, across - across // 2)
    starts = [sum(widths[:i]) for i in range(len(widths))]
    pieces, own_kept, own_arrived, arrived, kept = [], [], [], [], []

    arguments = (term_shift, wavefn, left_ops, right_ops)
    wide = widths[0]
    send, keep, left, right, chosen, lops, psi, rops = call(
        first_others,
        [pltpu.with_memory_space_constraint(value, pltpu.HBM) for value in arguments],
        [HBM] * 4,
        [result(ny - 1, wide)] * 2 + [
            jax.ShapeDtypeStruct((slots, terms * others, 2 * size), bf16),
            jax.ShapeDtypeStruct((wide, terms, 2 * size, size), bf16),
            jax.ShapeDtypeStruct((terms, 2, 8, size), f32),
            jax.ShapeDtypeStruct((terms, slots, share, size), f32),
            jax.ShapeDtypeStruct(wavefn.shape, f32),
            jax.ShapeDtypeStruct((terms, max(across - wide, 1), size, size), f32),
        ],
        [
            pltpu.SMEM(term_shift.shape, jnp.int32),
            pltpu.VMEM((terms, slots, others, size), f32),
            pltpu.VMEM((terms, wide, size, size), f32),
            *work(others),
            pltpu.SemaphoreType.DMA((5,)),
            pltpu.SemaphoreType.DMA((ny,)),
        ],
    )
    kept.append(keep)
    arrived.append(swap(send))
    send, keep, own = call(
        first_own,
        [lops, psi, right, chosen],
        [VMEM] * 4,
        [result(1, wide)] * 2 + [jax.ShapeDtypeStruct((slots, terms * share, 2 * size), bf16)],
        work(share),
    )
    own_kept.append(keep)
    own_arrived.append(swap(send))
    pieces.append(sums(add_cores, [(blocks(wide), rows, size)] * (ny - 1), [kept[0], arrived[0]], keep))
    for start, wide in zip(starts[1:], widths[1:]):
        *send, keep, right = call(
            functools.partial(later_others, start, widths[0]),
            [left, psi, rops, chosen, pieces[-1][0]],
            [VMEM] * 4 + [ANY],
            [result(ny - 1, 1)] * wide + [
                result(ny - 1, wide), jax.ShapeDtypeStruct((wide, terms, 2 * size, size), bf16)
            ],
            work(others),
        )
        arrived.append([swap(value) for value in send])
        kept.append(keep)
        send, keep = call(
            functools.partial(later_own, start),
            [own, psi, right, chosen, keep],
            [VMEM] * 4 + [ANY],
            [result(1, wide)] * 2,
            work(share),
        )
        own_kept.append(keep)
        own_arrived.append(swap(send))
        groups = [(number * wide, rows, size) for number in (second, slots)]
        pieces.append(sums(add_cores, groups * (ny - 1), [kept[-1], *arrived[-1]], own_kept[-1]))

    def land(values):
        return [ahead(value, by) for by, value in enumerate(values, 1)]

    wide = widths[0]
    total = sums(add_all, [own_kept[0].shape], [own_kept[0], *land(pieces[0])], pieces[1][0])[0]
    value = sums(
        add_all, [(slots, wide, rows, size), (second, wide, rows, size)], [total, own_arrived[0]], None, ADD_COST
    )
    ready = value[1]
    value = [sectors(part, way) for way, part in enumerate(value)]
    value[1] = sums(landed_first, [value[1].shape], [value[1]], None, LANDED_COST)[0]
    arranged = [arrange(slots, *value)]

    wide = widths[1]
    total = sums(add_all, [(blocks(wide), rows, size)], [own_kept[1], own_arrived[1]], ready)[0]

    def add_group(refs, outs):
        block = refs[0][first:first + refs[1].shape[0]]
        for ref in refs[1:]:
            block = block + ref[...]
        outs[0][...] = block.reshape(outs[0].shape)

    value = []
    for way, number, first in ((1, second, slots * wide), (0, slots, 0)):
        came = land(pieces[1][1 - way::2])
        ready = sums(add_group, [(number, wide, rows, size)], [total, *came], ready)[0]
        value.append(sectors(ready, way))
    value[0] = sums(landed_first, [value[0].shape], [value[0]], arranged[0], LANDED_COST)[0]
    return settle(arranged, value[1], value[0])


def solution(mesh):
    placed = (
        P("lsec", "rsec", None, None),
        P("op", "lsec", None, None),
        P("op", "rsec", None, None),
        P("op"),
    )
    return jax.shard_map(
        shards, mesh=mesh, in_specs=placed, out_specs=P("lsec", "rsec", "op", None), check_vma=False
    )
```

```python
import functools

import jax
import jax.numpy as jnp
from jax import lax
from jax.experimental import pallas as pl
from jax.experimental.pallas import tpu as pltpu
from jax.sharding import PartitionSpec as P

CORES = 2
ARRANGE_COST = 1
ADD_COST = 2 * 10 ** 9
LANDED_COST = 6 * 10 ** 8
LIMIT = 32 * 1024 * 1024
NT = (((1,), (1,)), ((), ()))
PARAMS = pltpu.CompilerParams(vmem_limit_bytes=LIMIT)
HBM = pl.BlockSpec(memory_space=pltpu.HBM)
VMEM = pl.BlockSpec(memory_space=pltpu.VMEM)
ANY = pl.BlockSpec(memory_space=pl.ANY)


def split(value):
    high = value.astype(jnp.bfloat16)
    low = (value - high.astype(jnp.float32)).astype(jnp.bfloat16)
    return high, low


def choose_rows(lops, left, l):
    terms, _, many, _ = lops.shape
    for t in range(terms):
        left[l, t * many:(t + 1) * many, :] = jnp.concatenate(split(lops[t, l]), axis=1)


def lines(many, rows, slots, second):
    core = lax.rem(lax.axis_index("op"), CORES)
    return core * (rows // 8), (1 - core) * (rows // 8), skipped(slots, second) * (many // 8)


def products(left, psi, right, chosen, inner, total, send, keep, start, begins, lops=None, rops=None, ready=()):
    slots, height, twice = left.shape
    size = twice // 2
    wide, terms = right.shape[:2]
    many = height // terms
    chips, blocks, rows, _ = keep.shape
    second = blocks // wide - slots
    here, there, skip = begins
    for r in range(wide):
        for l in range(slots):
            if r == 0 and lops is not None:
                choose_rows(lops, left, l)
            both = jnp.concatenate(split(psi[l, start + r]), axis=1)
            out = jnp.dot(left[l], jnp.concatenate([both, both], axis=0), preferred_element_type=jnp.float32)
            for t in range(terms):
                block = out[t * many:(t + 1) * many]
                parts = split(block[:, :size] + block[:, size:])
                inner[t, l * many:(l + 1) * many, :] = jnp.concatenate(parts, axis=1)
        if r == 0:
            for copy in ready:
                copy.wait()
        for t in range(terms):
            if rops is not None:
                right[r, t] = jnp.concatenate(split(rops[t, r]), axis=0)
            both = right[r, t]
            out = lax.dot_general(
                inner[t], jnp.concatenate([both, both], axis=1), NT, preferred_element_type=jnp.float32
            )
            out = (out[:, :size] + out[:, size:]).reshape(-1, 8, size)
            mine = out * chosen[t, 0]
            total[0] = mine if t == 0 else total[0] + mine
            total[1] = out if t == 0 else total[1] + out
        for chip in range(chips):
            for at in range(slots + second):
                way = 0 if at < slots else 1
                l = at if at < slots else at - slots
                for ref, begin in ((keep, here), (send, there)):
                    line = begin + (l * many + chip * CORES * rows) // 8 + (skip if way else 0)
                    block = total[way, pl.ds(line, rows // 8)]
                    if way:
                        block = block - total[0, pl.ds(line, rows // 8)]
                    block = block.reshape(rows, size)
                    if isinstance(ref, (list, tuple)):
                        ref[r][chip, at] = block
                    else:
                        ref[chip, at * wide + r] = block


def skipped(slots, second):
    return 0 if second == slots else 1 - lax.axis_index("lsec")


def first_others(shift, psi, lops, rops, send, keep, left, right, chosen, lops_own, psi_all, rops_rest, *refs):
    bits, lops_now, rops_now, inner, total, sems, lsems = refs
    terms, slots, size, _ = lops.shape
    wide = right.shape[0]
    ny = lax.axis_size("op") // CORES
    mine = lax.div(lax.axis_index("op"), CORES)
    share = size // ny

    def rows(ahead, target):
        at = pl.multiple_of(lax.rem(mine + ahead, ny) * share, share)
        return pltpu.make_async_copy(lops.at[:, :, pl.ds(at, share)], target, lsems.at[ahead])

    copies = [rows(ahead, lops_now.at[:, :, pl.ds((ahead - 1) * share, share)]) for ahead in range(1, ny)] + [
        pltpu.make_async_copy(psi.at[:, :wide], psi_all.at[:, :wide], sems.at[0]),
        pltpu.make_async_copy(shift, bits, sems.at[1]),
    ]
    ready = [pltpu.make_async_copy(rops.at[:, :wide], rops_now, sems.at[2])]
    later = [rows(0, lops_own)]
    if wide < rops.shape[1]:
        later += [
            pltpu.make_async_copy(psi.at[:, wide:], psi_all.at[:, wide:], sems.at[3]),
            pltpu.make_async_copy(rops.at[:, wide:], rops_rest, sems.at[4]),
        ]
    for copy in copies + ready:
        copy.start()
    second = keep.shape[1] // wide - slots
    begins = lines(lops_now.shape[2], keep.shape[2], slots, second)
    flip = lax.axis_index("lsec") if second < slots else 0
    for copy in copies:
        copy.wait()
    for copy in later:
        copy.start()
    for t in range(terms):
        kept = jnp.where(flip == 1, 1 - bits[t], bits[t]).astype(jnp.float32)
        chosen[t, 0] = jnp.full((8, size), kept, jnp.float32)
        chosen[t, 1] = jnp.full((8, size), 1.0 - kept, jnp.float32)
    products(
        left, psi_all, right, chosen, inner, total, send, keep, 0, begins, lops_now, rops_now, ready
    )
    for copy in later:
        copy.wait()


def find(left, keep, right):
    slots, height, _ = left.shape
    wide, terms = right.shape[:2]
    return lines(height // terms, keep.shape[2], slots, keep.shape[1] // wide - slots)


def first_own(lops, psi, right, chosen, send, keep, left, inner, total):
    products(left, psi, right, chosen, inner, total, send, keep, 0, find(left, keep, right), lops)


def later_others(start, skip, left, psi, rops, chosen, after, *refs):
    wide = refs[-3].shape[0]
    send, (keep, right, inner, total) = refs[:wide], refs[wide:]
    products(
        left, psi, right, chosen, inner, total, send, keep, start, find(left, keep, right),
        rops=rops.at[:, start - skip:],
    )


def later_own(start, left, psi, right, chosen, after, send, keep, inner, total):
    products(left, psi, right, chosen, inner, total, send, keep, start, find(left, keep, right))


def call(kernel, operands, in_specs, out_shape, scratch=(), flops=1):
    return pl.pallas_call(
        kernel,
        in_specs=in_specs,
        out_specs=[VMEM] * len(out_shape),
        out_shape=out_shape,
        scratch_shapes=scratch,
        compiler_params=PARAMS,
        cost_estimate=pl.CostEstimate(flops=flops, bytes_accessed=1024, transcendentals=0),
    )(*operands)


def sums(kernel, shapes, operands, after=None, flops=1):
    reads = len(operands)
    specs = [VMEM] * reads

    def body(*refs):
        kernel(refs[:reads], refs[len(specs):])

    if after is not None:
        operands = [*operands, after]
        specs.append(ANY)
    return call(body, operands, specs, [jax.ShapeDtypeStruct(shape, jnp.float32) for shape in shapes], (), flops)


def arrange(slots, first, second):
    wide, rows, size = first.shape[1:]
    more = second.shape[0]

    def kernel(refs, outs):
        way = 1 - lax.axis_index("lsec") if more < slots else 0
        skip = 1 - skipped(slots, more) if more < slots else 0
        for l in range(slots):
            outs[0][way, l] = refs[0][l]
        for j in range(more):
            outs[0][1 - way, j + skip] = refs[1][j]

    return sums(kernel, [(2, slots, wide, rows, size)], [first, second], None, ARRANGE_COST)[0]


def settle(arranged, first, second):
    slots = first.shape[0]
    rows, size = first.shape[2:]
    more = second.shape[0]
    widths = [value.shape[2] for value in arranged] + [first.shape[1]]
    across = sum(widths)
    n_left, n_right = lax.axis_size("lsec"), lax.axis_size("rsec")

    def kernel(*refs):
        out, every = refs[-2:]
        mine_l, mine_r = lax.axis_index("lsec"), lax.axis_index("rsec")
        first_l, last_l = (mine_l == 0).astype(jnp.int32), (mine_l == n_left - 1).astype(jnp.int32)
        first_r, last_r = (mine_r == 0).astype(jnp.int32), (mine_r == n_right - 1).astype(jnp.int32)
        steps = ((first_l, -last_r), (-last_l, first_r))
        start = 0
        for i, wide in enumerate(widths[:-1]):
            every[:, :, start:start + wide] = refs[i][...]
            start += wide
        way = 1 - mine_l if more < slots else 0
        skip = 1 - skipped(slots, more) if more < slots else 0
        a, b = refs[len(arranged):len(arranged) + 2]
        for l in range(slots):
            every[way, l, start:] = a[l]
        for j in range(more):
            every[1 - way, j + skip, start:] = b[j]
        for l in range(slots):
            for r in range(across):
                block = jnp.zeros((rows, size), jnp.float32)
                for side, (step_l, step_r) in enumerate(steps):
                    from_l, from_r = l - step_l, r - step_r
                    inside = (from_l >= 0) & (from_l < slots) & (from_r >= 0) & (from_r < across)
                    part = every[side, jnp.clip(from_l, 0, slots - 1), jnp.clip(from_r, 0, across - 1)]
                    block = block + jnp.where(inside, part, 0.0)
                out[l, r] = block

    operands = [*arranged, first, second]
    return call(
        kernel, operands, [VMEM] * len(operands),
        [jax.ShapeDtypeStruct((slots, across, rows, size), jnp.float32)],
        [pltpu.VMEM((2, slots, across, rows, size), jnp.float32)],
    )[0]


def shards(wavefn, left_ops, right_ops, term_shift):
    n_op, n_left, n_right = (lax.axis_size(axis) for axis in ("op", "lsec", "rsec"))
    across = wavefn.shape[1]
    terms, slots, size, _ = left_ops.shape
    ny = n_op // CORES
    share = size // ny
    others = (ny - 1) * share
    rows = size // n_op
    second = slots - 1 if n_left == 2 else slots
    f32, bf16 = jnp.float32, jnp.bfloat16

    def permute(value, target):
        def place(o, l, r):
            return (o % n_op * n_left + l % n_left) * n_right + r % n_right

        perm = [
            (place(o, l, r), place(*target(o, l, r)))
            for o in range(n_op) for l in range(n_left) for r in range(n_right)
        ]
        return lax.ppermute(value, ("op", "lsec", "rsec"), perm)

    def swap(value):
        return permute(value, lambda o, l, r: (o ^ 1, l, r))

    def ahead(value, by):
        return permute(value, lambda o, l, r: (o + CORES * by, l, r))

    def sectors(value, way):
        def target(o, l, r):
            up = way == (l if second < slots else 0)
            return (o, l + 1, r - 1) if up else (o, l - 1, r + 1)

        return permute(value, target)

    def blocks(wide):
        return (slots + second) * wide

    def result(chips, wide):
        return jax.ShapeDtypeStruct((chips, blocks(wide), rows, size), f32)

    def work(many):
        return [
            pltpu.VMEM((terms, slots * many, 2 * size), bf16),
            pltpu.VMEM((2, slots * many // 8, 8, size), f32),
        ]

    def add_cores(refs, outs):
        for at, out in enumerate(outs):
            if len(refs) == 2:
                out[...] = refs[0][at] + refs[1][at]
            else:
                wide = len(refs) - 1
                first = 0 if at % 2 else slots * wide
                for block in range(first, first + out.shape[0]):
                    out[block - first] = refs[0][at // 2, block] + refs[1 + block % wide][at // 2, block // wide]

    def add_all(refs, outs):
        total = refs[0][...]
        for ref in refs[1:]:
            total = total + ref[...].reshape(total.shape)
        total = total.reshape(-1, rows, size)
        start = 0
        for out in outs:
            count = 1
            for length in out.shape[:-2]:
                count *= length
            out[...] = total[start:start + count].reshape(out.shape)
            start += count

    def landed_first(refs, outs):
        outs[0][...] = refs[0][...]

    widths = (across // 2, across - across // 2)
    starts = [sum(widths[:i]) for i in range(len(widths))]
    pieces, own_kept, own_arrived, arrived, kept = [], [], [], [], []

    arguments = (term_shift, wavefn, left_ops, right_ops)
    wide = widths[0]
    send, keep, left, right, chosen, lops, psi, rops = call(
        first_others,
        [pltpu.with_memory_space_constraint(value, pltpu.HBM) for value in arguments],
        [HBM] * 4,
        [result(ny - 1, wide)] * 2 + [
            jax.ShapeDtypeStruct((slots, terms * others, 2 * size), bf16),
            jax.ShapeDtypeStruct((wide, terms, 2 * size, size), bf16),
            jax.ShapeDtypeStruct((terms, 2, 8, size), f32),
            jax.ShapeDtypeStruct((terms, slots, share, size), f32),
            jax.ShapeDtypeStruct(wavefn.shape, f32),
            jax.ShapeDtypeStruct((terms, max(across - wide, 1), size, size), f32),
        ],
        [
            pltpu.SMEM(term_shift.shape, jnp.int32),
            pltpu.VMEM((terms, slots, others, size), f32),
            pltpu.VMEM((terms, wide, size, size), f32),
            *work(others),
            pltpu.SemaphoreType.DMA((5,)),
            pltpu.SemaphoreType.DMA((ny,)),
        ],
    )
    kept.append(keep)
    arrived.append(swap(send))
    send, keep, own = call(
        first_own,
        [lops, psi, right, chosen],
        [VMEM] * 4,
        [result(1, wide)] * 2 + [jax.ShapeDtypeStruct((slots, terms * share, 2 * size), bf16)],
        work(share),
    )
    own_kept.append(keep)
    own_arrived.append(swap(send))
    pieces.append(sums(add_cores, [(blocks(wide), rows, size)] * (ny - 1), [kept[0], arrived[0]], keep))
    for start, wide in zip(starts[1:], widths[1:]):
        *send, keep, right = call(
            functools.partial(later_others, start, widths[0]),
            [left, psi, rops, chosen, pieces[-1][0]],
            [VMEM] * 4 + [ANY],
            [result(ny - 1, 1)] * wide + [
                result(ny - 1, wide), jax.ShapeDtypeStruct((wide, terms, 2 * size, size), bf16)
            ],
            work(others),
        )
        arrived.append([swap(value) for value in send])
        kept.append(keep)
        send, keep = call(
            functools.partial(later_own, start),
            [own, psi, right, chosen, keep],
            [VMEM] * 4 + [ANY],
            [result(1, wide)] * 2,
            work(share),
        )
        own_kept.append(keep)
        own_arrived.append(swap(send))
        groups = [(number * wide, rows, size) for number in (second, slots)]
        pieces.append(sums(add_cores, groups * (ny - 1), [kept[-1], *arrived[-1]], own_kept[-1]))

    def land(values):
        return [ahead(value, by) for by, value in enumerate(values, 1)]

    wide = widths[0]
    total = sums(add_all, [own_kept[0].shape], [own_kept[0], *land(pieces[0])], pieces[1][0])[0]
    value = sums(
        add_all, [(slots, wide, rows, size), (second, wide, rows, size)], [total, own_arrived[0]], None, ADD_COST
    )
    ready = value[1]
    value = [sectors(part, way) for way, part in enumerate(value)]
    value[1] = sums(landed_first, [value[1].shape], [value[1]], None, LANDED_COST)[0]
    arranged = [arrange(slots, *value)]

    wide = widths[1]
    total = sums(add_all, [(blocks(wide), rows, size)], [own_kept[1], own_arrived[1]], ready)[0]

    def add_group(refs, outs):
        block = refs[0][first:first + refs[1].shape[0]]
        for ref in refs[1:]:
            block = block + ref[...]
        outs[0][...] = block.reshape(outs[0].shape)

    value = []
    for way, number, first in ((1, second, slots * wide), (0, slots, 0)):
        came = land(pieces[1][1 - way::2])
        ready = sums(add_group, [(number, wide, rows, size)], [total, *came], ready)[0]
        value.append(sectors(ready, way))
    value[0] = sums(landed_first, [value[0].shape], [value[0]], arranged[0], LANDED_COST)[0]
    return settle(arranged, value[1], value[0])


def solution(mesh):
    placed = (
        P("lsec", "rsec", None, None),
        P("op", "lsec", None, None),
        P("op", "rsec", None, None),
        P("op"),
    )
    return jax.shard_map(
        shards, mesh=mesh, in_specs=placed, out_specs=P("lsec", "rsec", "op", None), check_vma=False
    )
```

```python
import functools

import jax
import jax.numpy as jnp
from jax import lax
from jax.experimental import pallas as pl
from jax.experimental.pallas import tpu as pltpu
from jax.sharding import PartitionSpec as P

CORES = 2
ARRANGE_COST = 1
ADD_COST = 2 * 10 ** 9
LANDED_COST = 6 * 10 ** 8
LIMIT = 32 * 1024 * 1024
NT = (((1,), (1,)), ((), ()))
PARAMS = pltpu.CompilerParams(vmem_limit_bytes=LIMIT)
HBM = pl.BlockSpec(memory_space=pltpu.HBM)
VMEM = pl.BlockSpec(memory_space=pltpu.VMEM)
ANY = pl.BlockSpec(memory_space=pl.ANY)


def split(value):
    high = value.astype(jnp.bfloat16)
    low = (value - high.astype(jnp.float32)).astype(jnp.bfloat16)
    return high, low


def choose_rows(lops, left, l):
    terms, _, many, _ = lops.shape
    for t in range(terms):
        left[l, t * many:(t + 1) * many, :] = jnp.concatenate(split(lops[t, l]), axis=1)


def lines(many, rows, slots, second):
    core = lax.rem(lax.axis_index("op"), CORES)
    return core * (rows // 8), (1 - core) * (rows // 8), skipped(slots, second) * (many // 8)


def products(left, psi, right, chosen, inner, total, send, keep, start, begins, lops=None, rops=None, ready=()):
    slots, height, twice = left.shape
    size = twice // 2
    wide, terms = right.shape[:2]
    many = height // terms
    chips, blocks, rows, _ = keep.shape
    second = blocks // wide - slots
    here, there, skip = begins
    for r in range(wide):
        for l in range(slots):
            if r == 0 and lops is not None:
                choose_rows(lops, left, l)
            both = jnp.concatenate(split(psi[l, start + r]), axis=1)
            out = jnp.dot(left[l], jnp.concatenate([both, both], axis=0), preferred_element_type=jnp.float32)
            for t in range(terms):
                block = out[t * many:(t + 1) * many]
                parts = split(block[:, :size] + block[:, size:])
                inner[t, l * many:(l + 1) * many, :] = jnp.concatenate(parts, axis=1)
        if r == 0:
            for copy in ready:
                copy.wait()
        for t in range(terms):
            if rops is not None:
                right[r, t] = jnp.concatenate(split(rops[t, r]), axis=0)
            both = right[r, t]
            out = lax.dot_general(
                inner[t], jnp.concatenate([both, both], axis=1), NT, preferred_element_type=jnp.float32
            )
            out = (out[:, :size] + out[:, size:]).reshape(-1, 8, size)
            mine = out * chosen[t, 0]
            total[0] = mine if t == 0 else total[0] + mine
            total[1] = out if t == 0 else total[1] + out
        for chip in range(chips):
            for at in range(slots + second):
                way = 0 if at < slots else 1
                l = at if at < slots else at - slots
                for ref, begin in ((keep, here), (send, there)):
                    line = begin + (l * many + chip * CORES * rows) // 8 + (skip if way else 0)
                    block = total[way, pl.ds(line, rows // 8)]
                    if way:
                        block = block - total[0, pl.ds(line, rows // 8)]
                    block = block.reshape(rows, size)
                    if isinstance(ref, (list, tuple)):
                        ref[r][chip, at] = block
                    else:
                        ref[chip, at * wide + r] = block


def skipped(slots, second):
    return 0 if second == slots else 1 - lax.axis_index("lsec")


def first_others(shift, psi, lops, rops, send, keep, left, right, chosen, lops_own, psi_all, rops_rest, *refs):
    bits, lops_now, rops_now, inner, total, sems, lsems = refs
    terms, slots, size, _ = lops.shape
    wide = right.shape[0]
    ny = lax.axis_size("op") // CORES
    mine = lax.div(lax.axis_index("op"), CORES)
    share = size // ny

    def rows(ahead, target):
        at = pl.multiple_of(lax.rem(mine + ahead, ny) * share, share)
        return pltpu.make_async_copy(lops.at[:, :, pl.ds(at, share)], target, lsems.at[ahead])

    copies = [rows(ahead, lops_now.at[:, :, pl.ds((ahead - 1) * share, share)]) for ahead in range(1, ny)] + [
        pltpu.make_async_copy(psi.at[:, :wide], psi_all.at[:, :wide], sems.at[0]),
        pltpu.make_async_copy(shift, bits, sems.at[1]),
    ]
    ready = [pltpu.make_async_copy(rops.at[:, :wide], rops_now, sems.at[2])]
    later = [rows(0, lops_own)]
    if wide < rops.shape[1]:
        later += [
            pltpu.make_async_copy(psi.at[:, wide:], psi_all.at[:, wide:], sems.at[3]),
            pltpu.make_async_copy(rops.at[:, wide:], rops_rest, sems.at[4]),
        ]
    for copy in copies + ready:
        copy.start()
    second = keep.shape[1] // wide - slots
    begins = lines(lops_now.shape[2], keep.shape[2], slots, second)
    flip = lax.axis_index("lsec") if second < slots else 0
    for copy in copies:
        copy.wait()
    for copy in later:
        copy.start()
    for t in range(terms):
        kept = jnp.where(flip == 1, 1 - bits[t], bits[t]).astype(jnp.float32)
        chosen[t, 0] = jnp.full((8, size), kept, jnp.float32)
        chosen[t, 1] = jnp.full((8, size), 1.0 - kept, jnp.float32)
    products(
        left, psi_all, right, chosen, inner, total, send, keep, 0, begins, lops_now, rops_now, ready
    )
    for copy in later:
        copy.wait()


def find(left, keep, right):
    slots, height, _ = left.shape
    wide, terms = right.shape[:2]
    return lines(height // terms, keep.shape[2], slots, keep.shape[1] // wide - slots)


def first_own(lops, psi, right, chosen, send, keep, left, inner, total):
    products(left, psi, right, chosen, inner, total, send, keep, 0, find(left, keep, right), lops)


def later_others(start, skip, left, psi, rops, chosen, after, *refs):
    wide = refs[-3].shape[0]
    send, (keep, right, inner, total) = refs[:wide], refs[wide:]
    products(
        left, psi, right, chosen, inner, total, send, keep, start, find(left, keep, right),
        rops=rops.at[:, start - skip:],
    )


def later_own(start, left, psi, right, chosen, after, send, keep, inner, total):
    products(left, psi, right, chosen, inner, total, send, keep, start, find(left, keep, right))


def call(kernel, operands, in_specs, out_shape, scratch=(), flops=1):
    return pl.pallas_call(
        kernel,
        in_specs=in_specs,
        out_specs=[VMEM] * len(out_shape),
        out_shape=out_shape,
        scratch_shapes=scratch,
        compiler_params=PARAMS,
        cost_estimate=pl.CostEstimate(flops=flops, bytes_accessed=1024, transcendentals=0),
    )(*operands)


def sums(kernel, shapes, operands, after=None, flops=1):
    reads = len(operands)
    specs = [VMEM] * reads

    def body(*refs):
        kernel(refs[:reads], refs[len(specs):])

    if after is not None:
        operands = [*operands, after]
        specs.append(ANY)
    return call(body, operands, specs, [jax.ShapeDtypeStruct(shape, jnp.float32) for shape in shapes], (), flops)


def arrange(slots, first, second):
    wide, rows, size = first.shape[1:]
    more = second.shape[0]

    def kernel(refs, outs):
        way = 1 - lax.axis_index("lsec") if more < slots else 0
        skip = 1 - skipped(slots, more) if more < slots else 0
        for l in range(slots):
            outs[0][way, l] = refs[0][l]
        for j in range(more):
            outs[0][1 - way, j + skip] = refs[1][j]

    return sums(kernel, [(2, slots, wide, rows, size)], [first, second], None, ARRANGE_COST)[0]


def settle(arranged, first, second):
    slots = first.shape[0]
    rows, size = first.shape[2:]
    more = second.shape[0]
    widths = [value.shape[2] for value in arranged] + [first.shape[1]]
    across = sum(widths)
    n_left, n_right = lax.axis_size("lsec"), lax.axis_size("rsec")

    def kernel(*refs):
        out, every = refs[-2:]
        mine_l, mine_r = lax.axis_index("lsec"), lax.axis_index("rsec")
        first_l, last_l = (mine_l == 0).astype(jnp.int32), (mine_l == n_left - 1).astype(jnp.int32)
        first_r, last_r = (mine_r == 0).astype(jnp.int32), (mine_r == n_right - 1).astype(jnp.int32)
        steps = ((first_l, -last_r), (-last_l, first_r))
        start = 0
        for i, wide in enumerate(widths[:-1]):
            every[:, :, start:start + wide] = refs[i][...]
            start += wide
        way = 1 - mine_l if more < slots else 0
        skip = 1 - skipped(slots, more) if more < slots else 0
        a, b = refs[len(arranged):len(arranged) + 2]
        for l in range(slots):
            every[way, l, start:] = a[l]
        for j in range(more):
            every[1 - way, j + skip, start:] = b[j]
        for l in range(slots):
            for r in range(across):
                block = jnp.zeros((rows, size), jnp.float32)
                for side, (step_l, step_r) in enumerate(steps):
                    from_l, from_r = l - step_l, r - step_r
                    inside = (from_l >= 0) & (from_l < slots) & (from_r >= 0) & (from_r < across)
                    part = every[side, jnp.clip(from_l, 0, slots - 1), jnp.clip(from_r, 0, across - 1)]
                    block = block + jnp.where(inside, part, 0.0)
                out[l, r] = block

    operands = [*arranged, first, second]
    return call(
        kernel, operands, [VMEM] * len(operands),
        [jax.ShapeDtypeStruct((slots, across, rows, size), jnp.float32)],
        [pltpu.VMEM((2, slots, across, rows, size), jnp.float32)],
    )[0]


def shards(wavefn, left_ops, right_ops, term_shift):
    n_op, n_left, n_right = (lax.axis_size(axis) for axis in ("op", "lsec", "rsec"))
    across = wavefn.shape[1]
    terms, slots, size, _ = left_ops.shape
    ny = n_op // CORES
    share = size // ny
    others = (ny - 1) * share
    rows = size // n_op
    second = slots - 1 if n_left == 2 else slots
    f32, bf16 = jnp.float32, jnp.bfloat16

    def permute(value, target):
        def place(o, l, r):
            return (o % n_op * n_left + l % n_left) * n_right + r % n_right

        perm = [
            (place(o, l, r), place(*target(o, l, r)))
            for o in range(n_op) for l in range(n_left) for r in range(n_right)
        ]
        return lax.ppermute(value, ("op", "lsec", "rsec"), perm)

    def swap(value):
        return permute(value, lambda o, l, r: (o ^ 1, l, r))

    def ahead(value, by):
        return permute(value, lambda o, l, r: (o + CORES * by, l, r))

    def sectors(value, way):
        def target(o, l, r):
            up = way == (l if second < slots else 0)
            return (o, l + 1, r - 1) if up else (o, l - 1, r + 1)

        return permute(value, target)

    def blocks(wide):
        return (slots + second) * wide

    def result(chips, wide):
        return jax.ShapeDtypeStruct((chips, blocks(wide), rows, size), f32)

    def work(many):
        return [
            pltpu.VMEM((terms, slots * many, 2 * size), bf16),
            pltpu.VMEM((2, slots * many // 8, 8, size), f32),
        ]

    def add_cores(refs, outs):
        for at, out in enumerate(outs):
            if len(refs) == 2:
                out[...] = refs[0][at] + refs[1][at]
            else:
                wide = len(refs) - 1
                first = 0 if at % 2 else slots * wide
                for block in range(first, first + out.shape[0]):
                    out[block - first] = refs[0][at // 2, block] + refs[1 + block % wide][at // 2, block // wide]

    def add_all(refs, outs):
        total = refs[0][...]
        for ref in refs[1:]:
            total = total + ref[...].reshape(total.shape)
        total = total.reshape(-1, rows, size)
        start = 0
        for out in outs:
            count = 1
            for length in out.shape[:-2]:
                count *= length
            out[...] = total[start:start + count].reshape(out.shape)
            start += count

    def landed_first(refs, outs):
        outs[0][...] = refs[0][...]

    widths = (across // 2, across - across // 2)
    starts = [sum(widths[:i]) for i in range(len(widths))]
    pieces, own_kept, own_arrived, arrived, kept = [], [], [], [], []

    arguments = (term_shift, wavefn, left_ops, right_ops)
    wide = widths[0]
    send, keep, left, right, chosen, lops, psi, rops = call(
        first_others,
        [pltpu.with_memory_space_constraint(value, pltpu.HBM) for value in arguments],
        [HBM] * 4,
        [result(ny - 1, wide)] * 2 + [
            jax.ShapeDtypeStruct((slots, terms * others, 2 * size), bf16),
            jax.ShapeDtypeStruct((wide, terms, 2 * size, size), bf16),
            jax.ShapeDtypeStruct((terms, 2, 8, size), f32),
            jax.ShapeDtypeStruct((terms, slots, share, size), f32),
            jax.ShapeDtypeStruct(wavefn.shape, f32),
            jax.ShapeDtypeStruct((terms, max(across - wide, 1), size, size), f32),
        ],
        [
            pltpu.SMEM(term_shift.shape, jnp.int32),
            pltpu.VMEM((terms, slots, others, size), f32),
            pltpu.VMEM((terms, wide, size, size), f32),
            *work(others),
            pltpu.SemaphoreType.DMA((5,)),
            pltpu.SemaphoreType.DMA((ny,)),
        ],
    )
    kept.append(keep)
    arrived.append(swap(send))
    send, keep, own = call(
        first_own,
        [lops, psi, right, chosen],
        [VMEM] * 4,
        [result(1, wide)] * 2 + [jax.ShapeDtypeStruct((slots, terms * share, 2 * size), bf16)],
        work(share),
    )
    own_kept.append(keep)
    own_arrived.append(swap(send))
    pieces.append(sums(add_cores, [(blocks(wide), rows, size)] * (ny - 1), [kept[0], arrived[0]], keep))
    for start, wide in zip(starts[1:], widths[1:]):
        *send, keep, right = call(
            functools.partial(later_others, start, widths[0]),
            [left, psi, rops, chosen, pieces[-1][0]],
            [VMEM] * 4 + [ANY],
            [result(ny - 1, 1)] * wide + [
                result(ny - 1, wide), jax.ShapeDtypeStruct((wide, terms, 2 * size, size), bf16)
            ],
            work(others),
        )
        arrived.append([swap(value) for value in send])
        kept.append(keep)
        send, keep = call(
            functools.partial(later_own, start),
            [own, psi, right, chosen, keep],
            [VMEM] * 4 + [ANY],
            [result(1, wide)] * 2,
            work(share),
        )
        own_kept.append(keep)
        own_arrived.append(swap(send))
        groups = [(number * wide, rows, size) for number in (second, slots)]
        pieces.append(sums(add_cores, groups * (ny - 1), [kept[-1], *arrived[-1]], own_kept[-1]))

    def land(values):
        return [ahead(value, by) for by, value in enumerate(values, 1)]

    wide = widths[0]
    total = sums(add_all, [own_kept[0].shape], [own_kept[0], *land(pieces[0])], pieces[1][0])[0]
    value = sums(
        add_all, [(slots, wide, rows, size), (second, wide, rows, size)], [total, own_arrived[0]], None, ADD_COST
    )
    ready = value[1]
    value = [sectors(part, way) for way, part in enumerate(value)]
    arranged = [arrange(slots, *value)]

    wide = widths[1]
    total = sums(add_all, [(blocks(wide), rows, size)], [own_kept[1], own_arrived[1]], ready)[0]

    def add_group(refs, outs):
        block = refs[0][first:first + refs[1].shape[0]]
        for ref in refs[1:]:
            block = block + ref[...]
        outs[0][...] = block.reshape(outs[0].shape)

    value = []
    for way, number, first in ((1, second, slots * wide), (0, slots, 0)):
        came = land(pieces[1][1 - way::2])
        ready = sums(add_group, [(number, wide, rows, size)], [total, *came], ready)[0]
        value.append(sectors(ready, way))
    value[0] = sums(landed_first, [value[0].shape], [value[0]], arranged[0], LANDED_COST)[0]
    return settle(arranged, value[1], value[0])


def solution(mesh):
    placed = (
        P("lsec", "rsec", None, None),
        P("op", "lsec", None, None),
        P("op", "rsec", None, None),
        P("op"),
    )
    return jax.shard_map(
        shards, mesh=mesh, in_specs=placed, out_specs=P("lsec", "rsec", "op", None), check_vma=False
    )
```
